32 devices in a mesh: row: 8 (over y, x, core), col: 4 (over z).
Axes of the slice: x: 2, y: 2, z: 4, core: 2. Of those that a mesh axis runs over, the one named last changes fastest.
Arguments:
- panel_cols: float32 [256, 8192], P('col', 'row'), as said below
- window_cols: float32 [16384, 8192], P('col', 'row'), may hold values from -6 to 6
Outputs:
- triangle: float32 [256, 256], replicated
- top_rows: float32 [16384, 256], P(('col', 'row'))
- residual: float32 [16384, 8192], P('col', 'row')
The draws below stay inside these ranges and needn't reach their ends.
Inputs may be any that keep to these rules, and one draw needn't show every extreme that they name: `panel_cols`: the 256 rows are linearly independent over the 1024 columns of every block of row.
All inputs are finite; a program needn't handle non-finite values.
Results may differ from the reference program's by a relative error of at most 0.000084.
Values sent between devices are 32-bit elements; how exact they have to be, the bound alone decides.
No kernel may reach another device: no remote copies, remote signals or barrier semaphores. Data moves between devices by JAX's collectives and lax.ppermute only.
A program may use at most 128 MiB of HBM per device.

```python
import math
import jax
import jax.numpy as jnp
from jax import lax

PANEL = 256
WINDOW = 16384
ROWS = 8192


def draw_panel_cols(key, part):
    key_col = jax.random.fold_in(key, 11)
    key_row = jax.random.fold_in(key, 23)
    key_base = jax.random.fold_in(key, 37)
    column_scale = jnp.exp(jax.random.uniform(key_col, (PANEL, 1), jnp.float32) * math.log(10.0))
    row_scale = jnp.exp(jax.random.uniform(key_row, (1, ROWS), jnp.float32) * math.log(10.0))
    normal_part = jnp.clip(jax.random.normal(key_base, (PANEL, ROWS), jnp.float32), -6.0, 6.0)
    return (column_scale * row_scale * normal_part / math.sqrt(21.5 * ROWS)).astype(jnp.float32)


def raised(result, stream_key, source, target, shards_of, factor):
    owner, partner = [(jnp.arange(result.shape[dim]) // (result.shape[dim] // shards_of)).reshape([-1 if axis == dim else 1 for axis in range(result.ndim)]) for dim in (source, target)]
    chosen = jax.random.permutation(stream_key, shards_of)[partner]
    strong = (owner == chosen) | (owner == (partner + shards_of // 2) % shards_of)
    return jnp.where(strong, factor * result, result)


def shard_levels(stream_key, extent, pieces, smallest, largest):
    def one(axis_at, blocks):
        draws = jax.random.uniform(jax.random.fold_in(jax.random.fold_in(stream_key, 6), axis_at), (blocks,), jnp.float32, smallest / len(pieces), largest / len(pieces))
        return jnp.repeat(jnp.exp(draws), extent[axis_at] // blocks).reshape((-1,) + (1,) * (len(extent) - axis_at - 1))

    factor_of = one(*pieces[0])
    for cut in pieces[1:]:
        factor_of = factor_of * one(*cut)
    return factor_of


def noise_with(stream_key, dims, deviation, most, shards, heavy, kind=jnp.bfloat16):
    result = deviation * jax.random.normal(stream_key, dims, jnp.float32)
    if shards:
        result = result * shard_levels(stream_key, dims, shards, -0.22, 0.18)
    return jnp.clip(raised(result, jax.random.fold_in(stream_key, 3), *heavy), -most, most).astype(kind)


def setup_inputs(seed: int = 0) -> dict:
    streams_of = jax.random.split(jax.random.key(seed), 3)
    panel_cols = draw_panel_cols(jax.random.fold_in(streams_of[2], 71), 0)
    window_cols = noise_with(streams_of[1], (WINDOW, ROWS), 1.0, 6.0, ((0, 4), (1, 8)), (1, 0, 8, 2.0), jnp.float32)
    return dict(panel_cols=panel_cols, window_cols=window_cols)


def reference(panel_cols, window_cols):
    precise = lax.Precision.HIGHEST
    gram = jnp.dot(panel_cols.astype(jnp.float32), panel_cols.T.astype(jnp.float32), precision=precise, preferred_element_type=jnp.float32)
    lower_part = jnp.linalg.cholesky(gram)
    identity = jnp.eye(PANEL, dtype=jnp.float32)
    inverse = lax.linalg.triangular_solve(lower_part, identity, left_side=True, lower=True)
    cross = jnp.dot(window_cols.astype(jnp.float32), panel_cols.T.astype(jnp.float32), precision=precise, preferred_element_type=jnp.float32)
    top_rows = jnp.dot(cross.astype(jnp.float32), inverse.T.astype(jnp.float32), precision=precise, preferred_element_type=jnp.float32)
    combined = jnp.dot(top_rows.astype(jnp.float32), inverse.astype(jnp.float32), precision=precise, preferred_element_type=jnp.float32)
    residual = window_cols - jnp.dot(combined.astype(jnp.float32), panel_cols.astype(jnp.float32), precision=precise, preferred_element_type=jnp.float32)
    return (lower_part.T, top_rows, residual)
```

```python
import functools

import jax
import jax.numpy as jnp
import numpy as np
from jax import lax
from jax.experimental import pallas as pl
from jax.experimental.pallas import tpu as pltpu
from jax.sharding import PartitionSpec as P

precise = lax.Precision.HIGHEST
f32, bf16 = jnp.float32, jnp.bfloat16
BLOCK = 32
MIB = 1 << 20


def dot(left, right, dims, precision=None):
    return lax.dot_general(
        left, right, (dims, ((), ())), precision=precision, preferred_element_type=f32
    )


def split(value):
    high = value.astype(bf16)
    return high, (value - high.astype(f32)).astype(bf16)


def dot3(left, right_high, right_low, dims):
    left_high, left_low = split(left)
    return dot(left_high, right_high, dims) + (
        dot(left_high, right_low, dims) + dot(left_low, right_high, dims)
    )


def gram_kernel(n, first_ref, *refs):
    shards, (whole_ref, high_ref, low_ref, gram_ref) = refs[:-4], refs[-4:]
    per = len(shards) // n
    rows = shards[0].shape[0]
    for step in range(n):
        owner = lax.rem(first_ref[0] + (n - step), n)
        for part in range(per):
            start = pl.multiple_of((owner * per + part) * rows, rows)
            whole_ref[pl.ds(start, rows), :] = shards[step * per + part][...]
    whole = whole_ref[...]
    gram_ref[...] = dot(whole, whole, ((1,), (1,)), precise)
    high, low = split(whole)
    high_ref[...] = high
    low_ref[...] = low


def gram_call(n, first, shards):
    columns = shards[0].shape[1]
    panel = shards[0].shape[0] * len(shards)
    full = lambda shape: pl.BlockSpec(shape, lambda i, first: (0, 0))
    return pl.pallas_call(
        functools.partial(gram_kernel, n),
        grid_spec=pltpu.PrefetchScalarGridSpec(
            num_scalar_prefetch=1,
            grid=(1,),
            in_specs=[full(shard.shape) for shard in shards],
            out_specs=[full((panel, columns))] * 3 + [full((panel, panel))],
        ),
        out_shape=[
            jax.ShapeDtypeStruct((panel, columns), f32),
            jax.ShapeDtypeStruct((panel, columns), bf16),
            jax.ShapeDtypeStruct((panel, columns), bf16),
            jax.ShapeDtypeStruct((panel, panel), f32),
        ],
        compiler_params=pltpu.CompilerParams(vmem_limit_bytes=24 * MIB),
        cost_estimate=pl.CostEstimate(
            flops=12 * panel * panel * columns, bytes_accessed=12 * panel * columns, transcendentals=0
        ),
        name="gram",
    )(first, *shards)


def cross_kernel(table_ref, window_ref, high_ref, low_ref, cross_ref):
    cross_ref[...] = dot3(window_ref[...], high_ref[...], low_ref[...], ((1,), (1,)))


def cross_call(table, rows, window, high, low):
    count, columns, panel = table.shape[0], window.shape[1], high.shape[0]
    return pl.pallas_call(
        cross_kernel,
        grid_spec=pltpu.PrefetchScalarGridSpec(
            num_scalar_prefetch=1,
            grid=(count,),
            in_specs=[
                pl.BlockSpec((rows, columns), lambda i, table: (table[i], 0)),
                pl.BlockSpec((panel, columns), lambda i, table: (0, 0)),
                pl.BlockSpec((panel, columns), lambda i, table: (0, 0)),
            ],
            out_specs=pl.BlockSpec((rows, panel), lambda i, table: (i, 0)),
        ),
        out_shape=jax.ShapeDtypeStruct((count * rows, panel), f32),
        compiler_params=pltpu.CompilerParams(vmem_limit_bytes=24 * MIB),
        cost_estimate=pl.CostEstimate(
            flops=6 * count * rows * columns * panel,
            bytes_accessed=4 * count * rows * (columns + panel),
            transcendentals=0,
        ),
        name="cross",
    )(table, window, high, low)


def residual_kernel(count, table_ref, window_ref, high_ref, low_ref, *refs):
    pieces, out_ref, held = refs[:count], refs[-2], refs[-1]
    for place in range(count):

        @pl.when(pl.program_id(0) == place)
        def _():
            held[...] = pieces[place][...]

    out_ref[...] = window_ref[...] - dot3(held[...], high_ref[...], low_ref[...], ((1,), (0,)))


def residual_call(table, window, high, low, pieces, before):
    count, (rows, panel), columns = len(pieces), pieces[0].shape, window.shape[1]
    block = pl.BlockSpec((rows, columns), lambda i, table: (table[i], 0))
    full = lambda shape: pl.BlockSpec(shape, lambda i, table: (0, 0))
    operands = [table, window, high, low, *pieces]
    in_specs = [block, full(high.shape), full(low.shape)] + [full((rows, panel))] * count
    aliases = {}
    if before is not None:
        aliases = {len(operands): 0}
        operands.append(before)
        in_specs.append(pl.BlockSpec(memory_space=pl.ANY))
    return pl.pallas_call(
        functools.partial(residual_kernel, count),
        grid_spec=pltpu.PrefetchScalarGridSpec(
            num_scalar_prefetch=1,
            grid=(count,),
            in_specs=in_specs,
            out_specs=block,
            scratch_shapes=[pltpu.VMEM((rows, panel), f32)],
        ),
        out_shape=jax.ShapeDtypeStruct(window.shape, f32),
        input_output_aliases=aliases,
        compiler_params=pltpu.CompilerParams(vmem_limit_bytes=24 * MIB),
        cost_estimate=pl.CostEstimate(
            flops=6 * count * rows * columns * panel,
            bytes_accessed=8 * count * rows * columns,
            transcendentals=0,
        ),
        name="residual",
    )(*operands)


def eliminate(diagonal):
    size, lanes, tile = BLOCK, 128, 8
    tiles = size // tile
    row_at = [lax.broadcasted_iota(jnp.int32, (tile, lanes), 0) + tile * t for t in range(tiles)]
    lane_at = lax.broadcasted_iota(jnp.int32, (tile, lanes), 1)
    spread = [
        [
            jnp.broadcast_to(diagonal[tile * t : tile * (t + 1), k : k + 1], (tile, lanes))
            for t in range(tiles)
        ]
        for k in range(size)
    ]
    inverse = [jnp.where(row_at[t] == lane_at, 1.0, 0.0) for t in range(tiles)]
    lower = [jnp.zeros((tile, lanes), f32) for _ in range(tiles)]
    scale = [jnp.zeros((tile, lanes), f32) for _ in range(tiles)]
    for j in range(size):
        own, at = j // tile, j % tile
        pivot = spread[j][own][at : at + 1, :]
        reciprocal = 1.0 / pivot
        root = lax.rsqrt(pivot)
        inverse_row = inverse[own][at : at + 1, :]
        factor = {}
        for t in range(own, tiles):
            column = spread[j][t]
            factor[t] = column * reciprocal
            if t == own:
                factor[t] = jnp.where(row_at[t] > j, factor[t], 0.0)
                scale[t] = jnp.where(row_at[t] == j, root, scale[t])
                lower[t] = jnp.where((lane_at == j) & (row_at[t] >= j), column * root, lower[t])
            else:
                lower[t] = jnp.where(lane_at == j, column * root, lower[t])
            inverse[t] = inverse[t] - factor[t] * inverse_row
        for k in range(j + 1, size):
            entry = spread[j][k // tile][k % tile : k % tile + 1, :]
            for t in range(k // tile, tiles):
                spread[k][t] = spread[k][t] - factor[t] * entry
    inverse = [inverse[t] * scale[t] for t in range(tiles)]
    return jnp.concatenate(lower, 0), jnp.concatenate(inverse, 0)


def factor_kernel(begin, end, last, *refs):
    if begin:
        state_in, lower_in, state_ref, lower_ref = refs[:4]
        lower_ref[...] = lower_in[...]
    else:
        state_in, state_ref, lower_ref = refs[:3]
    state_ref[...] = state_in[...]
    size = state_ref.shape[0]
    column_at = lax.broadcasted_iota(jnp.int32, (BLOCK, size), 1)
    row_at = lax.broadcasted_iota(jnp.int32, (BLOCK, size), 0)
    for step in range(begin, end):
        start, stop = step * BLOCK, (step + 1) * BLOCK
        rows = state_ref[start:stop, :]
        lower, inverse = eliminate(rows[:, start:stop])
        lower_ref[start:stop, :] = lower
        inside = (column_at >= start) & (column_at < stop)
        rows = jnp.where(inside, jnp.where(column_at - start == row_at, 1.0, 0.0), rows)
        done = dot(inverse[:, :BLOCK], rows, ((1,), (0,)), precise)
        state_ref[start:stop, :] = done
        if stop < size:
            upper = jnp.where(column_at >= stop, done, 0.0)
            update = dot(upper, done, ((0,), (0,)), precise)[stop:, :]
            below_at = lax.broadcasted_iota(jnp.int32, (size - stop, size), 1)
            below = jnp.where(
                (below_at >= start) & (below_at < stop), 0.0, state_ref[stop:, :]
            )
            state_ref[stop:, :] = below - update
    if last:
        whole_ref = refs[4]
        triangle_ref, inverse_ref, high_ref, low_ref = refs[5:]
        column_at = lax.broadcasted_iota(jnp.int32, (size, size), 1)
        row_at = lax.broadcasted_iota(jnp.int32, (size, size), 0)
        edge = (row_at // BLOCK + 1) * BLOCK
        state = state_ref[...]
        inverse = jnp.where(column_at <= row_at, state, 0.0)
        inverse_ref[...] = inverse
        lower = lower_ref[...]
        wide = jnp.concatenate([lower] * (size // lower.shape[1]), 1)
        for step in range(size // BLOCK):
            start, stop = step * BLOCK, (step + 1) * BLOCK
            shift = start % lower.shape[1]
            part = wide[start:stop, :]
            if shift:
                part = pltpu.roll(part, shift, 1)
            lower_full = jnp.where(
                (column_at[start:stop, :] >= start) & (column_at[start:stop, :] < stop), part, 0.0
            )
            state_ref[start:stop, :] = lower_full
        triangle_ref[...] = jnp.where(column_at >= edge, state, 0.0) + state_ref[...].T
        half = dot(inverse, whole_ref[...], ((1,), (0,)), precise)
        weight = dot(inverse, half, ((0,), (0,)), precise)
        high, low = split(weight)
        high_ref[...] = high
        low_ref[...] = low


def factor_call(begin, end, last, operands):
    size = operands[0].shape[0]
    shapes = [
        jax.ShapeDtypeStruct((size, size), f32),
        jax.ShapeDtypeStruct((size, 128), f32),
    ]
    if last:
        columns = operands[-1].shape[1]
        shapes += [
            jax.ShapeDtypeStruct((size, size), f32),
            jax.ShapeDtypeStruct((size, size), f32),
            jax.ShapeDtypeStruct((size, columns), bf16),
            jax.ShapeDtypeStruct((size, columns), bf16),
        ]
    if last:
        def body(*refs):
            factor_kernel(begin, end, True, *refs[:2], *refs[3:5], refs[2], *refs[5:])
    else:
        body = functools.partial(factor_kernel, begin, end, False)
    return pl.pallas_call(
        body,
        out_shape=shapes,
        in_specs=[pl.BlockSpec(memory_space=pltpu.VMEM)] * len(operands),
        out_specs=[pl.BlockSpec(memory_space=pltpu.VMEM)] * len(shapes),
        compiler_params=pltpu.CompilerParams(vmem_limit_bytes=24 * MIB),
        cost_estimate=pl.CostEstimate(
            flops=6_000_000_000 * (end - begin), bytes_accessed=MIB, transcendentals=0
        ),
        name="factor",
    )(*operands)


def flip(value, bit, size):
    return lax.ppermute(value, "row", [(i, i ^ bit) for i in range(size)])


def total_everywhere(value, bits, size):
    value = value + flip(value, bits[0], size)
    half = value.shape[0] // 2
    top, bottom = value[:half], value[half:]
    for one, other in zip(bits[1:], bits[:0:-1]):
        top, bottom = top + flip(top, one, size), bottom + flip(bottom, other, size)
    return jnp.concatenate([top, bottom], 0)


def sorted_pieces(order):
    owners = [0]
    for bit in reversed(order):
        owners = [owner | bit for owner in owners] + owners
    return owners


def local(panel_cols, window_cols):
    size = lax.axis_size("row")
    depth = lax.axis_size("col")
    here = lax.axis_index("row")
    bits = [1 << place for place in range(size.bit_length() - 1)]
    orders = (bits[1:], bits[:0:-1])
    share = window_cols.shape[0] // size
    piece = share // 2

    parts = 2 if panel_cols.shape[0] % 16 == 0 else 1
    cut = panel_cols.shape[0] // parts
    ring = [(i, (i + 1) % depth) for i in range(depth)]
    held = [panel_cols[part * cut : (part + 1) * cut] for part in range(parts)]
    shards = list(held)
    for _ in range(depth - 1):
        held = [lax.ppermute(part, "col", ring) for part in held]
        shards += held
    first = lax.axis_index("col").astype(jnp.int32).reshape(1)
    whole, high, low, gram = gram_call(depth, first, shards)

    owners = [(owner, half) for half in (0, 1) for owner in sorted_pieces(orders[half])]
    table_of = lambda bit: jnp.stack(
        [((here ^ (owner | bit)) * 2 + half).astype(jnp.int32) for owner, half in owners]
    )
    given, kept = table_of(1), table_of(0)

    gram_total = total_everywhere(gram, bits, size)

    cross_given = cross_call(given, piece, window_cols, high, low)
    arrived = flip(cross_given, 1, size)
    cross_kept = cross_call(kept, piece, window_cols, high, low)

    middle = cross_kept.shape[0] // 2
    sums = []
    for half in (0, 1):
        begin, count = half * middle, middle
        pairs = [(cross_kept, begin), (arrived, begin)]
        for bit in orders[half]:
            count //= 2
            cut_at = lambda array, at: lax.slice_in_dim(array, at, at + count, axis=0)
            out = sum(cut_at(array, at) for array, at in pairs)
            pairs = [(array, at + count) for array, at in pairs] + [(flip(out, bit, size), 0)]
        sums.append(
            sum(lax.slice_in_dim(array, at, at + count, axis=0) for array, at in pairs)
        )

    steps = gram.shape[0] // BLOCK
    cut_step = steps // 2
    state = factor_call(0, cut_step, False, [gram_total])
    _, _, triangle, inverse, weight_high, weight_low = factor_call(
        cut_step, steps, True, [*state, whole]
    )

    top_rows = dot(jnp.concatenate(sums, 0), inverse, ((1,), (1,)), precise)

    own = []
    for half in (0, 1):
        pieces = [sums[half]]
        for bit in reversed(orders[half]):
            pieces = [flip(part, bit, size) for part in pieces] + pieces
        own += pieces
    others = [flip(part, 1, size) for part in own]
    residual = residual_call(kept, window_cols, weight_high, weight_low, own, None)
    residual = residual_call(given, window_cols, weight_high, weight_low, others, residual)
    return triangle, top_rows, residual


def solution(mesh):
    return jax.shard_map(
        local,
        mesh=mesh,
        in_specs=(P("col", "row"), P("col", "row")),
        out_specs=(P(), P(("col", "row"), None), P("col", "row")),
        check_vma=False,
    )
```

```python
import functools

import jax
import jax.numpy as jnp
from jax import lax
from jax.experimental import pallas as pl
from jax.experimental.pallas import tpu as pltpu
from jax.sharding import PartitionSpec as P

precise = lax.Precision.HIGHEST
f32, bf16 = jnp.float32, jnp.bfloat16
BLOCK = 32
MIB = 1 << 20
STREAM = 50 * MIB
GROUPS = 1


def dot(left, right, dims, precision=None):
    return lax.dot_general(
        left, right, (dims, ((), ())), precision=precision, preferred_element_type=f32
    )


def split(value):
    high = value.astype(bf16)
    return high, (value - high.astype(f32)).astype(bf16)


def dot3(left, right_high, right_low, dims):
    left_high, left_low = split(left)
    return dot(left_high, right_high, dims) + (
        dot(left_high, right_low, dims) + dot(left_low, right_high, dims)
    )


def gram_kernel(first_ref, *refs):
    shards, (whole_ref, gram_ref) = refs[:-2], refs[-2:]
    rows = shards[0].shape[0]
    for step, shard in enumerate(shards):
        owner = lax.rem(first_ref[0] + step, len(shards))
        whole_ref[pl.ds(pl.multiple_of(owner * rows, rows), rows), :] = shard[...]
    whole = whole_ref[...]
    gram_ref[...] = dot(whole, whole, ((1,), (1,)), precise)


def full(shape):
    return pl.BlockSpec(shape, lambda i, *tables: (0, 0))


def gram_call(first, shards):
    rows, columns = shards[0].shape
    panel = rows * len(shards)
    return pl.pallas_call(
        gram_kernel,
        grid_spec=pltpu.PrefetchScalarGridSpec(
            num_scalar_prefetch=1,
            grid=(1,),
            in_specs=[full(shard.shape) for shard in shards],
            out_specs=[full((panel, columns)), full((panel, panel))],
        ),
        out_shape=[
            jax.ShapeDtypeStruct((panel, columns), f32),
            jax.ShapeDtypeStruct((panel, panel), f32),
        ],
        compiler_params=pltpu.CompilerParams(vmem_limit_bytes=STREAM),
        cost_estimate=pl.CostEstimate(
            flops=12 * panel * panel * columns, bytes_accessed=12 * panel * columns, transcendentals=0
        ),
        name="gram",
    )(first, *shards)


def cross_kernel(shares, table_ref, window_ref, *refs):
    shards, (cross_ref, panel_ref) = refs[:-2], refs[-2:]
    step = pl.program_id(0)
    width = cross_ref.shape[1]
    rows = shards[0].shape[0]

    @pl.when(step == 0)
    def _():
        for place, shard in enumerate(shards):
            high, low = split(shard[...])
            panel_ref[place * rows : (place + 1) * rows, :] = high
            panel_ref[width + place * rows : width + (place + 1) * rows, :] = low

    window = window_ref[...]
    window_high, window_low = split(window)
    by_high = dot(window_high, panel_ref[...], ((1,), (1,)))
    by_low = dot(window_low, panel_ref[:width, :], ((1,), (1,)))
    result = by_high[:, :width] + (by_high[:, width:] + by_low)
    piece = window.shape[0] // 2
    cross_ref[pl.ds(pl.multiple_of(step * piece, piece), piece), :] = result[:piece]
    place = shares + table_ref[shares + step]
    cross_ref[pl.ds(pl.multiple_of(place * piece, piece), piece), :] = result[piece:]


def cross_call(table, share, window, shards):
    shares, columns = table.shape[0] // 2, window.shape[1]
    width = shards[0].shape[0] * len(shards)
    return pl.pallas_call(
        functools.partial(cross_kernel, shares),
        grid_spec=pltpu.PrefetchScalarGridSpec(
            num_scalar_prefetch=1,
            grid=(shares,),
            in_specs=[pl.BlockSpec((share, columns), lambda i, table: (table[i], 0))]
            + [full(shard.shape) for shard in shards],
            out_specs=full((shares * share, width)),
            scratch_shapes=[pltpu.VMEM((2 * width, columns), bf16)],
        ),
        out_shape=jax.ShapeDtypeStruct((shares * share, width), f32),
        compiler_params=pltpu.CompilerParams(vmem_limit_bytes=STREAM),
        cost_estimate=pl.CostEstimate(
            flops=6 * shares * share * columns * width,
            bytes_accessed=4 * shares * share * (columns + width),
            transcendentals=0,
        ),
        name="cross",
    )(table, window, *shards)


def residual_kernel(shares, groups, table_ref, window_ref, high_ref, low_ref, *refs):
    totals, out_ref, held = refs[:groups], refs[-2], refs[-1]
    step = pl.program_id(0)
    piece = held.shape[0] // 2
    place = shares + table_ref[shares + step]
    begin = 0
    for total in totals:
        end = begin + total.shape[1]
        held[:piece, begin:end] = total[pl.ds(pl.multiple_of(step * piece, piece), piece), :]
        held[piece:, begin:end] = total[pl.ds(pl.multiple_of(place * piece, piece), piece), :]
        begin = end
    out_ref[...] = window_ref[...] - dot3(held[...], high_ref[...], low_ref[...], ((1,), (0,)))


def residual_call(table, share, window, high, low, totals, before):
    shares, columns = table.shape[0] // 2, window.shape[1]
    panel = high.shape[0]
    block = pl.BlockSpec((share, columns), lambda i, table: (table[i], 0))
    operands = [table, window, high, low, *totals]
    in_specs = [block, full(high.shape), full(low.shape)] + [full(total.shape) for total in totals]
    aliases = {}
    if before is not None:
        aliases = {len(operands): 0}
        operands.append(before)
        in_specs.append(pl.BlockSpec(memory_space=pl.ANY))
    return pl.pallas_call(
        functools.partial(residual_kernel, shares, len(totals)),
        grid_spec=pltpu.PrefetchScalarGridSpec(
            num_scalar_prefetch=1,
            grid=(shares,),
            in_specs=in_specs,
            out_specs=block,
            scratch_shapes=[pltpu.VMEM((share, panel), f32)],
        ),
        out_shape=jax.ShapeDtypeStruct(window.shape, f32),
        input_output_aliases=aliases,
        compiler_params=pltpu.CompilerParams(vmem_limit_bytes=STREAM),
        cost_estimate=pl.CostEstimate(
            flops=6 * shares * share * columns * panel,
            bytes_accessed=8 * shares * share * columns,
            transcendentals=0,
        ),
        name="residual",
    )(*operands)


def eliminate(diagonal):
    size, lanes, tile = BLOCK, 128, 8
    tiles = size // tile
    row_at = [lax.broadcasted_iota(jnp.int32, (tile, lanes), 0) + tile * t for t in range(tiles)]
    lane_at = lax.broadcasted_iota(jnp.int32, (tile, lanes), 1)
    spread = [
        [
            jnp.broadcast_to(diagonal[tile * t : tile * (t + 1), k : k + 1], (tile, lanes))
            for t in range(tiles)
        ]
        for k in range(size)
    ]
    inverse = [jnp.where(row_at[t] == lane_at, 1.0, 0.0) for t in range(tiles)]
    lower = [jnp.zeros((tile, lanes), f32) for _ in range(tiles)]
    scale = [jnp.zeros((tile, lanes), f32) for _ in range(tiles)]
    for j in range(size):
        own, at = j // tile, j % tile
        pivot = spread[j][own][at : at + 1, :]
        reciprocal = 1.0 / pivot
        root = lax.rsqrt(pivot)
        inverse_row = inverse[own][at : at + 1, :]
        factor = {}
        for t in range(own, tiles):
            column = spread[j][t]
            factor[t] = column * reciprocal
            if t == own:
                factor[t] = jnp.where(row_at[t] > j, factor[t], 0.0)
                scale[t] = jnp.where(row_at[t] == j, root, scale[t])
                lower[t] = jnp.where((lane_at == j) & (row_at[t] >= j), column * root, lower[t])
            else:
                lower[t] = jnp.where(lane_at == j, column * root, lower[t])
            inverse[t] = inverse[t] - factor[t] * inverse_row
        for k in range(j + 1, size):
            entry = spread[j][k // tile][k % tile : k % tile + 1, :]
            for t in range(k // tile, tiles):
                spread[k][t] = spread[k][t] - factor[t] * entry
    inverse = [inverse[t] * scale[t] for t in range(tiles)]
    return jnp.concatenate(lower, 0), jnp.concatenate(inverse, 0)


def factor_kernel(begin, end, depth, *refs):
    last = depth is not None
    if begin:
        state_in, lower_in, state_ref, lower_ref = refs[:4]
        lower_ref[...] = lower_in[...]
    else:
        state_in, state_ref, lower_ref = refs[:3]
    state_ref[...] = state_in[...]
    size = state_ref.shape[0]
    column_at = lax.broadcasted_iota(jnp.int32, (BLOCK, size), 1)
    row_at = lax.broadcasted_iota(jnp.int32, (BLOCK, size), 0)
    for step in range(begin, end):
        start, stop = step * BLOCK, (step + 1) * BLOCK
        rows = state_ref[start:stop, :]
        lower, inverse = eliminate(rows[:, start:stop])
        lower_ref[start:stop, :] = lower
        inside = (column_at >= start) & (column_at < stop)
        rows = jnp.where(inside, jnp.where(column_at - start == row_at, 1.0, 0.0), rows)
        done = dot(inverse[:, :BLOCK], rows, ((1,), (0,)), precise)
        state_ref[start:stop, :] = done
        if stop < size:
            upper = jnp.where(column_at >= stop, done, 0.0)
            update = dot(upper, done, ((0,), (0,)), precise)[stop:, :]
            below_at = lax.broadcasted_iota(jnp.int32, (size - stop, size), 1)
            below = jnp.where(
                (below_at >= start) & (below_at < stop), 0.0, state_ref[stop:, :]
            )
            state_ref[stop:, :] = below - update
    if last:
        whole_ref, first_ref = refs[4:6]
        triangle_ref, inverse_ref, high_ref, low_ref = refs[6:]
        column_at = lax.broadcasted_iota(jnp.int32, (size, size), 1)
        row_at = lax.broadcasted_iota(jnp.int32, (size, size), 0)
        edge = (row_at // BLOCK + 1) * BLOCK
        state = state_ref[...]
        inverse = jnp.where(column_at <= row_at, state, 0.0)
        lower = lower_ref[...]
        wide = jnp.concatenate([lower] * (size // lower.shape[1]), 1)
        for step in range(size // BLOCK):
            start, stop = step * BLOCK, (step + 1) * BLOCK
            shift = start % lower.shape[1]
            part = wide[start:stop, :]
            if shift:
                part = pltpu.roll(part, shift, 1)
            lower_full = jnp.where(
                (column_at[start:stop, :] >= start) & (column_at[start:stop, :] < stop), part, 0.0
            )
            state_ref[start:stop, :] = lower_full
        triangle_ref[...] = jnp.where(column_at >= edge, state, 0.0) + state_ref[...].T
        half = dot(inverse, whole_ref[...], ((1,), (0,)), precise)
        shift = lax.rem(size - first_ref[0] * (size // depth), size)
        inverse = pltpu.roll(inverse, shift, 1)
        inverse_ref[...] = inverse
        weight = dot(inverse, half, ((0,), (0,)), precise)
        high, low = split(weight)
        high_ref[...] = high
        low_ref[...] = low


def factor_call(begin, end, operands, whole=None, first=None, depth=None):
    size = operands[0].shape[0]
    operands = list(operands)
    in_specs = [pl.BlockSpec(memory_space=pltpu.VMEM)] * len(operands)
    shapes = [
        jax.ShapeDtypeStruct((size, size), f32),
        jax.ShapeDtypeStruct((size, 128), f32),
    ]
    if depth is None:
        body = functools.partial(factor_kernel, begin, end, None)
    else:
        operands += [whole, first]
        in_specs += [
            pl.BlockSpec(memory_space=pltpu.VMEM),
            pl.BlockSpec(memory_space=pltpu.SMEM),
        ]
        shapes += [
            jax.ShapeDtypeStruct((size, size), f32),
            jax.ShapeDtypeStruct((size, size), f32),
            jax.ShapeDtypeStruct((size, whole.shape[1]), bf16),
            jax.ShapeDtypeStruct((size, whole.shape[1]), bf16),
        ]

        def body(*refs):
            factor_kernel(begin, end, depth, *refs[:2], *refs[4:6], *refs[2:4], *refs[6:])

    return pl.pallas_call(
        body,
        out_shape=shapes,
        in_specs=in_specs,
        out_specs=[pl.BlockSpec(memory_space=pltpu.VMEM)] * len(shapes),
        compiler_params=pltpu.CompilerParams(vmem_limit_bytes=24 * MIB),
        cost_estimate=pl.CostEstimate(
            flops=1_500_000_000 * (end - begin), bytes_accessed=MIB, transcendentals=0
        ),
        name="factor",
    )(*operands)


def flip(value, bit, size):
    return lax.ppermute(value, "row", [(i, i ^ bit) for i in range(size)])


def sorted_pieces(order):
    owners = [0]
    for bit in reversed(order):
        owners = [owner | bit for owner in owners] + owners
    return owners


def gather_panel(shard, depth):
    up = [(i, (i - 1) % depth) for i in range(depth)]
    down = [(i, (i + 1) % depth) for i in range(depth)]
    above = [lax.ppermute(shard, "col", up)]
    below = []
    later, _ = lax.optimization_barrier((shard, above[0]))
    for step in range(2, depth):
        if step % 2 == 0:
            above.append(lax.ppermute(above[-1], "col", up))
        else:
            below.append(lax.ppermute(below[-1] if below else later, "col", down))
    return [shard, *above, *below[::-1]]


def sum_shares(kept, arrived, orders, size):
    middle = kept.shape[0] // 2
    sums = []
    for half in (0, 1):
        count = middle
        pairs = [(kept, half * middle), (arrived, half * middle)]
        for bit in orders[half]:
            count //= 2
            out = sum(lax.slice_in_dim(array, at, at + count, axis=0) for array, at in pairs)
            pairs = [(array, at + count) for array, at in pairs] + [(flip(out, bit, size), 0)]
        sums.append(sum(lax.slice_in_dim(array, at, at + count, axis=0) for array, at in pairs))
    return sums


def spread_shares(sums, orders, size):
    held = []
    for half in (0, 1):
        part = sums[half]
        for bit in reversed(orders[half]):
            part = jnp.concatenate([flip(part, bit, size), part], 0)
        held.append(part)
    return jnp.concatenate(held, 0)


def local(panel_cols, window_cols):
    size = lax.axis_size("row")
    depth = lax.axis_size("col")
    here = lax.axis_index("row").astype(jnp.int32)
    first = lax.axis_index("col").astype(jnp.int32).reshape(1)
    bits = [1 << place for place in range(size.bit_length() - 1)]
    orders = (bits[1:], bits[:0:-1])
    share = window_cols.shape[0] // size

    shards = gather_panel(panel_cols, depth)

    owners, seconds = sorted_pieces(orders[0]), sorted_pieces(orders[1])
    places = jnp.asarray([seconds.index(owner) for owner in owners], jnp.int32)
    relative = jnp.asarray(owners, jnp.int32)
    given = jnp.concatenate([here ^ (relative | 1), places])
    kept = jnp.concatenate([here ^ relative, places])

    per = depth // GROUPS
    sums = []
    for group in range(GROUPS):
        some = shards[group * per : (group + 1) * per]
        if group == GROUPS - 1:
            whole, gram = gram_call(first, shards)
            gram_total = lax.psum(gram, "row")
        cross_given = cross_call(given, share, window_cols, some)
        arrived = flip(cross_given, 1, size)
        cross_kept = cross_call(kept, share, window_cols, some)
        sums.append(sum_shares(cross_kept, arrived, orders, size))

    steps = gram.shape[0] // BLOCK
    cuts = [0, steps * 3 // 8, steps * 6 // 8, steps]
    state = [gram_total]
    for begin, end in zip(cuts[:-2], cuts[1:-1]):
        state = factor_call(begin, end, state)
    _, _, triangle, inverse, weight_high, weight_low = factor_call(
        cuts[-2], steps, state, whole, first, depth
    )

    mine = [spread_shares(part, orders, size) for part in sums]
    others = [flip(total, 1, size) for total in mine]
    summed = jnp.concatenate([jnp.concatenate(part, 0) for part in sums], 1)
    top_rows = dot(summed, inverse, ((1,), (1,)), precise)
    residual = residual_call(kept, share, window_cols, weight_high, weight_low, mine, None)
    residual = residual_call(given, share, window_cols, weight_high, weight_low, others, residual)
    return triangle, top_rows, residual


def solution(mesh):
    return jax.shard_map(
        local,
        mesh=mesh,
        in_specs=(P("col", "row"), P("col", "row")),
        out_specs=(P(), P(("col", "row"), None), P("col", "row")),
        check_vma=False,
    )
```

```python
import functools

import jax
import jax.numpy as jnp
from jax import lax
from jax.experimental import pallas as pl
from jax.experimental.pallas import tpu as pltpu
from jax.sharding import PartitionSpec as P

precise = lax.Precision.HIGHEST
f32, bf16 = jnp.float32, jnp.bfloat16
BLOCK = 32
MIB = 1 << 20
STREAM = 50 * MIB
GROUPS = 1


def dot(left, right, dims, precision=None):
    return lax.dot_general(
        left, right, (dims, ((), ())), precision=precision, preferred_element_type=f32
    )


def split(value):
    high = value.astype(bf16)
    return high, (value - high.astype(f32)).astype(bf16)


def full(shape):
    return pl.BlockSpec(shape, lambda i, *tables: (0, 0))


def after(value, *others):
    return lax.optimization_barrier((value, *others))[0]


def gram_kernel(place_ref, *refs):
    shards, (whole_ref, kept_ref, given_ref, gram_ref) = refs[:-4], refs[-4:]
    rows = shards[0].shape[0]
    for step, shard in enumerate(shards):
        owner = lax.rem(place_ref[0] + step, len(shards))
        whole_ref[pl.ds(pl.multiple_of(owner * rows, rows), rows), :] = shard[...]
    whole = whole_ref[...]
    gram_ref[...] = dot(whole, whole, ((1,), (1,)), precise)
    half = kept_ref.shape[0]
    side = place_ref[1]
    kept_ref[...] = gram_ref[pl.ds(pl.multiple_of(side * half, half), half), :]
    given_ref[...] = gram_ref[pl.ds(pl.multiple_of((1 - side) * half, half), half), :]


def gram_call(place, shards):
    rows, columns = shards[0].shape
    panel = rows * len(shards)
    return pl.pallas_call(
        gram_kernel,
        grid_spec=pltpu.PrefetchScalarGridSpec(
            num_scalar_prefetch=1,
            grid=(1,),
            in_specs=[full(shard.shape) for shard in shards],
            out_specs=[full((panel, columns)), full((panel // 2, panel)), full((panel // 2, panel))],
            scratch_shapes=[pltpu.VMEM((panel, panel), f32)],
        ),
        out_shape=[
            jax.ShapeDtypeStruct((panel, columns), f32),
            jax.ShapeDtypeStruct((panel // 2, panel), f32),
            jax.ShapeDtypeStruct((panel // 2, panel), f32),
        ],
        compiler_params=pltpu.CompilerParams(vmem_limit_bytes=24 * MIB),
        cost_estimate=pl.CostEstimate(
            flops=12 * panel * panel * columns, bytes_accessed=12 * panel * columns, transcendentals=0
        ),
        name="gram",
    )(place, *shards)


def cross_kernel(terms, table_ref, window_ref, *refs):
    shards, (cross_ref, panel_ref) = refs[:-2], refs[-2:]
    width, columns = cross_ref.shape[1], window_ref.shape[1]
    rows = shards[0].shape[0]

    @pl.when(pl.program_id(0) == 0)
    def _():
        for place, shard in enumerate(shards):
            high, low = split(shard[...])
            here, beside = slice(place * rows, (place + 1) * rows), slice(
                width + place * rows, width + (place + 1) * rows
            )
            if terms == 2:
                for term in range(2):
                    panel_ref[here, term * columns : (term + 1) * columns] = high
                    panel_ref[beside, term * columns : (term + 1) * columns] = low
            else:
                for term, part in enumerate((high, low, high)):
                    panel_ref[here, term * columns : (term + 1) * columns] = part

    high, low = split(window_ref[...])
    if terms == 2:
        result = dot(jnp.concatenate([high, low], 1), panel_ref[...], ((1,), (1,)))
        cross_ref[...] = result[:, :width] + result[:, width:]
    else:
        cross_ref[...] = dot(jnp.concatenate([high, high, low], 1), panel_ref[...], ((1,), (1,)))


def cross_call(table, share, window, shards):
    shares, columns = table.shape[0], window.shape[1]
    width = shards[0].shape[0] * len(shards)
    terms = 2 if 2 * width <= 256 else 3
    return pl.pallas_call(
        functools.partial(cross_kernel, terms),
        grid_spec=pltpu.PrefetchScalarGridSpec(
            num_scalar_prefetch=1,
            grid=(shares,),
            in_specs=[pl.BlockSpec((share, columns), lambda i, table: (table[i], 0))]
            + [full(shard.shape) for shard in shards],
            out_specs=pl.BlockSpec((share, width), lambda i, table: (i, 0)),
            scratch_shapes=[
                pltpu.VMEM((2 * width if terms == 2 else width, terms * columns), bf16)
            ],
        ),
        out_shape=jax.ShapeDtypeStruct((shares * share, width), f32),
        compiler_params=pltpu.CompilerParams(vmem_limit_bytes=STREAM),
        cost_estimate=pl.CostEstimate(
            flops=6 * shares * share * columns * width,
            bytes_accessed=4 * shares * share * (columns + width),
            transcendentals=0,
        ),
        name="cross",
    )(table, window, *shards)


def residual_kernel(groups, table_ref, window_ref, weight_ref, *refs):
    totals, out_ref = refs[:groups], refs[-1]
    pairs = [split(total[...]) for total in totals]
    high, low = [jnp.concatenate(part, 1) for part in zip(*pairs)]
    out_ref[...] = window_ref[...] - dot(
        jnp.concatenate([high, high, low], 1), weight_ref[...], ((1,), (0,))
    )


def residual_call(table, share, window, weight, totals, before):
    shares, columns = table.shape[0], window.shape[1]
    block = pl.BlockSpec((share, columns), lambda i, table: (table[i], 0))
    operands = [table, window, weight, *totals]
    in_specs = [block, full(weight.shape)] + [
        pl.BlockSpec((share, total.shape[1]), lambda i, table: (i, 0)) for total in totals
    ]
    aliases = {}
    if before is not None:
        aliases = {len(operands): 0}
        operands.append(before)
        in_specs.append(pl.BlockSpec(memory_space=pl.ANY))
    return pl.pallas_call(
        functools.partial(residual_kernel, len(totals)),
        grid_spec=pltpu.PrefetchScalarGridSpec(
            num_scalar_prefetch=1,
            grid=(shares,),
            in_specs=in_specs,
            out_specs=block,
        ),
        out_shape=jax.ShapeDtypeStruct(window.shape, f32),
        input_output_aliases=aliases,
        compiler_params=pltpu.CompilerParams(vmem_limit_bytes=STREAM),
        cost_estimate=pl.CostEstimate(
            flops=2 * shares * share * columns * weight.shape[0],
            bytes_accessed=8 * shares * share * columns,
            transcendentals=0,
        ),
        name="residual",
    )(*operands)


def eliminate(diagonal):
    size, lanes, tile = BLOCK, 128, 8
    tiles = size // tile
    row_at = [lax.broadcasted_iota(jnp.int32, (tile, lanes), 0) + tile * t for t in range(tiles)]
    lane_at = lax.broadcasted_iota(jnp.int32, (tile, lanes), 1)
    spread = [
        [
            jnp.broadcast_to(diagonal[tile * t : tile * (t + 1), k : k + 1], (tile, lanes))
            for t in range(tiles)
        ]
        for k in range(size)
    ]
    inverse = [jnp.where(row_at[t] == lane_at, 1.0, 0.0) for t in range(tiles)]
    lower = [jnp.zeros((tile, lanes), f32) for _ in range(tiles)]
    scale = [jnp.zeros((tile, lanes), f32) for _ in range(tiles)]
    for j in range(size):
        own, at = j // tile, j % tile
        pivot = spread[j][own][at : at + 1, :]
        reciprocal = 1.0 / pivot
        root = lax.rsqrt(pivot)
        inverse_row = inverse[own][at : at + 1, :]
        factor = {}
        for t in range(own, tiles):
            column = spread[j][t]
            factor[t] = column * reciprocal
            if t == own:
                factor[t] = jnp.where(row_at[t] > j, factor[t], 0.0)
                scale[t] = jnp.where(row_at[t] == j, root, scale[t])
                lower[t] = jnp.where((lane_at == j) & (row_at[t] >= j), column * root, lower[t])
            else:
                lower[t] = jnp.where(lane_at == j, column * root, lower[t])
            inverse[t] = inverse[t] - factor[t] * inverse_row
        for k in range(j + 1, size):
            entry = spread[j][k // tile][k % tile : k % tile + 1, :]
            for t in range(k // tile, tiles):
                spread[k][t] = spread[k][t] - factor[t] * entry
    inverse = [inverse[t] * scale[t] for t in range(tiles)]
    return jnp.concatenate(lower, 0), jnp.concatenate(inverse, 0)


def factor_kernel(begin, end, depth, ins, outs):
    last = depth is not None
    state_ref, lower_ref = outs[:2]
    if begin:
        state_ref[...] = ins[0][...]
        lower_ref[...] = ins[1][...]
    else:
        half, side = ins[0].shape[0], ins[2][1]
        state_ref[pl.ds(pl.multiple_of(side * half, half), half), :] = ins[0][...]
        state_ref[pl.ds(pl.multiple_of((1 - side) * half, half), half), :] = ins[1][...]
    size = state_ref.shape[0]
    column_at = lax.broadcasted_iota(jnp.int32, (BLOCK, size), 1)
    row_at = lax.broadcasted_iota(jnp.int32, (BLOCK, size), 0)
    for step in range(begin, end):
        start, stop = step * BLOCK, (step + 1) * BLOCK
        rows = state_ref[start:stop, :]
        lower, inverse = eliminate(rows[:, start:stop])
        lower_ref[start:stop, :] = lower
        inside = (column_at >= start) & (column_at < stop)
        rows = jnp.where(inside, jnp.where(column_at - start == row_at, 1.0, 0.0), rows)
        done = dot(inverse[:, :BLOCK], rows, ((1,), (0,)), precise)
        state_ref[start:stop, :] = done
        if stop < size:
            upper = jnp.where(column_at >= stop, done, 0.0)
            update = dot(upper, done, ((0,), (0,)), precise)[stop:, :]
            below_at = lax.broadcasted_iota(jnp.int32, (size - stop, size), 1)
            below = jnp.where(
                (below_at >= start) & (below_at < stop), 0.0, state_ref[stop:, :]
            )
            state_ref[stop:, :] = below - update
    if last:
        whole_ref, place_ref = ins[2:]
        triangle_ref, inverse_ref, weight_ref = outs[2:]
        column_at = lax.broadcasted_iota(jnp.int32, (size, size), 1)
        row_at = lax.broadcasted_iota(jnp.int32, (size, size), 0)
        edge = (row_at // BLOCK + 1) * BLOCK
        state = state_ref[...]
        inverse = jnp.where(column_at <= row_at, state, 0.0)
        lower = lower_ref[...]
        wide = jnp.concatenate([lower] * (size // lower.shape[1]), 1)
        for step in range(size // BLOCK):
            start, stop = step * BLOCK, (step + 1) * BLOCK
            shift = start % lower.shape[1]
            part = wide[start:stop, :]
            if shift:
                part = pltpu.roll(part, shift, 1)
            lower_full = jnp.where(
                (column_at[start:stop, :] >= start) & (column_at[start:stop, :] < stop), part, 0.0
            )
            state_ref[start:stop, :] = lower_full
        triangle_ref[...] = jnp.where(column_at >= edge, state, 0.0) + state_ref[...].T
        half = dot(inverse, whole_ref[...], ((1,), (0,)), precise)
        shift = lax.rem(size - place_ref[0] * (size // depth), size)
        inverse = pltpu.roll(inverse, shift, 1)
        inverse_ref[...] = inverse
        weight = dot(inverse, half, ((0,), (0,)), precise)
        for term, part in enumerate(split(weight) + split(weight)[:1]):
            weight_ref[term * size : (term + 1) * size, :] = part


def factor_call(begin, end, operands, place, whole=None, depth=None):
    size = operands[0].shape[1]
    operands = list(operands)
    shapes = [
        jax.ShapeDtypeStruct((size, size), f32),
        jax.ShapeDtypeStruct((size, 128), f32),
    ]
    if depth is not None:
        operands.append(whole)
        shapes += [
            jax.ShapeDtypeStruct((size, size), f32),
            jax.ShapeDtypeStruct((size, size), f32),
            jax.ShapeDtypeStruct((3 * size, whole.shape[1]), bf16),
        ]
    in_specs = [pl.BlockSpec(memory_space=pltpu.VMEM)] * len(operands)
    if depth is not None or not begin:
        operands.append(place)
        in_specs.append(pl.BlockSpec(memory_space=pltpu.SMEM))

    def body(*refs):
        factor_kernel(begin, end, depth, refs[: len(operands)], refs[len(operands) :])

    return pl.pallas_call(
        body,
        out_shape=shapes,
        in_specs=in_specs,
        out_specs=[pl.BlockSpec(memory_space=pltpu.VMEM)] * len(shapes),
        compiler_params=pltpu.CompilerParams(vmem_limit_bytes=24 * MIB),
        cost_estimate=pl.CostEstimate(
            flops=1_500_000_000 * (end - begin), bytes_accessed=MIB, transcendentals=0
        ),
        name="factor",
    )(*operands)


def flip(value, bit, size):
    return lax.ppermute(value, "row", [(i, i ^ bit) for i in range(size)])


def exchange(value, step, bits):
    size = 2 << len(bits)
    return lax.ppermute(
        value, "row", [(i, i ^ (bits[-1 - step] if i & 1 else bits[step])) for i in range(size)]
    )


def relative_owners(bits):
    owners = [0]
    for bit in reversed(bits):
        owners = [owner | bit for owner in owners] + owners
    return owners


def gather_panel(shard, depth):
    shards = [shard]
    for _ in range(depth - 1):
        shards.append(lax.ppermute(shards[-1], "col", [(i, (i - 1) % depth) for i in range(depth)]))
    return shards


def local(panel_cols, window_cols):
    size = lax.axis_size("row")
    depth = lax.axis_size("col")
    here = lax.axis_index("row").astype(jnp.int32)
    place = jnp.stack([lax.axis_index("col").astype(jnp.int32), here & 1])
    bits = [1 << shift for shift in range(1, size.bit_length() - 1)]
    steps = len(bits)
    share = window_cols.shape[0] // size

    owners = [jnp.asarray(relative_owners(order), jnp.int32) for order in (bits, bits[::-1])]
    table_of = lambda device: device ^ jnp.where(device & 1, owners[1], owners[0])
    kept, given = table_of(here), table_of(here ^ 1)

    shards = gather_panel(panel_cols, depth)
    per = depth // GROUPS
    state = None
    sums = []
    for group in range(GROUPS):
        some = shards[group * per : (group + 1) * per]
        final = group == GROUPS - 1
        if final:
            whole, gram, gram_given = gram_call(place, shards)
            given = after(given, gram)
            gram = gram + flip(gram_given, 1, size)
        cross_given = cross_call(given, share, window_cols, some)
        arrived = flip(cross_given, 1, size)
        if final:
            cross_kept = cross_call(after(kept, gram), share, window_cols, some)
            gram_arrived = [exchange(gram, 0, bits)]
        else:
            cross_kept = cross_call(kept, share, window_cols, some)
        pairs = [(cross_kept, 0), (arrived, 0)]
        count = cross_kept.shape[0]
        blocks = whole.shape[0] // BLOCK if final else 0
        for step in range(steps):
            count //= 2
            out = sum(lax.slice_in_dim(array, at, at + count, axis=0) for array, at in pairs)
            if final and step == 0:
                gram = gram + gram_arrived[0]
                out = after(out, gram)
                for later in range(1, steps):
                    gram = gram + exchange(gram, later, bits)
                gram_other = flip(gram, 1, size)
                state = factor_call(0, blocks * 3 // 8, [gram, gram_other], place)
            elif final and step == 1:
                out = after(out, state[0])
                state = factor_call(blocks * 3 // 8, blocks * 6 // 8, state, place)
            pairs = [(array, at + count) for array, at in pairs] + [(exchange(out, step, bits), 0)]
        sums.append(sum(lax.slice_in_dim(array, at, at + count, axis=0) for array, at in pairs))
    sums[-1] = after(sums[-1], state[0])
    if steps < 2:
        state = factor_call(blocks * 3 // 8, blocks * 6 // 8, state, place)
    _, _, triangle, inverse, weight = factor_call(
        blocks * 6 // 8, blocks, state, place, whole, depth
    )

    near = sums
    for step in reversed(range(1, steps)):
        near = [jnp.concatenate([exchange(part, step, bits), part], 0) for part in near]
    near[-1] = after(near[-1], weight)
    far = [exchange(part, 0, bits) for part in near]
    middle = kept.shape[0] // 2
    residual = None
    for table, totals in (
        (kept[middle:], near),
        (given[middle:], [flip(part, 1, size) for part in near]),
    ):
        residual = residual_call(table, share, window_cols, weight, totals, residual)
    far[-1], residual = lax.optimization_barrier((far[-1], residual))
    for table, totals in (
        (kept[:middle], far),
        (given[:middle], [flip(part, 1, size) for part in far]),
    ):
        residual = residual_call(table, share, window_cols, weight, totals, residual)
    top_rows = dot(jnp.concatenate(sums, 1), inverse, ((1,), (1,)), precise)
    return triangle, top_rows, residual


def solution(mesh):
    return jax.shard_map(
        local,
        mesh=mesh,
        in_specs=(P("col", "row"), P("col", "row")),
        out_specs=(P(), P(("col", "row"), None), P("col", "row")),
        check_vma=False,
    )
```

```python
import functools

import jax
import jax.numpy as jnp
from jax import lax
from jax.experimental import pallas as pl
from jax.experimental.pallas import tpu as pltpu
from jax.sharding import PartitionSpec as P

precise = lax.Precision.HIGHEST
f32, bf16 = jnp.float32, jnp.bfloat16
BLOCK = 32
MIB = 1 << 20
STREAM = 50 * MIB
LONG = pl.CostEstimate(flops=100_000_000_000, bytes_accessed=1, transcendentals=0)
BRIEF = pl.CostEstimate(flops=1, bytes_accessed=1, transcendentals=0)


def dot(left, right, dims, precision=None):
    return lax.dot_general(
        left, right, (dims, ((), ())), precision=precision, preferred_element_type=f32
    )


def split(value):
    high = value.astype(bf16)
    return high, (value - high.astype(f32)).astype(bf16)


def full(shape):
    return pl.BlockSpec(shape, lambda i, *tables: (0, 0))


def after(value, *others):
    return lax.optimization_barrier((value, *others))[0]


def gram_kernel(place_ref, *refs):
    shards, (whole_ref, kept_ref, given_ref, gram_ref) = refs[:-4], refs[-4:]
    rows = shards[0].shape[0]
    for step, shard in enumerate(shards):
        owner = lax.rem(place_ref[0] + step, len(shards))
        whole_ref[pl.ds(pl.multiple_of(owner * rows, rows), rows), :] = shard[...]
    whole = whole_ref[...]
    gram_ref[...] = dot(whole, whole, ((1,), (1,)), precise)
    half = kept_ref.shape[0]
    side = place_ref[1]
    kept_ref[...] = gram_ref[pl.ds(pl.multiple_of(side * half, half), half), :]
    given_ref[...] = gram_ref[pl.ds(pl.multiple_of((1 - side) * half, half), half), :]


def gram_call(place, shards):
    rows, columns = shards[0].shape
    panel = rows * len(shards)
    return pl.pallas_call(
        gram_kernel,
        grid_spec=pltpu.PrefetchScalarGridSpec(
            num_scalar_prefetch=1,
            grid=(1,),
            in_specs=[full(shard.shape) for shard in shards],
            out_specs=[full((panel, columns)), full((panel // 2, panel)), full((panel // 2, panel))],
            scratch_shapes=[pltpu.VMEM((panel, panel), f32)],
        ),
        out_shape=[
            jax.ShapeDtypeStruct((panel, columns), f32),
            jax.ShapeDtypeStruct((panel // 2, panel), f32),
            jax.ShapeDtypeStruct((panel // 2, panel), f32),
        ],
        compiler_params=pltpu.CompilerParams(vmem_limit_bytes=24 * MIB),
        cost_estimate=LONG,
        name="gram",
    )(place, *shards)


def part_rows(share):
    return min(share, 256)


def window_copies(table_ref, window_ref, held, arrivals, share):
    part = part_rows(share)
    parts = share // part
    copies = []
    for place in range(table_ref.shape[0] * parts):
        start = pl.multiple_of(table_ref[place // parts] * share + place % parts * part, part)
        copies.append(
            pltpu.make_async_copy(
                window_ref.at[pl.ds(start, part), :],
                held.at[pl.ds(place * part, part), :],
                arrivals.at[place],
            )
        )
    return copies


def cross_kernel(terms, share, table_ref, window_ref, *refs):
    shards, (cross_ref, held, panel_ref, arrivals) = refs[:-4], refs[-4:]
    copies = window_copies(table_ref, window_ref, held, arrivals, share)
    for copy in copies:
        copy.start()
    width, columns = cross_ref.shape[1], window_ref.shape[1]
    rows = shards[0].shape[0]
    for place, shard in enumerate(shards):
        high, low = split(shard[...])
        here = slice(place * rows, (place + 1) * rows)
        beside = slice(width + place * rows, width + (place + 1) * rows)
        if terms == 2:
            for term in range(2):
                panel_ref[here, term * columns : (term + 1) * columns] = high
                panel_ref[beside, term * columns : (term + 1) * columns] = low
        else:
            for term, value in enumerate((high, low, high)):
                panel_ref[here, term * columns : (term + 1) * columns] = value

    part = part_rows(share)
    parts = share // part
    for place in range(table_ref.shape[0]):
        for copy in copies[place * parts : (place + 1) * parts]:
            copy.wait()
        here = slice(place * share, (place + 1) * share)
        high, low = split(held[here, :])
        if terms == 2:
            result = dot(jnp.concatenate([high, low], 1), panel_ref[...], ((1,), (1,)))
            cross_ref[here, :] = result[:, :width] + result[:, width:]
        else:
            cross_ref[here, :] = dot(
                jnp.concatenate([high, high, low], 1), panel_ref[...], ((1,), (1,))
            )


def cross_call(table, share, window, shards):
    shares, columns = table.shape[0], window.shape[1]
    width = shards[0].shape[0] * len(shards)
    terms = 2 if 2 * width <= 256 else 3
    return pl.pallas_call(
        functools.partial(cross_kernel, terms, share),
        in_specs=[
            pl.BlockSpec(memory_space=pltpu.SMEM),
            pl.BlockSpec(memory_space=pl.ANY),
        ]
        + [pl.BlockSpec(memory_space=pltpu.VMEM)] * len(shards),
        out_specs=pl.BlockSpec(memory_space=pltpu.VMEM),
        scratch_shapes=[
            pltpu.VMEM((shares * share, columns), f32),
            pltpu.VMEM((2 * width if terms == 2 else width, terms * columns), bf16),
            pltpu.SemaphoreType.DMA((shares * share // part_rows(share),)),
        ],
        out_shape=jax.ShapeDtypeStruct((shares * share, width), f32),
        compiler_params=pltpu.CompilerParams(vmem_limit_bytes=STREAM),
        cost_estimate=BRIEF,
        name="cross",
    )(table, window, *shards)


def residual_kernel(groups, share, table_ref, window_ref, weight_ref, *refs):
    totals, (out_ref, held, sent, arrivals, departures) = refs[:groups], refs[-5:]
    copies = window_copies(table_ref, window_ref, held, arrivals, share)
    for copy in copies:
        copy.start()
    part = part_rows(share)
    parts = share // part
    leaving = []
    for place in range(table_ref.shape[0] * parts):
        here = slice(place * part, (place + 1) * part)
        pairs = [split(total[here, :]) for total in totals]
        high, low = [jnp.concatenate(term, 1) for term in zip(*pairs)]
        product = dot(jnp.concatenate([high, high, low], 1), weight_ref[...], ((1,), (0,)))
        copies[place].wait()
        sent[here, :] = held[here, :] - product
        start = pl.multiple_of(table_ref[place // parts] * share + place % parts * part, part)
        leaving.append(
            pltpu.make_async_copy(
                sent.at[pl.ds(place * part, part), :],
                out_ref.at[pl.ds(start, part), :],
                departures.at[place],
            )
        )
        leaving[-1].start()
    for copy in leaving:
        copy.wait()


def residual_call(table, share, window, weight, totals, before):
    shares, columns = table.shape[0], window.shape[1]
    operands = [table, window, weight, *totals]
    in_specs = [pl.BlockSpec(memory_space=pltpu.SMEM), pl.BlockSpec(memory_space=pl.ANY)] + [
        pl.BlockSpec(memory_space=pltpu.VMEM)
    ] * (1 + len(totals))
    aliases = {}
    if before is not None:
        aliases = {len(operands): 0}
        operands.append(before)
        in_specs.append(pl.BlockSpec(memory_space=pl.ANY))
    return pl.pallas_call(
        functools.partial(residual_kernel, len(totals), share),
        in_specs=in_specs,
        out_specs=pl.BlockSpec(memory_space=pl.ANY),
        scratch_shapes=[
            pltpu.VMEM((shares * share, columns), f32),
            pltpu.VMEM((shares * share, columns), f32),
            pltpu.SemaphoreType.DMA((shares * share // part_rows(share),)),
            pltpu.SemaphoreType.DMA((shares * share // part_rows(share),)),
        ],
        out_shape=jax.ShapeDtypeStruct(window.shape, f32),
        input_output_aliases=aliases,
        compiler_params=pltpu.CompilerParams(vmem_limit_bytes=STREAM),
        cost_estimate=BRIEF,
        name="residual",
    )(*operands)


def eliminate(diagonal):
    size, lanes, tile = BLOCK, 128, 8
    tiles = size // tile
    row_at = [lax.broadcasted_iota(jnp.int32, (tile, lanes), 0) + tile * t for t in range(tiles)]
    lane_at = lax.broadcasted_iota(jnp.int32, (tile, lanes), 1)
    spread = [
        [
            jnp.broadcast_to(diagonal[tile * t : tile * (t + 1), k : k + 1], (tile, lanes))
            for t in range(tiles)
        ]
        for k in range(size)
    ]
    inverse = [jnp.where(row_at[t] == lane_at, 1.0, 0.0) for t in range(tiles)]
    lower = [jnp.zeros((tile, lanes), f32) for _ in range(tiles)]
    scale = [jnp.zeros((tile, lanes), f32) for _ in range(tiles)]
    for j in range(size):
        own, at = j // tile, j % tile
        pivot = spread[j][own][at : at + 1, :]
        reciprocal = 1.0 / pivot
        root = lax.rsqrt(pivot)
        inverse_row = inverse[own][at : at + 1, :]
        factor = {}
        for t in range(own, tiles):
            column = spread[j][t]
            factor[t] = column * reciprocal
            if t == own:
                factor[t] = jnp.where(row_at[t] > j, factor[t], 0.0)
                scale[t] = jnp.where(row_at[t] == j, root, scale[t])
                lower[t] = jnp.where((lane_at == j) & (row_at[t] >= j), column * root, lower[t])
            else:
                lower[t] = jnp.where(lane_at == j, column * root, lower[t])
            inverse[t] = inverse[t] - factor[t] * inverse_row
        for k in range(j + 1, size):
            entry = spread[j][k // tile][k % tile : k % tile + 1, :]
            for t in range(k // tile, tiles):
                spread[k][t] = spread[k][t] - factor[t] * entry
    inverse = [inverse[t] * scale[t] for t in range(tiles)]
    return jnp.concatenate(lower, 0), jnp.concatenate(inverse, 0)


def factor_kernel(begin, end, depth, ins, outs):
    last = depth is not None
    state_ref, lower_ref = outs[:2]
    if begin:
        state_ref[...] = ins[0][...]
        lower_ref[...] = ins[1][...]
    else:
        half, side = ins[0].shape[0], ins[2][1]
        state_ref[pl.ds(pl.multiple_of(side * half, half), half), :] = ins[0][...]
        state_ref[pl.ds(pl.multiple_of((1 - side) * half, half), half), :] = ins[1][...]
    size = state_ref.shape[0]
    column_at = lax.broadcasted_iota(jnp.int32, (BLOCK, size), 1)
    row_at = lax.broadcasted_iota(jnp.int32, (BLOCK, size), 0)
    for step in range(begin, end):
        start, stop = step * BLOCK, (step + 1) * BLOCK
        rows = state_ref[start:stop, :]
        lower, inverse = eliminate(rows[:, start:stop])
        lower_ref[start:stop, :] = lower
        inside = (column_at >= start) & (column_at < stop)
        rows = jnp.where(inside, jnp.where(column_at - start == row_at, 1.0, 0.0), rows)
        done = dot(inverse[:, :BLOCK], rows, ((1,), (0,)), precise)
        state_ref[start:stop, :] = done
        if stop < size:
            upper = jnp.where(column_at >= stop, done, 0.0)
            update = dot(upper, done, ((0,), (0,)), precise)[stop:, :]
            below_at = lax.broadcasted_iota(jnp.int32, (size - stop, size), 1)
            below = jnp.where(
                (below_at >= start) & (below_at < stop), 0.0, state_ref[stop:, :]
            )
            state_ref[stop:, :] = below - update
    if last:
        whole_ref, place_ref = ins[2:]
        triangle_ref, inverse_ref, weight_ref = outs[2:]
        column_at = lax.broadcasted_iota(jnp.int32, (size, size), 1)
        row_at = lax.broadcasted_iota(jnp.int32, (size, size), 0)
        edge = (row_at // BLOCK + 1) * BLOCK
        state = state_ref[...]
        inverse = jnp.where(column_at <= row_at, state, 0.0)
        lower = lower_ref[...]
        wide = jnp.concatenate([lower] * (size // lower.shape[1]), 1)
        for step in range(size // BLOCK):
            start, stop = step * BLOCK, (step + 1) * BLOCK
            shift = start % lower.shape[1]
            part = wide[start:stop, :]
            if shift:
                part = pltpu.roll(part, shift, 1)
            lower_full = jnp.where(
                (column_at[start:stop, :] >= start) & (column_at[start:stop, :] < stop), part, 0.0
            )
            state_ref[start:stop, :] = lower_full
        triangle_ref[...] = jnp.where(column_at >= edge, state, 0.0) + state_ref[...].T
        half = dot(inverse, whole_ref[...], ((1,), (0,)), precise)
        shift = lax.rem(size - place_ref[0] * (size // depth), size)
        inverse = pltpu.roll(inverse, shift, 1)
        inverse_ref[...] = inverse
        weight = dot(inverse, half, ((0,), (0,)), precise)
        for term, part in enumerate(split(weight) + split(weight)[:1]):
            weight_ref[term * size : (term + 1) * size, :] = part


def factor_call(begin, end, operands, place, whole=None, depth=None):
    size = operands[0].shape[1]
    operands = list(operands)
    shapes = [
        jax.ShapeDtypeStruct((size, size), f32),
        jax.ShapeDtypeStruct((size, 128), f32),
    ]
    if depth is not None:
        operands.append(whole)
        shapes += [
            jax.ShapeDtypeStruct((size, size), f32),
            jax.ShapeDtypeStruct((size, size), f32),
            jax.ShapeDtypeStruct((3 * size, whole.shape[1]), bf16),
        ]
    in_specs = [pl.BlockSpec(memory_space=pltpu.VMEM)] * len(operands)
    if depth is not None or not begin:
        operands.append(place)
        in_specs.append(pl.BlockSpec(memory_space=pltpu.SMEM))

    def body(*refs):
        factor_kernel(begin, end, depth, refs[: len(operands)], refs[len(operands) :])

    return pl.pallas_call(
        body,
        out_shape=shapes,
        in_specs=in_specs,
        out_specs=[pl.BlockSpec(memory_space=pltpu.VMEM)] * len(shapes),
        compiler_params=pltpu.CompilerParams(vmem_limit_bytes=24 * MIB),
        cost_estimate=BRIEF,
        name="factor",
    )(*operands)


def flip(value, bit, size):
    return lax.ppermute(value, "row", [(i, i ^ bit) for i in range(size)])


def exchange(value, step, bits):
    size = 2 << len(bits)
    return lax.ppermute(
        value, "row", [(i, i ^ (bits[-1 - step] if i & 1 else bits[step])) for i in range(size)]
    )


def relative_owners(bits):
    owners = [0]
    for bit in reversed(bits):
        owners = [owner | bit for owner in owners] + owners
    return owners


def sum_shares(kept, arrived, bits):
    pairs, count = [(kept, 0), (arrived, 0)], kept.shape[0]
    cut = lambda array, at: lax.slice_in_dim(array, at, at + count, axis=0)
    for step in range(len(bits)):
        count //= 2
        out = yield sum(cut(array, at) for array, at in pairs)
        pairs = [(array, at + count) for array, at in pairs] + [(exchange(out, step, bits), 0)]
    yield sum(cut(array, at) for array, at in pairs)


def gather_panel(shard, depth):
    up = [(i, (i - 1) % depth) for i in range(depth)]
    down = [(i, (i + 1) % depth) for i in range(depth)]
    above = [lax.ppermute(shard, "col", up)]
    below = []
    later, _ = lax.optimization_barrier((shard, above[0]))
    for step in range(2, depth):
        if step % 2 == 0:
            above.append(lax.ppermute(above[-1], "col", up))
        else:
            below.append(lax.ppermute(below[-1] if below else later, "col", down))
    return [shard, *above, *below[::-1]]


def spread(part, bits):
    for step in reversed(range(1, len(bits))):
        part = jnp.concatenate([exchange(part, step, bits), part], 0)
    return part


def local(panel_cols, window_cols):
    size = lax.axis_size("row")
    depth = lax.axis_size("col")
    here = lax.axis_index("row").astype(jnp.int32)
    place = jnp.stack([lax.axis_index("col").astype(jnp.int32), here & 1])
    bits = [1 << shift for shift in range(1, size.bit_length() - 1)]
    steps = len(bits)
    share = window_cols.shape[0] // size

    owners = [jnp.asarray(relative_owners(order), jnp.int32) for order in (bits, bits[::-1])]
    table_of = lambda device: device ^ jnp.where(device & 1, owners[1], owners[0])
    kept, given = table_of(here), table_of(here ^ 1)

    shards = gather_panel(panel_cols, depth)
    per = depth // 2
    sent, late = shards[:per], shards[per:]

    cross_given = cross_call(given, share, window_cols, sent)
    arrived = flip(cross_given, 1, size)
    cross_kept = cross_call(after(kept, cross_given), share, window_cols, sent)
    early = sum_shares(cross_kept, arrived, bits)
    early_sum = next(early)
    late[0] = after(late[0], early_sum)
    early_sum = early.send(early_sum)

    whole, gram, gram_given = gram_call(place, sent + late)
    given_late = after(given, gram, early_sum)
    gram = gram + flip(gram_given, 1, size)
    cross_given = cross_call(given_late, share, window_cols, late)
    arrived = flip(cross_given, 1, size)
    for _ in range(1, steps):
        early_sum = early.send(early_sum)
    cross_kept = cross_call(after(kept, gram, early_sum), share, window_cols, late)
    gram = gram + exchange(gram, 0, bits)
    rest = sum_shares(cross_kept, arrived, bits)
    late_sum = after(next(rest), gram)
    for step in range(1, steps):
        gram = gram + exchange(gram, step, bits)

    blocks = whole.shape[0] // BLOCK
    cuts = (0, blocks * 3 // 8, blocks * 6 // 8, blocks)
    state = factor_call(0, cuts[1], [gram, flip(gram, 1, size)], place)
    early_near = spread(early_sum, bits)
    late_sum = after(rest.send(late_sum), state[0], early_near)
    state = factor_call(cuts[1], cuts[2], state, place)
    for _ in range(1, steps):
        late_sum = rest.send(late_sum)
    late_sum = after(late_sum, state[0])
    _, _, triangle, inverse, weight = factor_call(
        cuts[2], blocks, state, place, whole, depth
    )

    near = [early_near, after(spread(late_sum, bits), weight)]
    far = [exchange(part, 0, bits) for part in near]
    middle = kept.shape[0] // 2
    residual = None
    for table, totals in (
        (kept[middle:], near),
        (given[middle:], [flip(part, 1, size) for part in near]),
    ):
        residual = residual_call(table, share, window_cols, weight, totals, residual)
    far[-1], residual = lax.optimization_barrier((far[-1], residual))
    for table, totals in (
        (kept[:middle], far),
        (given[:middle], [flip(part, 1, size) for part in far]),
    ):
        residual = residual_call(table, share, window_cols, weight, totals, residual)
    top_rows = dot(jnp.concatenate([early_sum, late_sum], 1), inverse, ((1,), (1,)), precise)
    return triangle, top_rows, residual


def solution(mesh):
    return jax.shard_map(
        local,
        mesh=mesh,
        in_specs=(P("col", "row"), P("col", "row")),
        out_specs=(P(), P(("col", "row"), None), P("col", "row")),
        check_vma=False,
    )
```

```python
import functools

import jax
import jax.numpy as jnp
from jax import lax
from jax.experimental import pallas as pl
from jax.experimental.pallas import tpu as pltpu
from jax.sharding import PartitionSpec as P

precise = lax.Precision.HIGHEST
f32, bf16 = jnp.float32, jnp.bfloat16
BLOCK = 32
MIB = 1 << 20
ROOM = 28 * MIB
LONG = pl.CostEstimate(flops=100_000_000_000, bytes_accessed=1, transcendentals=0)
BRIEF = pl.CostEstimate(flops=1, bytes_accessed=1, transcendentals=0)


def dot(left, right, dims, precision=None):
    return lax.dot_general(
        left, right, (dims, ((), ())), precision=precision, preferred_element_type=f32
    )


def split(value):
    high = value.astype(bf16)
    return high, (value - high.astype(f32)).astype(bf16)


def dot3(left, right_high, right_low, dims):
    left_high, left_low = split(left)
    return dot(left_high, right_high, dims) + (
        dot(left_high, right_low, dims) + dot(left_low, right_high, dims)
    )


def full(shape):
    return pl.BlockSpec(shape, lambda i, *tables: (0, 0))


def after(value, *others):
    return lax.optimization_barrier((value, *others))[0]


def gram_kernel(place_ref, *refs):
    shards, (whole_ref, high_ref, low_ref, kept_ref, given_ref, gram_ref) = refs[:-6], refs[-6:]
    rows = shards[0].shape[0]
    for step, shard in enumerate(shards):
        owner = lax.rem(place_ref[0] + step, len(shards))
        whole_ref[pl.ds(pl.multiple_of(owner * rows, rows), rows), :] = shard[...]
    whole = whole_ref[...]
    gram_ref[...] = dot(whole, whole, ((1,), (1,)), precise)
    high_ref[...], low_ref[...] = split(whole)
    half = kept_ref.shape[0]
    side = place_ref[1]
    kept_ref[...] = gram_ref[pl.ds(pl.multiple_of(side * half, half), half), :]
    given_ref[...] = gram_ref[pl.ds(pl.multiple_of((1 - side) * half, half), half), :]


def gram_call(place, shards):
    rows, columns = shards[0].shape
    panel = rows * len(shards)
    return pl.pallas_call(
        gram_kernel,
        grid_spec=pltpu.PrefetchScalarGridSpec(
            num_scalar_prefetch=1,
            grid=(1,),
            in_specs=[full(shard.shape) for shard in shards],
            out_specs=[full((panel, columns))] * 3 + [full((panel // 2, panel))] * 2,
            scratch_shapes=[pltpu.VMEM((panel, panel), f32)],
        ),
        out_shape=[
            jax.ShapeDtypeStruct((panel, columns), f32),
            jax.ShapeDtypeStruct((panel, columns), bf16),
            jax.ShapeDtypeStruct((panel, columns), bf16),
            jax.ShapeDtypeStruct((panel // 2, panel), f32),
            jax.ShapeDtypeStruct((panel // 2, panel), f32),
        ],
        compiler_params=pltpu.CompilerParams(vmem_limit_bytes=24 * MIB),
        cost_estimate=LONG,
        name="gram",
    )(place, *shards)


def hold_kernel(window_ref, held_ref, arrivals):
    count = arrivals.shape[0]
    rows = window_ref.shape[0] // count
    copies = [
        pltpu.make_async_copy(
            window_ref.at[pl.ds(place * rows, rows), :],
            held_ref.at[pl.ds(place * rows, rows), :],
            arrivals.at[place],
        )
        for place in range(count)
    ]
    for copy in copies:
        copy.start()
    for copy in copies:
        copy.wait()


def hold_call(window):
    return pl.pallas_call(
        hold_kernel,
        in_specs=[pl.BlockSpec(memory_space=pl.ANY)],
        out_specs=pl.BlockSpec(memory_space=pltpu.VMEM),
        scratch_shapes=[pltpu.SemaphoreType.DMA((8,))],
        out_shape=jax.ShapeDtypeStruct(window.shape, f32),
        compiler_params=pltpu.CompilerParams(vmem_limit_bytes=ROOM),
        cost_estimate=BRIEF,
        name="hold",
    )(window)


def cross_kernel(count, table_ref, window_ref, high_ref, low_ref, cross_ref):
    tile = cross_ref.shape[0] // count

    @pl.loop(0, count)
    def _(place):
        rows = window_ref[pl.ds(pl.multiple_of(table_ref[place], tile), tile), :]
        cross_ref[pl.ds(pl.multiple_of(place * tile, tile), tile), :] = dot3(
            rows, high_ref[...], low_ref[...], ((1,), (1,))
        )


def cross_call(table, tile, window, high, low):
    count, panel = table.shape[0], high.shape[0]
    in_vmem = pl.BlockSpec(memory_space=pltpu.VMEM)
    return pl.pallas_call(
        functools.partial(cross_kernel, count),
        in_specs=[pl.BlockSpec(memory_space=pltpu.SMEM), in_vmem, in_vmem, in_vmem],
        out_specs=in_vmem,
        out_shape=jax.ShapeDtypeStruct((count * tile, panel), f32),
        compiler_params=pltpu.CompilerParams(vmem_limit_bytes=ROOM),
        cost_estimate=BRIEF,
        name="cross",
    )(table, window, high, low)


def residual_kernel(parts, table_ref, window_ref, high_ref, low_ref, *refs):
    totals, (out_ref, sent, departures) = refs[:parts], refs[-3:]
    tile = sent.shape[1]
    each = table_ref.shape[0] // parts

    def leaving(place):
        start = pl.multiple_of(table_ref[place], tile)
        return pltpu.make_async_copy(
            sent.at[place], out_ref.at[pl.ds(start, tile), :], departures.at[place]
        )

    for part, total in enumerate(totals):

        @pl.loop(0, each)
        def _(step):
            place = part * each + step
            start = pl.multiple_of(table_ref[place], tile)
            rows = total[pl.ds(pl.multiple_of(step * tile, tile), tile), :]
            product = dot3(rows, high_ref[...], low_ref[...], ((1,), (0,)))
            sent[place] = window_ref[pl.ds(start, tile), :] - product
            leaving(place).start()

    @pl.loop(0, parts * each)
    def _(place):
        leaving(place).wait()


def residual_call(table, tile, window, high, low, totals, before):
    count, columns = table.shape[0], window.shape[1]
    in_vmem = pl.BlockSpec(memory_space=pltpu.VMEM)
    operands = [table, window, high, low, *totals]
    in_specs = [pl.BlockSpec(memory_space=pltpu.SMEM)] + [in_vmem] * (len(operands) - 1)
    aliases = {}
    if before is not None:
        aliases = {len(operands): 0}
        operands.append(before)
        in_specs.append(pl.BlockSpec(memory_space=pl.ANY))
    return pl.pallas_call(
        functools.partial(residual_kernel, len(totals)),
        in_specs=in_specs,
        out_specs=pl.BlockSpec(memory_space=pl.ANY),
        scratch_shapes=[
            pltpu.VMEM((count, tile, columns), f32),
            pltpu.SemaphoreType.DMA((count,)),
        ],
        out_shape=jax.ShapeDtypeStruct(window.shape, f32),
        input_output_aliases=aliases,
        compiler_params=pltpu.CompilerParams(vmem_limit_bytes=ROOM),
        cost_estimate=BRIEF,
        name="residual",
    )(*operands)


def eliminate(diagonal):
    size, lanes, tile = BLOCK, 128, 8
    tiles = size // tile
    row_at = [lax.broadcasted_iota(jnp.int32, (tile, lanes), 0) + tile * t for t in range(tiles)]
    lane_at = lax.broadcasted_iota(jnp.int32, (tile, lanes), 1)
    spread = [
        [
            jnp.broadcast_to(diagonal[tile * t : tile * (t + 1), k : k + 1], (tile, lanes))
            for t in range(tiles)
        ]
        for k in range(size)
    ]
    inverse = [jnp.where(row_at[t] == lane_at, 1.0, 0.0) for t in range(tiles)]
    lower = [jnp.zeros((tile, lanes), f32) for _ in range(tiles)]
    scale = [jnp.zeros((tile, lanes), f32) for _ in range(tiles)]
    for j in range(size):
        own, at = j // tile, j % tile
        pivot = spread[j][own][at : at + 1, :]
        reciprocal = 1.0 / pivot
        root = lax.rsqrt(pivot)
        inverse_row = inverse[own][at : at + 1, :]
        factor = {}
        for t in range(own, tiles):
            column = spread[j][t]
            factor[t] = column * reciprocal
            if t == own:
                factor[t] = jnp.where(row_at[t] > j, factor[t], 0.0)
                scale[t] = jnp.where(row_at[t] == j, root, scale[t])
                lower[t] = jnp.where((lane_at == j) & (row_at[t] >= j), column * root, lower[t])
            else:
                lower[t] = jnp.where(lane_at == j, column * root, lower[t])
            inverse[t] = inverse[t] - factor[t] * inverse_row
        for k in range(j + 1, size):
            entry = spread[j][k // tile][k % tile : k % tile + 1, :]
            for t in range(k // tile, tiles):
                spread[k][t] = spread[k][t] - factor[t] * entry
    inverse = [inverse[t] * scale[t] for t in range(tiles)]
    return jnp.concatenate(lower, 0), jnp.concatenate(inverse, 0)


def factor_kernel(begin, end, last, ins, outs):
    state_ref, lower_ref = outs[:2]
    if begin:
        state_ref[...] = ins[0][...]
        lower_ref[...] = ins[1][...]
    else:
        half, side = ins[0].shape[0], ins[2][1]
        state_ref[pl.ds(pl.multiple_of(side * half, half), half), :] = ins[0][...]
        state_ref[pl.ds(pl.multiple_of((1 - side) * half, half), half), :] = ins[1][...]
    size = state_ref.shape[0]
    column_at = lax.broadcasted_iota(jnp.int32, (BLOCK, size), 1)
    row_at = lax.broadcasted_iota(jnp.int32, (BLOCK, size), 0)
    for step in range(begin, end):
        start, stop = step * BLOCK, (step + 1) * BLOCK
        rows = state_ref[start:stop, :]
        lower, inverse = eliminate(rows[:, start:stop])
        lower_ref[start:stop, :] = lower
        inside = (column_at >= start) & (column_at < stop)
        rows = jnp.where(inside, jnp.where(column_at - start == row_at, 1.0, 0.0), rows)
        done = dot(inverse[:, :BLOCK], rows, ((1,), (0,)), precise)
        state_ref[start:stop, :] = done
        if stop < size:
            upper = jnp.where(column_at >= stop, done, 0.0)
            update = dot(upper, done, ((0,), (0,)), precise)[stop:, :]
            below_at = lax.broadcasted_iota(jnp.int32, (size - stop, size), 1)
            below = jnp.where(
                (below_at >= start) & (below_at < stop), 0.0, state_ref[stop:, :]
            )
            state_ref[stop:, :] = below - update
    if last:
        whole_ref = ins[2]
        triangle_ref, inverse_ref, high_ref, low_ref = outs[2:]
        column_at = lax.broadcasted_iota(jnp.int32, (size, size), 1)
        row_at = lax.broadcasted_iota(jnp.int32, (size, size), 0)
        edge = (row_at // BLOCK + 1) * BLOCK
        state = state_ref[...]
        inverse = jnp.where(column_at <= row_at, state, 0.0)
        lower = lower_ref[...]
        wide = jnp.concatenate([lower] * (size // lower.shape[1]), 1)
        for step in range(size // BLOCK):
            start, stop = step * BLOCK, (step + 1) * BLOCK
            shift = start % lower.shape[1]
            part = wide[start:stop, :]
            if shift:
                part = pltpu.roll(part, shift, 1)
            lower_full = jnp.where(
                (column_at[start:stop, :] >= start) & (column_at[start:stop, :] < stop), part, 0.0
            )
            state_ref[start:stop, :] = lower_full
        triangle_ref[...] = jnp.where(column_at >= edge, state, 0.0) + state_ref[...].T
        half = dot(inverse, whole_ref[...], ((1,), (0,)), precise)
        inverse_ref[...] = inverse
        weight = dot(inverse, half, ((0,), (0,)), precise)
        high_ref[...], low_ref[...] = split(weight)


def factor_call(begin, end, operands, place=None, whole=None):
    size = operands[0].shape[1]
    operands = list(operands)
    shapes = [
        jax.ShapeDtypeStruct((size, size), f32),
        jax.ShapeDtypeStruct((size, 128), f32),
    ]
    if whole is not None:
        operands.append(whole)
        shapes += [
            jax.ShapeDtypeStruct((size, size), f32),
            jax.ShapeDtypeStruct((size, size), f32),
            jax.ShapeDtypeStruct((size, whole.shape[1]), bf16),
            jax.ShapeDtypeStruct((size, whole.shape[1]), bf16),
        ]
    in_specs = [pl.BlockSpec(memory_space=pltpu.VMEM)] * len(operands)
    if not begin:
        operands.append(place)
        in_specs.append(pl.BlockSpec(memory_space=pltpu.SMEM))

    def body(*refs):
        factor_kernel(begin, end, whole is not None, refs[: len(operands)], refs[len(operands) :])

    return pl.pallas_call(
        body,
        out_shape=shapes,
        in_specs=in_specs,
        out_specs=[pl.BlockSpec(memory_space=pltpu.VMEM)] * len(shapes),
        compiler_params=pltpu.CompilerParams(vmem_limit_bytes=24 * MIB),
        cost_estimate=BRIEF,
        name="factor",
    )(*operands)


def flip(value, bit, size):
    return lax.ppermute(value, "row", [(i, i ^ bit) for i in range(size)])


def exchange(value, step, bits):
    size = 2 << len(bits)
    return lax.ppermute(
        value, "row", [(i, i ^ (bits[-1 - step] if i & 1 else bits[step])) for i in range(size)]
    )


def relative_owners(bits):
    owners = [0]
    for bit in reversed(bits):
        owners = [owner | bit for owner in owners] + owners
    return owners


def sum_shares(kept, arrived, bits):
    pairs, count = [(kept, 0), (arrived, 0)], kept.shape[0]
    cut = lambda array, at: lax.slice_in_dim(array, at, at + count, axis=0)
    for step in range(len(bits)):
        count //= 2
        out = yield sum(cut(array, at) for array, at in pairs)
        pairs = [(array, at + count) for array, at in pairs] + [(exchange(out, step, bits), 0)]
    yield sum(cut(array, at) for array, at in pairs)


def gather_panel(shard, depth):
    up = [(i, (i - 1) % depth) for i in range(depth)]
    down = [(i, (i + 1) % depth) for i in range(depth)]
    above = [lax.ppermute(shard, "col", up)]
    below = []
    later, _ = lax.optimization_barrier((shard, above[0]))
    for step in range(2, depth):
        if step % 2 == 0:
            above.append(lax.ppermute(above[-1], "col", up))
        else:
            below.append(lax.ppermute(below[-1] if below else later, "col", down))
    return [shard, *above, *below[::-1]]


def spread(part, bits):
    for step in reversed(range(1, len(bits))):
        part = jnp.concatenate([exchange(part, step, bits), part], 0)
    return part


def local(panel_cols, window_cols):
    size = lax.axis_size("row")
    depth = lax.axis_size("col")
    here = lax.axis_index("row").astype(jnp.int32)
    place = jnp.stack([lax.axis_index("col").astype(jnp.int32), here & 1])
    bits = [1 << shift for shift in range(1, size.bit_length() - 1)]
    steps = len(bits)
    share = window_cols.shape[0] // size

    owners = [jnp.asarray(relative_owners(order), jnp.int32) for order in (bits, bits[::-1])]
    table_of = lambda device: device ^ jnp.where(device & 1, owners[1], owners[0])
    kept, given = table_of(here), table_of(here ^ 1)

    tile = share // 2
    tables = lambda half: [owners * share + half * tile for owners in (kept, given)]

    whole, high, low, gram, gram_given = gram_call(place, gather_panel(panel_cols, depth))
    window = hold_call(window_cols)

    def products(half, *others):
        kept_rows, given_rows = tables(half)
        cross_given = cross_call(after(given_rows, *others), tile, window, high, low)
        cross_kept = cross_call(after(kept_rows, cross_given), tile, window, high, low)
        return sum_shares(cross_kept, flip(cross_given, 1, size), bits)

    early = products(0, gram)
    gram = gram + flip(gram_given, 1, size)
    early_sum = next(early)
    late = products(1, early_sum, gram)
    gram = gram + exchange(gram, 0, bits)
    late_sum = after(next(late), gram)
    early_sum = early.send(early_sum)
    gram = after(gram, early_sum)
    for step in range(1, steps):
        gram = gram + exchange(gram, step, bits)

    blocks = whole.shape[0] // BLOCK
    cuts = (0, blocks * 3 // 8, blocks * 6 // 8, blocks)
    state = factor_call(0, cuts[1], [gram, flip(gram, 1, size)], place)
    for _ in range(1, steps):
        early_sum = early.send(early_sum)
    late_sum = after(late.send(late_sum), state[0], early_sum)
    state = factor_call(cuts[1], cuts[2], [after(state[0], late_sum), state[1]])
    for _ in range(1, steps):
        late_sum = late.send(late_sum)
    late_sum = after(late_sum, state[0])
    early_near = spread(early_sum, bits)
    _, _, triangle, inverse, high, low = factor_call(
        cuts[2], blocks, [after(state[0], late_sum, early_near), state[1]], None, whole
    )

    late_near = after(spread(late_sum, bits), high)
    middle = kept.shape[0] // 2
    both = lambda side, part: jnp.concatenate([tables(half)[side][part] for half in (0, 1)])
    nearer, farther = slice(middle, None), slice(middle)
    early_far, late_far = [exchange(part, 0, bits) for part in (early_near, late_near)]
    residual = residual_call(
        both(0, nearer), tile, window, high, low, [early_near, late_near], None
    )
    near = [flip(part, 1, size) for part in (early_near, late_near)]
    residual = residual_call(both(1, nearer), tile, window, high, low, near, residual)
    early_far, residual = lax.optimization_barrier((early_far, residual))
    far_tables = [[tables(half)[side][farther] for side in (0, 1)] for half in (0, 1)]
    residual = residual_call(far_tables[0][0], tile, window, high, low, [early_far], residual)
    late_far, residual = lax.optimization_barrier((late_far, residual))
    mixed = jnp.concatenate([far_tables[0][1], far_tables[1][0]])
    parts = [flip(early_far, 1, size), late_far]
    residual = residual_call(mixed, tile, window, high, low, parts, residual)
    parts = [flip(late_far, 1, size)]
    residual = residual_call(far_tables[1][1], tile, window, high, low, parts, residual)
    summed = jnp.concatenate([early_sum, late_sum], 0)
    top_rows = dot(summed, inverse, ((1,), (1,)), precise)
    return triangle, top_rows, residual


def solution(mesh):
    return jax.shard_map(
        local,
        mesh=mesh,
        in_specs=(P("col", "row"), P("col", "row")),
        out_specs=(P(), P(("col", "row"), None), P("col", "row")),
        check_vma=False,
    )
```

```python
import functools

import jax
import jax.numpy as jnp
from jax import lax
from jax.experimental import pallas as pl
from jax.experimental.pallas import tpu as pltpu
from jax.sharding import PartitionSpec as P

precise = lax.Precision.HIGHEST
f32, bf16 = jnp.float32, jnp.bfloat16
BLOCK = 32
MIB = 1 << 20
ROOM = 28 * MIB
LONG = pl.CostEstimate(flops=100_000_000_000, bytes_accessed=1, transcendentals=0)
BRIEF = pl.CostEstimate(flops=1, bytes_accessed=1, transcendentals=0)


def dot(left, right, dims, precision=None):
    return lax.dot_general(
        left, right, (dims, ((), ())), precision=precision, preferred_element_type=f32
    )


def split(value):
    high = value.astype(bf16)
    return high, (value - high.astype(f32)).astype(bf16)


def full(shape):
    return pl.BlockSpec(shape, lambda i, *tables: (0, 0))


def after(value, *others):
    return lax.optimization_barrier((value, *others))[0]


def gram_kernel(place_ref, *refs):
    shards, (whole_ref, high_ref, low_ref, kept_ref, given_ref, gram_ref) = refs[:-6], refs[-6:]
    rows = shards[0].shape[0]
    for step, shard in enumerate(shards):
        owner = lax.rem(place_ref[0] + step, len(shards))
        whole_ref[pl.ds(pl.multiple_of(owner * rows, rows), rows), :] = shard[...]
    whole = whole_ref[...]
    gram_ref[...] = dot(whole, whole, ((1,), (1,)), precise)
    high_ref[...], low_ref[...] = split(whole)
    half = kept_ref.shape[0]
    side = place_ref[1]
    kept_ref[...] = gram_ref[pl.ds(pl.multiple_of(side * half, half), half), :]
    given_ref[...] = gram_ref[pl.ds(pl.multiple_of((1 - side) * half, half), half), :]


def gram_call(place, shards):
    rows, columns = shards[0].shape
    panel = rows * len(shards)
    return pl.pallas_call(
        gram_kernel,
        grid_spec=pltpu.PrefetchScalarGridSpec(
            num_scalar_prefetch=1,
            grid=(1,),
            in_specs=[full(shard.shape) for shard in shards],
            out_specs=[full((panel, columns))] * 3 + [full((panel // 2, panel))] * 2,
            scratch_shapes=[pltpu.VMEM((panel, panel), f32)],
        ),
        out_shape=[
            jax.ShapeDtypeStruct((panel, columns), f32),
            jax.ShapeDtypeStruct((panel, columns), bf16),
            jax.ShapeDtypeStruct((panel, columns), bf16),
            jax.ShapeDtypeStruct((panel // 2, panel), f32),
            jax.ShapeDtypeStruct((panel // 2, panel), f32),
        ],
        compiler_params=pltpu.CompilerParams(vmem_limit_bytes=24 * MIB),
        cost_estimate=LONG,
        name="gram",
    )(place, *shards)


def hold_kernel(table_ref, place_ref, window_ref, high_ref, low_ref, held, arrivals):
    slots, rows, _ = held.shape
    count = window_ref.shape[0] // rows

    def arriving(step):
        start = pl.multiple_of(step * rows, rows)
        slot = lax.rem(step, slots)
        return pltpu.make_async_copy(
            window_ref.at[pl.ds(start, rows), :], held.at[slot], arrivals.at[slot]
        )

    for step in range(min(slots, count)):
        arriving(step).start()

    @pl.loop(0, count)
    def _(step):
        arriving(step).wait()
        high, low = split(held[lax.rem(step, slots)])
        here = pl.ds(pl.multiple_of(step * rows, rows), rows)
        high_ref[here, :] = high
        low_ref[here, :] = low

        @pl.when(step + slots < count)
        def _():
            arriving(step + slots).start()


def hold_call(table, place, window):
    rows, columns = window.shape
    tile = min(256, rows)
    scalars = pl.BlockSpec(memory_space=pltpu.SMEM)
    return pl.pallas_call(
        hold_kernel,
        in_specs=[scalars, scalars, pl.BlockSpec(memory_space=pl.ANY)],
        out_specs=[pl.BlockSpec(memory_space=pltpu.VMEM)] * 2,
        scratch_shapes=[
            pltpu.VMEM((4, tile, columns), f32),
            pltpu.SemaphoreType.DMA((4,)),
        ],
        out_shape=[jax.ShapeDtypeStruct(window.shape, bf16)] * 2,
        compiler_params=pltpu.CompilerParams(vmem_limit_bytes=ROOM),
        cost_estimate=BRIEF,
        name="hold",
    )(table, place, window)


def cross_kernel(first, each, table_ref, window_high, window_low, high_ref, low_ref, *outs):
    tile = outs[0].shape[0] // each
    dims = ((1,), (1,))
    for part, cross_ref in enumerate(outs):

        @pl.loop(0, each)
        def _(step):
            entry = first + part * each + step
            rows = pl.ds(pl.multiple_of(table_ref[entry], tile), tile)
            here = pl.ds(pl.multiple_of(step * tile, tile), tile)
            cross_ref[here, :] = dot(window_high[rows, :], high_ref[...], dims) + (
                dot(window_high[rows, :], low_ref[...], dims)
                + dot(window_low[rows, :], high_ref[...], dims)
            )


def cross_call(table, first, parts, each, tile, window, panel):
    in_vmem = pl.BlockSpec(memory_space=pltpu.VMEM)
    return pl.pallas_call(
        functools.partial(cross_kernel, first, each),
        in_specs=[pl.BlockSpec(memory_space=pltpu.SMEM)] + [in_vmem] * 4,
        out_specs=[in_vmem] * parts,
        out_shape=[jax.ShapeDtypeStruct((each * tile, panel[0].shape[0]), f32)] * parts,
        compiler_params=pltpu.CompilerParams(vmem_limit_bytes=ROOM),
        cost_estimate=BRIEF,
        name="cross",
    )(table, *window, *panel)


def residual_kernel(
    firsts, each, table_ref, window_high, window_low, high_ref, low_ref, *refs
):
    totals, (out_ref, sent, departures) = refs[: len(firsts)], refs[-3:]
    _, tile, columns = sent.shape
    chunk = min(256, columns)

    def leaving(place, entry):
        start = pl.multiple_of(table_ref[entry], tile)
        return pltpu.make_async_copy(
            sent.at[place], out_ref.at[pl.ds(start, tile), :], departures.at[place]
        )

    for part, (first, total) in enumerate(zip(firsts, totals)):

        @pl.loop(0, each)
        def _(step):
            rows = pl.ds(pl.multiple_of(table_ref[first + step], tile), tile)
            left_high, left_low = split(total[pl.ds(pl.multiple_of(step * tile, tile), tile), :])
            dims = ((1,), (0,))
            for start in range(0, columns, chunk):
                here = slice(start, start + chunk)
                product = dot(left_high, high_ref[:, here], dims) + (
                    dot(left_high, low_ref[:, here], dims)
                    + dot(left_low, high_ref[:, here], dims)
                )
                window = window_high[rows, here].astype(f32) + window_low[rows, here].astype(f32)
                sent[part * each + step, :, here] = window - product
            leaving(part * each + step, first + step).start()

    for part, first in enumerate(firsts):

        @pl.loop(0, each)
        def _(step):
            leaving(part * each + step, first + step).wait()


def residual_call(table, firsts, tile, window, weight, totals, before, cost=BRIEF):
    (rows, columns), each = window[0].shape, totals[0].shape[0] // tile
    in_vmem = pl.BlockSpec(memory_space=pltpu.VMEM)
    operands = [table, *window, *weight, *totals]
    in_specs = [pl.BlockSpec(memory_space=pltpu.SMEM)] + [in_vmem] * (len(operands) - 1)
    aliases = {}
    if before is not None:
        aliases = {len(operands): 0}
        operands.append(before)
        in_specs.append(pl.BlockSpec(memory_space=pl.ANY))
    return pl.pallas_call(
        functools.partial(residual_kernel, firsts, each),
        in_specs=in_specs,
        out_specs=pl.BlockSpec(memory_space=pl.ANY),
        scratch_shapes=[
            pltpu.VMEM((len(firsts) * each, tile, columns), f32),
            pltpu.SemaphoreType.DMA((len(firsts) * each,)),
        ],
        out_shape=jax.ShapeDtypeStruct((rows, columns), f32),
        input_output_aliases=aliases,
        compiler_params=pltpu.CompilerParams(vmem_limit_bytes=ROOM),
        cost_estimate=cost,
        name="residual",
    )(*operands)


def eliminate(diagonal):
    size, lanes, tile = BLOCK, 128, 8
    tiles = size // tile
    row_at = [lax.broadcasted_iota(jnp.int32, (tile, lanes), 0) + tile * t for t in range(tiles)]
    lane_at = lax.broadcasted_iota(jnp.int32, (tile, lanes), 1)
    spread = [
        [
            jnp.broadcast_to(diagonal[tile * t : tile * (t + 1), k : k + 1], (tile, lanes))
            for t in range(tiles)
        ]
        for k in range(size)
    ]
    inverse = [jnp.where(row_at[t] == lane_at, 1.0, 0.0) for t in range(tiles)]
    lower = [jnp.zeros((tile, lanes), f32) for _ in range(tiles)]
    scale = [jnp.zeros((tile, lanes), f32) for _ in range(tiles)]
    for j in range(size):
        own, at = j // tile, j % tile
        pivot = spread[j][own][at : at + 1, :]
        reciprocal = 1.0 / pivot
        root = lax.rsqrt(pivot)
        inverse_row = inverse[own][at : at + 1, :]
        factor = {}
        for t in range(own, tiles):
            column = spread[j][t]
            factor[t] = column * reciprocal
            if t == own:
                factor[t] = jnp.where(row_at[t] > j, factor[t], 0.0)
                scale[t] = jnp.where(row_at[t] == j, root, scale[t])
                lower[t] = jnp.where((lane_at == j) & (row_at[t] >= j), column * root, lower[t])
            else:
                lower[t] = jnp.where(lane_at == j, column * root, lower[t])
            inverse[t] = inverse[t] - factor[t] * inverse_row
        for k in range(j + 1, size):
            entry = spread[j][k // tile][k % tile : k % tile + 1, :]
            for t in range(k // tile, tiles):
                spread[k][t] = spread[k][t] - factor[t] * entry
    inverse = [inverse[t] * scale[t] for t in range(tiles)]
    return jnp.concatenate(lower, 0), jnp.concatenate(inverse, 0)


def factor_kernel(begin, end, last, ins, outs):
    state_ref, lower_ref = outs[:2]
    if begin:
        state_ref[...] = ins[0][...]
        lower_ref[...] = ins[1][...]
    else:
        half, side = ins[0].shape[0], ins[2][1]
        state_ref[pl.ds(pl.multiple_of(side * half, half), half), :] = ins[0][...]
        state_ref[pl.ds(pl.multiple_of((1 - side) * half, half), half), :] = ins[1][...]
    size = state_ref.shape[0]
    column_at = lax.broadcasted_iota(jnp.int32, (BLOCK, size), 1)
    row_at = lax.broadcasted_iota(jnp.int32, (BLOCK, size), 0)
    for step in range(begin, end):
        start, stop = step * BLOCK, (step + 1) * BLOCK
        rows = state_ref[start:stop, :]
        lower, inverse = eliminate(rows[:, start:stop])
        lower_ref[start:stop, :] = lower
        inside = (column_at >= start) & (column_at < stop)
        rows = jnp.where(inside, jnp.where(column_at - start == row_at, 1.0, 0.0), rows)
        done = dot(inverse[:, :BLOCK], rows, ((1,), (0,)), precise)
        state_ref[start:stop, :] = done
        if stop < size:
            upper = jnp.where(column_at >= stop, done, 0.0)
            update = dot(upper, done, ((0,), (0,)), precise)[stop:, :]
            below_at = lax.broadcasted_iota(jnp.int32, (size - stop, size), 1)
            below = jnp.where(
                (below_at >= start) & (below_at < stop), 0.0, state_ref[stop:, :]
            )
            state_ref[stop:, :] = below - update
    if last:
        whole_ref = ins[2]
        triangle_ref, inverse_ref, high_ref, low_ref = outs[2:]
        column_at = lax.broadcasted_iota(jnp.int32, (size, size), 1)
        row_at = lax.broadcasted_iota(jnp.int32, (size, size), 0)
        edge = (row_at // BLOCK + 1) * BLOCK
        state = state_ref[...]
        inverse = jnp.where(column_at <= row_at, state, 0.0)
        lower = lower_ref[...]
        wide = jnp.concatenate([lower] * (size // lower.shape[1]), 1)
        for step in range(size // BLOCK):
            start, stop = step * BLOCK, (step + 1) * BLOCK
            shift = start % lower.shape[1]
            part = wide[start:stop, :]
            if shift:
                part = pltpu.roll(part, shift, 1)
            lower_full = jnp.where(
                (column_at[start:stop, :] >= start) & (column_at[start:stop, :] < stop), part, 0.0
            )
            state_ref[start:stop, :] = lower_full
        triangle_ref[...] = jnp.where(column_at >= edge, state, 0.0) + state_ref[...].T
        half = dot(inverse, whole_ref[...], ((1,), (0,)), precise)
        inverse_ref[...] = inverse
        weight = dot(inverse, half, ((0,), (0,)), precise)
        high_ref[...], low_ref[...] = split(weight)


def factor_call(begin, end, operands, place=None, whole=None):
    size = operands[0].shape[1]
    operands = list(operands)
    shapes = [
        jax.ShapeDtypeStruct((size, size), f32),
        jax.ShapeDtypeStruct((size, 128), f32),
    ]
    if whole is not None:
        operands.append(whole)
        shapes += [
            jax.ShapeDtypeStruct((size, size), f32),
            jax.ShapeDtypeStruct((size, size), f32),
            jax.ShapeDtypeStruct((size, whole.shape[1]), bf16),
            jax.ShapeDtypeStruct((size, whole.shape[1]), bf16),
        ]
    in_specs = [pl.BlockSpec(memory_space=pltpu.VMEM)] * len(operands)
    if not begin:
        operands.append(place)
        in_specs.append(pl.BlockSpec(memory_space=pltpu.SMEM))

    def body(*refs):
        factor_kernel(begin, end, whole is not None, refs[: len(operands)], refs[len(operands) :])

    return pl.pallas_call(
        body,
        out_shape=shapes,
        in_specs=in_specs,
        out_specs=[pl.BlockSpec(memory_space=pltpu.VMEM)] * len(shapes),
        compiler_params=pltpu.CompilerParams(vmem_limit_bytes=24 * MIB),
        cost_estimate=BRIEF,
        name="factor",
    )(*operands)


def flip(value, bit, size):
    return lax.ppermute(value, "row", [(i, i ^ bit) for i in range(size)])


def exchange(value, step, bits):
    size = 2 << len(bits)
    return lax.ppermute(
        value, "row", [(i, i ^ (bits[-1 - step] if i & 1 else bits[step])) for i in range(size)]
    )


def relative_owners(bits):
    owners = [0]
    for bit in reversed(bits):
        owners = [owner | bit for owner in owners] + owners
    return owners


def sum_shares(kept, arrived, bits):
    pairs, count = [(kept, 0), (arrived, 0)], kept.shape[0]
    cut = lambda array, at: lax.slice_in_dim(array, at, at + count, axis=0)
    for step in range(len(bits)):
        count //= 2
        out = yield sum(cut(array, at) for array, at in pairs)
        pairs = [(array, at + count) for array, at in pairs] + [(exchange(out, step, bits), 0)]
    yield sum(cut(array, at) for array, at in pairs)


def gather_panel(shard, depth):
    up = [(i, (i - 1) % depth) for i in range(depth)]
    down = [(i, (i + 1) % depth) for i in range(depth)]
    above = [lax.ppermute(shard, "col", up)]
    below = []
    later, _ = lax.optimization_barrier((shard, above[0]))
    for step in range(2, depth):
        if step % 2 == 0:
            above.append(lax.ppermute(above[-1], "col", up))
        else:
            below.append(lax.ppermute(below[-1] if below else later, "col", down))
    return [shard, *above, *below[::-1]]


def spread(part, bits):
    for step in reversed(range(1, len(bits))):
        part = jnp.concatenate([exchange(part, step, bits), part], 0)
    return part


def local(panel_cols, window_cols):
    size = lax.axis_size("row")
    depth = lax.axis_size("col")
    here = lax.axis_index("row").astype(jnp.int32)
    place = jnp.stack([lax.axis_index("col").astype(jnp.int32), here & 1])
    bits = [1 << shift for shift in range(1, size.bit_length() - 1)]
    steps = len(bits)
    share = window_cols.shape[0] // size

    tile = share // 2

    owners = [jnp.asarray(relative_owners(order), jnp.int32) for order in (bits, bits[::-1])]
    table_of = lambda device: share * (device ^ jnp.where(device & 1, owners[1], owners[0]))
    kept, given = table_of(here), table_of(here ^ 1)
    count = kept.shape[0]
    table = jnp.concatenate([kept, kept + tile, given, given + tile])
    entry = lambda side, half: (side * 2 + half) * count

    shards = gather_panel(panel_cols, depth)
    window = hold_call(table, place, window_cols)
    whole, high, low, gram, gram_given = gram_call(place, shards)

    def products(side, half, parts, *others):
        first = after(table, *others)
        return cross_call(first, entry(side, half), parts, count, tile, window, (high, low))

    given = products(1, 0, 2, gram)
    arrived = [flip(part, 1, size) for part in given]
    gram = gram + flip(gram_given, 1, size)
    (kept,) = products(0, 0, 1, gram, given[0])
    early = sum_shares(kept, arrived[0], bits)
    gram = after(gram + exchange(gram, 0, bits), kept)
    early_sum = after(next(early), gram)
    gram = after(gram, early_sum)
    for step in range(1, steps):
        gram = gram + exchange(gram, step, bits)
    (kept,) = products(0, 1, 1, early_sum)
    late = sum_shares(after(kept, gram), arrived[1], bits)
    early_sum = early.send(early_sum)
    late_sum = next(late)

    blocks = whole.shape[0] // BLOCK
    cuts = (0, blocks * 3 // 8, blocks * 6 // 8, blocks)
    halves = [after(gram, early_sum, late_sum), flip(gram, 1, size)]
    state = factor_call(0, cuts[1], halves, place)
    for _ in range(1, steps):
        early_sum = early.send(early_sum)
    late_sum = after(late.send(late_sum), state[0], early_sum)
    state = factor_call(cuts[1], cuts[2], [after(state[0], late_sum), state[1]])
    for _ in range(1, steps):
        late_sum = late.send(late_sum)
    late_sum = after(late_sum, state[0])
    early_near = spread(early_sum, bits)
    _, _, triangle, inverse, *weight = factor_call(
        cuts[2], blocks, [after(state[0], late_sum, early_near), state[1]], None, whole
    )

    late_near = after(spread(late_sum, bits), weight[0])
    early_far, late_far = [exchange(part, 0, bits) for part in (early_near, late_near)]
    nearer = lambda side: [entry(side, half) + count // 2 for half in (0, 1)]
    subtract = lambda firsts, *others: residual_call(table, firsts, tile, window, weight, *others)
    residual = subtract(nearer(0), [early_near, late_near], None, LONG)
    near = [flip(part, 1, size) for part in (early_near, late_near)]
    residual = subtract(nearer(1), near, residual)
    early_far, residual = lax.optimization_barrier((early_far, residual))
    residual = subtract([entry(0, 0)], [early_far], residual)
    late_far, residual = lax.optimization_barrier((late_far, residual))
    parts = [flip(early_far, 1, size), late_far]
    residual = subtract([entry(1, 0), entry(0, 1)], parts, residual)
    residual = subtract([entry(1, 1)], [flip(late_far, 1, size)], residual)
    summed = jnp.concatenate([early_sum, late_sum], 0)
    top_rows = dot(summed, inverse, ((1,), (1,)), precise)
    return triangle, top_rows, residual


def solution(mesh):
    return jax.shard_map(
        local,
        mesh=mesh,
        in_specs=(P("col", "row"), P("col", "row")),
        out_specs=(P(), P(("col", "row"), None), P("col", "row")),
        check_vma=False,
    )
```

```python
import functools

import jax
import jax.numpy as jnp
from jax import lax
from jax.experimental import pallas as pl
from jax.experimental.pallas import tpu as pltpu
from jax.sharding import PartitionSpec as P

precise = lax.Precision.HIGHEST
f32, bf16 = jnp.float32, jnp.bfloat16
BLOCK = 32
MIB = 1 << 20
ROOM = 24 * MIB
LONG = pl.CostEstimate(flops=100_000_000_000, bytes_accessed=1, transcendentals=0)
BRIEF = pl.CostEstimate(flops=1, bytes_accessed=1, transcendentals=0)


def dot(left, right, dims, precision=None):
    return lax.dot_general(
        left, right, (dims, ((), ())), precision=precision, preferred_element_type=f32
    )


def split(value):
    high = value.astype(bf16)
    return high, (value - high.astype(f32)).astype(bf16)


def after(value, *others):
    return lax.optimization_barrier((value, *others))[0]


def gram_kernel(place_ref, *refs):
    shards, (whole_ref, high_ref, low_ref, gram_ref) = refs[:-4], refs[-4:]
    rows = shards[0].shape[0]
    for step, shard in enumerate(shards):
        owner = lax.rem(place_ref[0] + step, len(shards))
        whole_ref[pl.ds(pl.multiple_of(owner * rows, rows), rows), :] = shard[...]
    whole = whole_ref[...]
    gram_ref[...] = dot(whole, whole, ((1,), (1,)), precise)
    high_ref[...], low_ref[...] = split(whole)


def gram_call(place, shards):
    rows, columns = shards[0].shape
    panel = rows * len(shards)
    in_vmem = pl.BlockSpec(memory_space=pltpu.VMEM)
    return pl.pallas_call(
        gram_kernel,
        in_specs=[pl.BlockSpec(memory_space=pltpu.SMEM)] + [in_vmem] * len(shards),
        out_specs=[in_vmem] * 4,
        out_shape=[
            jax.ShapeDtypeStruct((panel, columns), f32),
            jax.ShapeDtypeStruct((panel, columns), bf16),
            jax.ShapeDtypeStruct((panel, columns), bf16),
            jax.ShapeDtypeStruct((panel, panel), f32),
        ],
        compiler_params=pltpu.CompilerParams(vmem_limit_bytes=24 * MIB),
        cost_estimate=LONG,
        name="gram",
    )(place, *shards)


def hold_kernel(table_ref, place_ref, window_ref, high_ref, low_ref, held, arrivals):
    slots, rows, _ = held.shape
    count = window_ref.shape[0] // rows

    def arriving(step):
        start = pl.multiple_of(step * rows, rows)
        slot = lax.rem(step, slots)
        return pltpu.make_async_copy(
            window_ref.at[pl.ds(start, rows), :], held.at[slot], arrivals.at[slot]
        )

    for step in range(min(slots, count)):
        arriving(step).start()

    @pl.loop(0, count)
    def _(step):
        arriving(step).wait()
        high, low = split(held[lax.rem(step, slots)])
        here = pl.ds(pl.multiple_of(step * rows, rows), rows)
        high_ref[here, :] = high
        low_ref[here, :] = low

        @pl.when(step + slots < count)
        def _():
            arriving(step + slots).start()


def hold_call(table, place, window):
    rows, columns = window.shape
    tile = min(256, rows)
    scalars = pl.BlockSpec(memory_space=pltpu.SMEM)
    return pl.pallas_call(
        hold_kernel,
        in_specs=[scalars, scalars, pl.BlockSpec(memory_space=pl.ANY)],
        out_specs=[pl.BlockSpec(memory_space=pltpu.VMEM)] * 2,
        scratch_shapes=[
            pltpu.VMEM((4, tile, columns), f32),
            pltpu.SemaphoreType.DMA((4,)),
        ],
        out_shape=[jax.ShapeDtypeStruct(window.shape, bf16)] * 2,
        compiler_params=pltpu.CompilerParams(vmem_limit_bytes=ROOM),
        cost_estimate=BRIEF,
        name="hold",
    )(table, place, window)


def cross_kernel(first, each, table_ref, window_high, window_low, high_ref, low_ref, *outs):
    tile = outs[0].shape[0] // each
    dims = ((1,), (1,))

    @pl.loop(0, each)
    def _(step):
        rows = pl.ds(pl.multiple_of(table_ref[first + step], tile), len(outs) * tile)
        result = dot(window_high[rows, :], high_ref[...], dims) + (
            dot(window_high[rows, :], low_ref[...], dims)
            + dot(window_low[rows, :], high_ref[...], dims)
        )
        here = pl.ds(pl.multiple_of(step * tile, tile), tile)
        for part, cross_ref in enumerate(outs):
            cross_ref[here, :] = result[part * tile : (part + 1) * tile]


def cross_call(table, first, parts, each, tile, window, panel, cost):
    in_vmem = pl.BlockSpec(memory_space=pltpu.VMEM)
    return pl.pallas_call(
        functools.partial(cross_kernel, first, each),
        in_specs=[pl.BlockSpec(memory_space=pltpu.SMEM)] + [in_vmem] * 4,
        out_specs=[in_vmem] * parts,
        out_shape=[jax.ShapeDtypeStruct((each * tile, panel[0].shape[0]), f32)] * parts,
        compiler_params=pltpu.CompilerParams(vmem_limit_bytes=ROOM),
        cost_estimate=cost,
        name="cross",
    )(table, *window, *panel)


def residual_kernel(firsts, each, table_ref, window_high, window_low, weight_ref, *refs):
    totals, (out_ref, sent, departures) = refs[: len(firsts)], refs[-3:]
    _, tile, columns = sent.shape
    chunk = min(256, columns)

    def leaving(place, entry):
        start = pl.multiple_of(table_ref[entry], tile)
        return pltpu.make_async_copy(
            sent.at[place], out_ref.at[pl.ds(start, tile), :], departures.at[place]
        )

    for part, (first, total) in enumerate(zip(firsts, totals)):

        @pl.loop(0, each)
        def _(step):
            rows = pl.ds(pl.multiple_of(table_ref[first + step], tile), tile)
            high, low = split(total[pl.ds(pl.multiple_of(step * tile, tile), tile), :])
            terms = jnp.concatenate([high, high, low], 1)
            for start in range(0, columns, chunk):
                here = slice(start, start + chunk)
                product = dot(terms, weight_ref[:, here], ((1,), (0,)))
                window = window_high[rows, here].astype(f32) + window_low[rows, here].astype(f32)
                sent[part * each + step, :, here] = window - product
            leaving(part * each + step, first + step).start()

    for part, first in enumerate(firsts):

        @pl.loop(0, each)
        def _(step):
            leaving(part * each + step, first + step).wait()


def residual_call(table, firsts, tile, window, weight, totals, before, cost=BRIEF):
    (rows, columns), each = window[0].shape, totals[0].shape[0] // tile
    in_vmem = pl.BlockSpec(memory_space=pltpu.VMEM)
    operands = [table, *window, weight, *totals]
    in_specs = [pl.BlockSpec(memory_space=pltpu.SMEM)] + [in_vmem] * (len(operands) - 1)
    aliases = {}
    if before is not None:
        aliases = {len(operands): 0}
        operands.append(before)
        in_specs.append(pl.BlockSpec(memory_space=pl.ANY))
    return pl.pallas_call(
        functools.partial(residual_kernel, firsts, each),
        in_specs=in_specs,
        out_specs=pl.BlockSpec(memory_space=pl.ANY),
        scratch_shapes=[
            pltpu.VMEM((len(firsts) * each, tile, columns), f32),
            pltpu.SemaphoreType.DMA((len(firsts) * each,)),
        ],
        out_shape=jax.ShapeDtypeStruct((rows, columns), f32),
        input_output_aliases=aliases,
        compiler_params=pltpu.CompilerParams(vmem_limit_bytes=ROOM),
        cost_estimate=cost,
        name="residual",
    )(*operands)


def eliminate(diagonal):
    size, lanes, tile = BLOCK, 128, 8
    tiles = size // tile
    row_at = [lax.broadcasted_iota(jnp.int32, (tile, lanes), 0) + tile * t for t in range(tiles)]
    lane_at = lax.broadcasted_iota(jnp.int32, (tile, lanes), 1)
    spread = [
        [
            jnp.broadcast_to(diagonal[tile * t : tile * (t + 1), k : k + 1], (tile, lanes))
            for t in range(tiles)
        ]
        for k in range(size)
    ]
    inverse = [jnp.where(row_at[t] == lane_at, 1.0, 0.0) for t in range(tiles)]
    lower = [jnp.zeros((tile, lanes), f32) for _ in range(tiles)]
    scale = [jnp.zeros((tile, lanes), f32) for _ in range(tiles)]
    for j in range(size):
        own, at = j // tile, j % tile
        pivot = spread[j][own][at : at + 1, :]
        reciprocal = 1.0 / pivot
        root = lax.rsqrt(pivot)
        inverse_row = inverse[own][at : at + 1, :]
        factor = {}
        for t in range(own, tiles):
            column = spread[j][t]
            factor[t] = column * reciprocal
            if t == own:
                factor[t] = jnp.where(row_at[t] > j, factor[t], 0.0)
                scale[t] = jnp.where(row_at[t] == j, root, scale[t])
                lower[t] = jnp.where((lane_at == j) & (row_at[t] >= j), column * root, lower[t])
            else:
                lower[t] = jnp.where(lane_at == j, column * root, lower[t])
            inverse[t] = inverse[t] - factor[t] * inverse_row
        for k in range(j + 1, size):
            entry = spread[j][k // tile][k % tile : k % tile + 1, :]
            for t in range(k // tile, tiles):
                spread[k][t] = spread[k][t] - factor[t] * entry
    inverse = [inverse[t] * scale[t] for t in range(tiles)]
    return jnp.concatenate(lower, 0), jnp.concatenate(inverse, 0)


def factor_kernel(begin, end, last, ins, outs):
    state_ref, lower_ref = outs[:2]
    state_ref[...] = ins[0][...]
    if begin:
        lower_ref[...] = ins[1][...]
    size = state_ref.shape[0]
    column_at = lax.broadcasted_iota(jnp.int32, (BLOCK, size), 1)
    row_at = lax.broadcasted_iota(jnp.int32, (BLOCK, size), 0)
    for step in range(begin, end):
        start, stop = step * BLOCK, (step + 1) * BLOCK
        rows = state_ref[start:stop, :]
        lower, inverse = eliminate(rows[:, start:stop])
        lower_ref[start:stop, :] = lower
        inside = (column_at >= start) & (column_at < stop)
        rows = jnp.where(inside, jnp.where(column_at - start == row_at, 1.0, 0.0), rows)
        done = dot(inverse[:, :BLOCK], rows, ((1,), (0,)), precise)
        state_ref[start:stop, :] = done
        if stop < size:
            upper = jnp.where(column_at >= stop, done, 0.0)
            update = dot(upper, done, ((0,), (0,)), precise)[stop:, :]
            below_at = lax.broadcasted_iota(jnp.int32, (size - stop, size), 1)
            below = jnp.where(
                (below_at >= start) & (below_at < stop), 0.0, state_ref[stop:, :]
            )
            state_ref[stop:, :] = below - update
    if last:
        whole_ref = ins[2]
        triangle_ref, inverse_ref, weight_ref = outs[2:]
        column_at = lax.broadcasted_iota(jnp.int32, (size, size), 1)
        row_at = lax.broadcasted_iota(jnp.int32, (size, size), 0)
        edge = (row_at // BLOCK + 1) * BLOCK
        state = state_ref[...]
        inverse = jnp.where(column_at <= row_at, state, 0.0)
        lower = lower_ref[...]
        wide = jnp.concatenate([lower] * (size // lower.shape[1]), 1)
        for step in range(size // BLOCK):
            start, stop = step * BLOCK, (step + 1) * BLOCK
            shift = start % lower.shape[1]
            part = wide[start:stop, :]
            if shift:
                part = pltpu.roll(part, shift, 1)
            lower_full = jnp.where(
                (column_at[start:stop, :] >= start) & (column_at[start:stop, :] < stop), part, 0.0
            )
            state_ref[start:stop, :] = lower_full
        triangle_ref[...] = jnp.where(column_at >= edge, state, 0.0) + state_ref[...].T
        half = dot(inverse, whole_ref[...], ((1,), (0,)), precise)
        inverse_ref[...] = inverse
        weight = dot(inverse, half, ((0,), (0,)), precise)
        high, low = split(weight)
        for term, part in enumerate((high, low, high)):
            weight_ref[term * size : (term + 1) * size, :] = part


def factor_call(begin, end, operands, whole=None):
    size = operands[0].shape[1]
    operands = list(operands)
    shapes = [
        jax.ShapeDtypeStruct((size, size), f32),
        jax.ShapeDtypeStruct((size, 128), f32),
    ]
    if whole is not None:
        operands.append(whole)
        shapes += [
            jax.ShapeDtypeStruct((size, size), f32),
            jax.ShapeDtypeStruct((size, size), f32),
            jax.ShapeDtypeStruct((3 * size, whole.shape[1]), bf16),
        ]
    in_specs = [pl.BlockSpec(memory_space=pltpu.VMEM)] * len(operands)

    def body(*refs):
        factor_kernel(begin, end, whole is not None, refs[: len(operands)], refs[len(operands) :])

    return pl.pallas_call(
        body,
        out_shape=shapes,
        in_specs=in_specs,
        out_specs=[pl.BlockSpec(memory_space=pltpu.VMEM)] * len(shapes),
        compiler_params=pltpu.CompilerParams(vmem_limit_bytes=24 * MIB),
        cost_estimate=BRIEF,
        name="factor",
    )(*operands)


def flip(value, bit, size):
    return lax.ppermute(value, "row", [(i, i ^ bit) for i in range(size)])


def exchange(value, step, bits):
    size = 2 << len(bits)
    return lax.ppermute(
        value, "row", [(i, i ^ (bits[-1 - step] if i & 1 else bits[step])) for i in range(size)]
    )


def relative_owners(bits):
    owners = [0]
    for bit in reversed(bits):
        owners = [owner | bit for owner in owners] + owners
    return owners


def sum_shares(kept, arrived, bits):
    pairs, count = [(kept, 0), (arrived, 0)], kept.shape[0]
    cut = lambda array, at: lax.slice_in_dim(array, at, at + count, axis=0)
    for step in range(len(bits)):
        count //= 2
        out = yield sum(cut(array, at) for array, at in pairs)
        pairs = [(array, at + count) for array, at in pairs] + [(exchange(out, step, bits), 0)]
    yield sum(cut(array, at) for array, at in pairs)


def gather_panel(shard, depth):
    up = [(i, (i - 1) % depth) for i in range(depth)]
    down = [(i, (i + 1) % depth) for i in range(depth)]
    above = [lax.ppermute(shard, "col", up)]
    below = []
    later, _ = lax.optimization_barrier((shard, above[0]))
    for step in range(2, depth):
        if step % 2 == 0:
            above.append(lax.ppermute(above[-1], "col", up))
        else:
            below.append(lax.ppermute(below[-1] if below else later, "col", down))
    return [shard, *above, *below[::-1]]


def spread(part, bits, *others):
    for step in reversed(range(1, len(bits))):
        part = jnp.concatenate([after(exchange(part, step, bits), *others), part], 0)
    return part


def local(panel_cols, window_cols):
    size = lax.axis_size("row")
    depth = lax.axis_size("col")
    here = lax.axis_index("row").astype(jnp.int32)
    place = lax.axis_index("col").astype(jnp.int32).reshape(1)
    bits = [1 << shift for shift in range(1, size.bit_length() - 1)]
    steps = len(bits)
    share = window_cols.shape[0] // size

    tile = share // 2

    owners = [jnp.asarray(relative_owners(order), jnp.int32) for order in (bits, bits[::-1])]
    table_of = lambda device: share * (device ^ jnp.where(device & 1, owners[1], owners[0]))
    kept, given = table_of(here), table_of(here ^ 1)
    count = kept.shape[0]
    table = jnp.concatenate([kept, kept + tile, given, given + tile])
    entry = lambda side, half: (side * 2 + half) * count

    shards = gather_panel(panel_cols, depth)
    window = hold_call(table, place, window_cols)
    whole, high, low, gram = gram_call(after(place, window[0]), shards)

    def products(side, half, parts, cost, *others):
        first = after(table, *others)
        return cross_call(first, entry(side, half), parts, count, tile, window, (high, low), cost)

    given = products(1, 0, 2, BRIEF, gram)
    arrived = [flip(part, 1, size) for part in given]
    gram = gram + exchange(gram, 0, bits)
    (kept,) = products(0, 0, 1, LONG, gram, given[0])
    early = sum_shares(kept, arrived[0], bits)
    early_sum = after(next(early), gram)
    for step in range(1, steps):
        gram = gram + exchange(gram, step, bits)
    (kept,) = products(0, 1, 1, BRIEF, early_sum)
    late = sum_shares(after(kept, gram), arrived[1], bits)
    late_sum = next(late)
    gram = gram + flip(gram, 1, size)

    blocks = whole.shape[0] // BLOCK
    cuts = (0, blocks * 3 // 8, blocks * 6 // 8, blocks)
    state = factor_call(0, cuts[1], [after(gram, late_sum)])
    early_sum = after(early.send(early_sum), state[0])
    state = factor_call(cuts[1], cuts[2], [after(state[0], early_sum), state[1]])
    for _ in range(1, steps):
        early_sum = early.send(early_sum)
    late_sum = after(late.send(late_sum), state[0], early_sum)
    _, _, triangle, inverse, weight = factor_call(
        cuts[2], blocks, [after(state[0], late_sum), state[1]], whole
    )
    for _ in range(1, steps):
        late_sum = late.send(late_sum)
    late_sum = after(late_sum, weight)

    early_near = after(spread(early_sum, bits), weight)
    early_far = exchange(early_near, 0, bits)
    nearer = lambda side, half: entry(side, half) + count // 2
    subtract = lambda firsts, *others: residual_call(table, firsts, tile, window, weight, *others)
    parts = [early_near, flip(early_near, 1, size)]
    residual = subtract([nearer(0, 0), nearer(1, 0)], parts, None)
    late_near = spread(late_sum, bits, residual)
    late_far = exchange(late_near, 0, bits)
    late_back = flip(late_near, 1, size)
    residual = subtract([nearer(0, 1)], [late_near], residual, LONG)
    early_far, residual = lax.optimization_barrier((early_far, residual))
    parts = [late_back, early_far, flip(early_far, 1, size), late_far, flip(late_far, 1, size)]
    firsts = [nearer(1, 1), entry(0, 0), entry(1, 0), entry(0, 1), entry(1, 1)]
    residual = subtract(firsts, parts, residual)
    summed = jnp.concatenate([early_sum, late_sum], 0)
    top_rows = dot(summed, inverse, ((1,), (1,)), precise)
    return triangle, top_rows, residual


def solution(mesh):
    return jax.shard_map(
        local,
        mesh=mesh,
        in_specs=(P("col", "row"), P("col", "row")),
        out_specs=(P(), P(("col", "row"), None), P("col", "row")),
        check_vma=False,
    )
```

```python
import functools

import jax
import jax.numpy as jnp
from jax import lax
from jax.experimental import pallas as pl
from jax.experimental.pallas import tpu as pltpu
from jax.sharding import PartitionSpec as P

precise = lax.Precision.HIGHEST
f32, bf16 = jnp.float32, jnp.bfloat16
BLOCK = 32
MIB = 1 << 20
ROOM = 24 * MIB
LONG = pl.CostEstimate(flops=100_000_000_000, bytes_accessed=1, transcendentals=0)
BRIEF = pl.CostEstimate(flops=1, bytes_accessed=1, transcendentals=0)


def dot(left, right, dims, precision=None):
    return lax.dot_general(
        left, right, (dims, ((), ())), precision=precision, preferred_element_type=f32
    )


def split(value):
    high = value.astype(bf16)
    return high, (value - high.astype(f32)).astype(bf16)


def after(value, *others):
    return lax.optimization_barrier((value, *others))[0]


def gram_kernel(place_ref, *refs):
    shards, (whole_ref, high_ref, low_ref, gram_ref) = refs[:-4], refs[-4:]
    rows = shards[0].shape[0]
    for step, shard in enumerate(shards):
        owner = lax.rem(place_ref[0] + step, len(shards))
        whole_ref[pl.ds(pl.multiple_of(owner * rows, rows), rows), :] = shard[...]
    whole = whole_ref[...]
    gram_ref[...] = dot(whole, whole, ((1,), (1,)), precise)
    high_ref[...], low_ref[...] = split(whole)


def gram_call(place, shards):
    rows, columns = shards[0].shape
    panel = rows * len(shards)
    in_vmem = pl.BlockSpec(memory_space=pltpu.VMEM)
    return pl.pallas_call(
        gram_kernel,
        in_specs=[pl.BlockSpec(memory_space=pltpu.SMEM)] + [in_vmem] * len(shards),
        out_specs=[in_vmem] * 4,
        out_shape=[
            jax.ShapeDtypeStruct((panel, columns), f32),
            jax.ShapeDtypeStruct((panel, columns), bf16),
            jax.ShapeDtypeStruct((panel, columns), bf16),
            jax.ShapeDtypeStruct((panel, panel), f32),
        ],
        compiler_params=pltpu.CompilerParams(vmem_limit_bytes=24 * MIB),
        cost_estimate=LONG,
        name="gram",
    )(place, *shards)


def hold_kernel(table_ref, place_ref, window_ref, high_ref, low_ref, held, arrivals):
    slots, rows, _ = held.shape
    count = window_ref.shape[0] // rows

    def arriving(step):
        start = pl.multiple_of(step * rows, rows)
        slot = lax.rem(step, slots)
        return pltpu.make_async_copy(
            window_ref.at[pl.ds(start, rows), :], held.at[slot], arrivals.at[slot]
        )

    for step in range(min(slots, count)):
        arriving(step).start()

    @pl.loop(0, count)
    def _(step):
        arriving(step).wait()
        high, low = split(held[lax.rem(step, slots)])
        here = pl.ds(pl.multiple_of(step * rows, rows), rows)
        high_ref[here, :] = high
        low_ref[here, :] = low

        @pl.when(step + slots < count)
        def _():
            arriving(step + slots).start()


def hold_call(table, place, window):
    rows, columns = window.shape
    tile = min(256, rows)
    scalars = pl.BlockSpec(memory_space=pltpu.SMEM)
    return pl.pallas_call(
        hold_kernel,
        in_specs=[scalars, scalars, pl.BlockSpec(memory_space=pl.ANY)],
        out_specs=[pl.BlockSpec(memory_space=pltpu.VMEM)] * 2,
        scratch_shapes=[
            pltpu.VMEM((4, tile, columns), f32),
            pltpu.SemaphoreType.DMA((4,)),
        ],
        out_shape=[jax.ShapeDtypeStruct(window.shape, bf16)] * 2,
        compiler_params=pltpu.CompilerParams(vmem_limit_bytes=ROOM),
        cost_estimate=BRIEF,
        name="hold",
    )(table, place, window)


def cross_kernel(first, each, table_ref, window_high, window_low, high_ref, low_ref, *outs):
    tile = outs[0].shape[0] // each
    dims = ((1,), (1,))
    pair = 3 - len(outs) if each % 2 == 0 else 1

    @pl.loop(0, each // pair)
    def _(step):
        entries = [first + step * pair + place for place in range(pair)]
        rows = [pl.ds(pl.multiple_of(table_ref[at], tile), len(outs) * tile) for at in entries]
        window = [
            jnp.concatenate([term[at, :] for at in rows], 0) for term in (window_high, window_low)
        ]
        result = dot(window[0], high_ref[...], dims) + (
            dot(window[0], low_ref[...], dims) + dot(window[1], high_ref[...], dims)
        )
        here = pl.ds(pl.multiple_of(step * pair * tile, tile), pair * tile)
        for part, cross_ref in enumerate(outs):
            cross_ref[here, :] = result[part * pair * tile : (part + 1) * pair * tile]


def cross_call(table, first, parts, each, tile, window, panel, cost):
    in_vmem = pl.BlockSpec(memory_space=pltpu.VMEM)
    return pl.pallas_call(
        functools.partial(cross_kernel, first, each),
        in_specs=[pl.BlockSpec(memory_space=pltpu.SMEM)] + [in_vmem] * 4,
        out_specs=[in_vmem] * parts,
        out_shape=[jax.ShapeDtypeStruct((each * tile, panel[0].shape[0]), f32)] * parts,
        compiler_params=pltpu.CompilerParams(vmem_limit_bytes=ROOM),
        cost_estimate=cost,
        name="cross",
    )(table, *window, *panel)


def residual_kernel(firsts, each, table_ref, window_high, window_low, weight_ref, *refs):
    totals, (out_ref, sent, departures) = refs[: len(firsts)], refs[-3:]
    _, tile, columns = sent.shape
    chunk = min(256, columns)

    def leaving(place, entry):
        start = pl.multiple_of(table_ref[entry], tile)
        return pltpu.make_async_copy(
            sent.at[place], out_ref.at[pl.ds(start, tile), :], departures.at[place]
        )

    for part, (first, total) in enumerate(zip(firsts, totals)):
        high, low = split(total[...])
        terms = jnp.concatenate([high, high, low], 1)
        rows = [pl.ds(pl.multiple_of(table_ref[first + at], tile), tile) for at in range(each)]
        for start in range(0, columns, chunk):
            here = slice(start, start + chunk)
            product = dot(terms, weight_ref[:, here], ((1,), (0,)))
            for at in range(each):
                window = window_high[rows[at], here].astype(f32)
                window = window + window_low[rows[at], here].astype(f32)
                sent[part * each + at, :, here] = window - product[at * tile : (at + 1) * tile]
        for at in range(each):
            leaving(part * each + at, first + at).start()

    for part, first in enumerate(firsts):

        @pl.loop(0, each)
        def _(step):
            leaving(part * each + step, first + step).wait()


def residual_call(table, firsts, tile, window, weight, totals, before, cost=BRIEF):
    (rows, columns), each = window[0].shape, totals[0].shape[0] // tile
    in_vmem = pl.BlockSpec(memory_space=pltpu.VMEM)
    operands = [table, *window, weight, *totals]
    in_specs = [pl.BlockSpec(memory_space=pltpu.SMEM)] + [in_vmem] * (len(operands) - 1)
    aliases = {}
    if before is not None:
        aliases = {len(operands): 0}
        operands.append(before)
        in_specs.append(pl.BlockSpec(memory_space=pl.ANY))
    return pl.pallas_call(
        functools.partial(residual_kernel, firsts, each),
        in_specs=in_specs,
        out_specs=pl.BlockSpec(memory_space=pl.ANY),
        scratch_shapes=[
            pltpu.VMEM((len(firsts) * each, tile, columns), f32),
            pltpu.SemaphoreType.DMA((len(firsts) * each,)),
        ],
        out_shape=jax.ShapeDtypeStruct((rows, columns), f32),
        input_output_aliases=aliases,
        compiler_params=pltpu.CompilerParams(vmem_limit_bytes=ROOM),
        cost_estimate=cost,
        name="residual",
    )(*operands)


def eliminate(diagonal):
    size, lanes, tile = BLOCK, 128, 8
    tiles = size // tile
    row_at = [lax.broadcasted_iota(jnp.int32, (tile, lanes), 0) + tile * t for t in range(tiles)]
    lane_at = lax.broadcasted_iota(jnp.int32, (tile, lanes), 1)
    spread = [
        [
            jnp.broadcast_to(diagonal[tile * t : tile * (t + 1), k : k + 1], (tile, lanes))
            for t in range(tiles)
        ]
        for k in range(size)
    ]
    inverse = [jnp.where(row_at[t] == lane_at, 1.0, 0.0) for t in range(tiles)]
    lower = [jnp.zeros((tile, lanes), f32) for _ in range(tiles)]
    scale = [jnp.zeros((tile, lanes), f32) for _ in range(tiles)]
    for j in range(size):
        own, at = j // tile, j % tile
        pivot = spread[j][own][at : at + 1, :]
        reciprocal = 1.0 / pivot
        root = lax.rsqrt(pivot)
        inverse_row = inverse[own][at : at + 1, :]
        factor = {}
        for t in range(own, tiles):
            column = spread[j][t]
            factor[t] = column * reciprocal
            if t == own:
                factor[t] = jnp.where(row_at[t] > j, factor[t], 0.0)
                scale[t] = jnp.where(row_at[t] == j, root, scale[t])
                lower[t] = jnp.where((lane_at == j) & (row_at[t] >= j), column * root, lower[t])
            else:
                lower[t] = jnp.where(lane_at == j, column * root, lower[t])
            inverse[t] = inverse[t] - factor[t] * inverse_row
        for k in range(j + 1, size):
            entry = spread[j][k // tile][k % tile : k % tile + 1, :]
            for t in range(k // tile, tiles):
                spread[k][t] = spread[k][t] - factor[t] * entry
    inverse = [inverse[t] * scale[t] for t in range(tiles)]
    return jnp.concatenate(lower, 0), jnp.concatenate(inverse, 0)


def factor_kernel(begin, end, last, ins, outs):
    state_ref, lower_ref = outs[:2]
    state_ref[...] = ins[0][...]
    if begin:
        lower_ref[...] = ins[1][...]
    size = state_ref.shape[0]
    column_at = lax.broadcasted_iota(jnp.int32, (BLOCK, size), 1)
    row_at = lax.broadcasted_iota(jnp.int32, (BLOCK, size), 0)
    for step in range(begin, end):
        start, stop = step * BLOCK, (step + 1) * BLOCK
        rows = state_ref[start:stop, :]
        lower, inverse = eliminate(rows[:, start:stop])
        lower_ref[start:stop, :] = lower
        inside = (column_at >= start) & (column_at < stop)
        rows = jnp.where(inside, jnp.where(column_at - start == row_at, 1.0, 0.0), rows)
        done = dot(inverse[:, :BLOCK], rows, ((1,), (0,)), precise)
        state_ref[start:stop, :] = done
        if stop < size:
            upper = jnp.where(column_at >= stop, done, 0.0)
            update = dot(upper, done, ((0,), (0,)), precise)[stop:, :]
            below_at = lax.broadcasted_iota(jnp.int32, (size - stop, size), 1)
            below = jnp.where(
                (below_at >= start) & (below_at < stop), 0.0, state_ref[stop:, :]
            )
            state_ref[stop:, :] = below - update
    if last:
        whole_ref = ins[2]
        triangle_ref, inverse_ref, weight_ref = outs[2:]
        column_at = lax.broadcasted_iota(jnp.int32, (size, size), 1)
        row_at = lax.broadcasted_iota(jnp.int32, (size, size), 0)
        edge = (row_at // BLOCK + 1) * BLOCK
        state = state_ref[...]
        inverse = jnp.where(column_at <= row_at, state, 0.0)
        lower = lower_ref[...]
        wide = jnp.concatenate([lower] * (size // lower.shape[1]), 1)
        for step in range(size // BLOCK):
            start, stop = step * BLOCK, (step + 1) * BLOCK
            shift = start % lower.shape[1]
            part = wide[start:stop, :]
            if shift:
                part = pltpu.roll(part, shift, 1)
            lower_full = jnp.where(
                (column_at[start:stop, :] >= start) & (column_at[start:stop, :] < stop), part, 0.0
            )
            state_ref[start:stop, :] = lower_full
        triangle_ref[...] = jnp.where(column_at >= edge, state, 0.0) + state_ref[...].T
        half = dot(inverse, whole_ref[...], ((1,), (0,)), precise)
        inverse_ref[...] = inverse
        weight = dot(inverse, half, ((0,), (0,)), precise)
        high, low = split(weight)
        for term, part in enumerate((high, low, high)):
            weight_ref[term * size : (term + 1) * size, :] = part


def factor_call(begin, end, operands, whole=None):
    size = operands[0].shape[1]
    operands = list(operands)
    shapes = [
        jax.ShapeDtypeStruct((size, size), f32),
        jax.ShapeDtypeStruct((size, 128), f32),
    ]
    if whole is not None:
        operands.append(whole)
        shapes += [
            jax.ShapeDtypeStruct((size, size), f32),
            jax.ShapeDtypeStruct((size, size), f32),
            jax.ShapeDtypeStruct((3 * size, whole.shape[1]), bf16),
        ]
    in_specs = [pl.BlockSpec(memory_space=pltpu.VMEM)] * len(operands)

    def body(*refs):
        factor_kernel(begin, end, whole is not None, refs[: len(operands)], refs[len(operands) :])

    return pl.pallas_call(
        body,
        out_shape=shapes,
        in_specs=in_specs,
        out_specs=[pl.BlockSpec(memory_space=pltpu.VMEM)] * len(shapes),
        compiler_params=pltpu.CompilerParams(vmem_limit_bytes=24 * MIB),
        cost_estimate=BRIEF,
        name="factor",
    )(*operands)


def flip(value, bit, size):
    return lax.ppermute(value, "row", [(i, i ^ bit) for i in range(size)])


def exchange(value, step, bits):
    size = 2 << len(bits)
    return lax.ppermute(
        value, "row", [(i, i ^ (bits[-1 - step] if i & 1 else bits[step])) for i in range(size)]
    )


def relative_owners(bits):
    owners = [0]
    for bit in reversed(bits):
        owners = [owner | bit for owner in owners] + owners
    return owners


def sum_shares(kept, arrived, bits):
    pairs, count = [(kept, 0), (arrived, 0)], kept.shape[0]
    cut = lambda array, at: lax.slice_in_dim(array, at, at + count, axis=0)
    for step in range(len(bits)):
        count //= 2
        out = yield sum(cut(array, at) for array, at in pairs)
        pairs = [(array, at + count) for array, at in pairs] + [(exchange(out, step, bits), 0)]
    yield sum(cut(array, at) for array, at in pairs)


def gather_panel(shard, depth):
    up = [(i, (i - 1) % depth) for i in range(depth)]
    down = [(i, (i + 1) % depth) for i in range(depth)]
    above = [lax.ppermute(shard, "col", up)]
    below = []
    later, _ = lax.optimization_barrier((shard, above[0]))
    for step in range(2, depth):
        if step % 2 == 0:
            above.append(lax.ppermute(above[-1], "col", up))
        else:
            below.append(lax.ppermute(below[-1] if below else later, "col", down))
    return [shard, *above, *below[::-1]]


def spread(part, bits, *others):
    for step in reversed(range(1, len(bits))):
        part = jnp.concatenate([after(exchange(part, step, bits), *others), part], 0)
    return part


def local(panel_cols, window_cols):
    size = lax.axis_size("row")
    depth = lax.axis_size("col")
    here = lax.axis_index("row").astype(jnp.int32)
    place = lax.axis_index("col").astype(jnp.int32).reshape(1)
    bits = [1 << shift for shift in range(1, size.bit_length() - 1)]
    steps = len(bits)
    share = window_cols.shape[0] // size

    tile = share // 2

    owners = [jnp.asarray(relative_owners(order), jnp.int32) for order in (bits, bits[::-1])]
    table_of = lambda device: share * (device ^ jnp.where(device & 1, owners[1], owners[0]))
    kept, given = table_of(here), table_of(here ^ 1)
    count = kept.shape[0]
    table = jnp.concatenate([kept, kept + tile, given, given + tile])
    entry = lambda side, half: (side * 2 + half) * count

    shards = gather_panel(panel_cols, depth)
    window = hold_call(table, place, window_cols)
    whole, high, low, gram = gram_call(after(place, window[0]), shards)

    def products(side, half, parts, cost, *others):
        first = after(table, *others)
        return cross_call(first, entry(side, half), parts, count, tile, window, (high, low), cost)

    given = products(1, 0, 2, BRIEF, gram)
    arrived = [flip(part, 1, size) for part in given]
    gram = gram + exchange(gram, 0, bits)
    (kept,) = products(0, 0, 1, LONG, gram, given[0])
    early = sum_shares(kept, arrived[0], bits)
    early_sum = after(next(early), gram)
    for step in range(1, steps):
        gram = gram + after(exchange(gram, step, bits), early_sum)
    (kept,) = products(0, 1, 1, BRIEF, early_sum)
    late = sum_shares(after(kept, gram), arrived[1], bits)
    late_sum = next(late)
    gram = gram + flip(gram, 1, size)

    blocks = whole.shape[0] // BLOCK
    cuts = (0, blocks * 3 // 8, blocks * 6 // 8, blocks)
    state = factor_call(0, cuts[1], [after(gram, late_sum)])
    early_sum = after(early.send(early_sum), state[0])
    state = factor_call(cuts[1], cuts[2], [after(state[0], early_sum), state[1]])
    for _ in range(1, steps):
        early_sum = early.send(early_sum)
    late_sum = after(late.send(late_sum), state[0], early_sum)
    _, _, triangle, inverse, weight = factor_call(
        cuts[2], blocks, [after(state[0], late_sum), state[1]], whole
    )
    for _ in range(1, steps):
        late_sum = late.send(late_sum)
    late_sum = after(late_sum, weight)

    early_near = after(spread(early_sum, bits), weight)
    early_far = exchange(early_near, 0, bits)
    nearer = lambda side, half: entry(side, half) + count // 2
    subtract = lambda firsts, *others: residual_call(table, firsts, tile, window, weight, *others)
    parts = [early_near, flip(early_near, 1, size)]
    residual = subtract([nearer(0, 0), nearer(1, 0)], parts, None)
    late_near = spread(late_sum, bits, residual)
    late_far = exchange(late_near, 0, bits)
    late_back = flip(late_near, 1, size)
    residual = subtract([nearer(0, 1)], [late_near], residual, LONG)
    parts = [late_back, early_far, flip(early_far, 1, size)]
    residual = subtract([nearer(1, 1), entry(0, 0), entry(1, 0)], parts, residual)
    late_far, residual = lax.optimization_barrier((late_far, residual))
    parts = [late_far, flip(late_far, 1, size)]
    residual = subtract([entry(0, 1), entry(1, 1)], parts, residual)
    summed = jnp.concatenate([after(early_sum, late_far), late_sum], 0)
    top_rows = dot(summed, inverse, ((1,), (1,)), precise)
    return triangle, top_rows, residual


def solution(mesh):
    return jax.shard_map(
        local,
        mesh=mesh,
        in_specs=(P("col", "row"), P("col", "row")),
        out_specs=(P(), P(("col", "row"), None), P("col", "row")),
        check_vma=False,
    )
```

```python
import functools

import jax
import jax.numpy as jnp
from jax import lax
from jax.experimental import pallas as pl
from jax.experimental.pallas import tpu as pltpu
from jax.sharding import PartitionSpec as P

precise = lax.Precision.HIGHEST
f32, bf16 = jnp.float32, jnp.bfloat16
BLOCK = 32
MIB = 1 << 20
ROOM = 24 * MIB
LONG = pl.CostEstimate(flops=100_000_000_000, bytes_accessed=1, transcendentals=0)
BRIEF = pl.CostEstimate(flops=1, bytes_accessed=1, transcendentals=0)


def dot(left, right, dims, precision=None):
    return lax.dot_general(
        left, right, (dims, ((), ())), precision=precision, preferred_element_type=f32
    )


def split(value):
    high = value.astype(bf16)
    return high, (value - high.astype(f32)).astype(bf16)


def after(value, *others):
    return lax.optimization_barrier((value, *others))[0]


def gram_kernel(place_ref, *refs):
    shards, (whole_ref, high_ref, low_ref, gram_ref) = refs[:-4], refs[-4:]
    rows = shards[0].shape[0]
    for step, shard in enumerate(shards):
        owner = lax.rem(place_ref[0] + step, len(shards))
        whole_ref[pl.ds(pl.multiple_of(owner * rows, rows), rows), :] = shard[...]
    whole = whole_ref[...]
    gram_ref[...] = dot(whole, whole, ((1,), (1,)), precise)
    high_ref[...], low_ref[...] = split(whole)


def gram_call(place, shards):
    rows, columns = shards[0].shape
    panel = rows * len(shards)
    in_vmem = pl.BlockSpec(memory_space=pltpu.VMEM)
    return pl.pallas_call(
        gram_kernel,
        in_specs=[pl.BlockSpec(memory_space=pltpu.SMEM)] + [in_vmem] * len(shards),
        out_specs=[in_vmem] * 4,
        out_shape=[
            jax.ShapeDtypeStruct((panel, columns), f32),
            jax.ShapeDtypeStruct((panel, columns), bf16),
            jax.ShapeDtypeStruct((panel, columns), bf16),
            jax.ShapeDtypeStruct((panel, panel), f32),
        ],
        compiler_params=pltpu.CompilerParams(vmem_limit_bytes=24 * MIB),
        cost_estimate=LONG,
        name="gram",
    )(place, *shards)


def hold_kernel(table_ref, place_ref, window_ref, high_ref, low_ref, held, arrivals):
    slots, rows, _ = held.shape
    count = window_ref.shape[0] // rows

    def arriving(step):
        start = pl.multiple_of(step * rows, rows)
        slot = lax.rem(step, slots)
        return pltpu.make_async_copy(
            window_ref.at[pl.ds(start, rows), :], held.at[slot], arrivals.at[slot]
        )

    for step in range(min(slots, count)):
        arriving(step).start()

    @pl.loop(0, count)
    def _(step):
        arriving(step).wait()
        high, low = split(held[lax.rem(step, slots)])
        here = pl.ds(pl.multiple_of(step * rows, rows), rows)
        high_ref[here, :] = high
        low_ref[here, :] = low

        @pl.when(step + slots < count)
        def _():
            arriving(step + slots).start()


def hold_call(table, place, window):
    rows, columns = window.shape
    tile = min(256, rows)
    scalars = pl.BlockSpec(memory_space=pltpu.SMEM)
    return pl.pallas_call(
        hold_kernel,
        in_specs=[scalars, scalars, pl.BlockSpec(memory_space=pl.ANY)],
        out_specs=[pl.BlockSpec(memory_space=pltpu.VMEM)] * 2,
        scratch_shapes=[
            pltpu.VMEM((4, tile, columns), f32),
            pltpu.SemaphoreType.DMA((4,)),
        ],
        out_shape=[jax.ShapeDtypeStruct(window.shape, bf16)] * 2,
        compiler_params=pltpu.CompilerParams(vmem_limit_bytes=ROOM),
        cost_estimate=BRIEF,
        name="hold",
    )(table, place, window)


def cross_kernel(first, each, table_ref, window_high, window_low, high_ref, low_ref, *outs):
    tile = outs[0].shape[0] // each
    dims = ((1,), (1,))
    pair = 3 - len(outs) if each % 2 == 0 else 1

    @pl.loop(0, each // pair)
    def _(step):
        entries = [first + step * pair + place for place in range(pair)]
        rows = [pl.ds(pl.multiple_of(table_ref[at], tile), len(outs) * tile) for at in entries]
        window = [
            jnp.concatenate([term[at, :] for at in rows], 0) for term in (window_high, window_low)
        ]
        result = dot(window[0], high_ref[...], dims) + (
            dot(window[0], low_ref[...], dims) + dot(window[1], high_ref[...], dims)
        )
        here = pl.ds(pl.multiple_of(step * pair * tile, tile), pair * tile)
        for part, cross_ref in enumerate(outs):
            cross_ref[here, :] = result[part * pair * tile : (part + 1) * pair * tile]


def cross_call(table, first, parts, each, tile, window, panel, cost):
    in_vmem = pl.BlockSpec(memory_space=pltpu.VMEM)
    return pl.pallas_call(
        functools.partial(cross_kernel, first, each),
        in_specs=[pl.BlockSpec(memory_space=pltpu.SMEM)] + [in_vmem] * 4,
        out_specs=[in_vmem] * parts,
        out_shape=[jax.ShapeDtypeStruct((each * tile, panel[0].shape[0]), f32)] * parts,
        compiler_params=pltpu.CompilerParams(vmem_limit_bytes=ROOM),
        cost_estimate=cost,
        name="cross",
    )(table, *window, *panel)


def residual_kernel(firsts, each, table_ref, window_high, window_low, weight_ref, *refs):
    totals, (out_ref, sent, departures) = refs[: len(firsts)], refs[-3:]
    _, tile, columns = sent.shape
    chunk = min(256, columns)

    def leaving(place, entry):
        start = pl.multiple_of(table_ref[entry], tile)
        return pltpu.make_async_copy(
            sent.at[place], out_ref.at[pl.ds(start, tile), :], departures.at[place]
        )

    for part, (first, total) in enumerate(zip(firsts, totals)):
        high, low = split(total[...])
        terms = jnp.concatenate([high, high, low], 1)
        rows = [pl.ds(pl.multiple_of(table_ref[first + at], tile), tile) for at in range(each)]
        for start in range(0, columns, chunk):
            here = slice(start, start + chunk)
            product = dot(terms, weight_ref[:, here], ((1,), (0,)))
            for at in range(each):
                window = window_high[rows[at], here].astype(f32)
                window = window + window_low[rows[at], here].astype(f32)
                sent[part * each + at, :, here] = window - product[at * tile : (at + 1) * tile]
        for at in range(each):
            leaving(part * each + at, first + at).start()

    for part, first in enumerate(firsts):

        @pl.loop(0, each)
        def _(step):
            leaving(part * each + step, first + step).wait()


def residual_call(table, firsts, tile, window, weight, totals, before, cost=BRIEF):
    (rows, columns), each = window[0].shape, totals[0].shape[0] // tile
    in_vmem = pl.BlockSpec(memory_space=pltpu.VMEM)
    operands = [table, *window, weight, *totals]
    in_specs = [pl.BlockSpec(memory_space=pltpu.SMEM)] + [in_vmem] * (len(operands) - 1)
    aliases = {}
    if before is not None:
        aliases = {len(operands): 0}
        operands.append(before)
        in_specs.append(pl.BlockSpec(memory_space=pl.ANY))
    return pl.pallas_call(
        functools.partial(residual_kernel, firsts, each),
        in_specs=in_specs,
        out_specs=pl.BlockSpec(memory_space=pl.ANY),
        scratch_shapes=[
            pltpu.VMEM((len(firsts) * each, tile, columns), f32),
            pltpu.SemaphoreType.DMA((len(firsts) * each,)),
        ],
        out_shape=jax.ShapeDtypeStruct((rows, columns), f32),
        input_output_aliases=aliases,
        compiler_params=pltpu.CompilerParams(vmem_limit_bytes=ROOM),
        cost_estimate=cost,
        name="residual",
    )(*operands)


def eliminate(diagonal):
    size, lanes, tile = BLOCK, 128, 8
    tiles = size // tile
    row_at = [lax.broadcasted_iota(jnp.int32, (tile, lanes), 0) + tile * t for t in range(tiles)]
    lane_at = lax.broadcasted_iota(jnp.int32, (tile, lanes), 1)
    spread = [
        [
            jnp.broadcast_to(diagonal[tile * t : tile * (t + 1), k : k + 1], (tile, lanes))
            for t in range(tiles)
        ]
        for k in range(size)
    ]
    inverse = [jnp.where(row_at[t] == lane_at, 1.0, 0.0) for t in range(tiles)]
    lower = [jnp.zeros((tile, lanes), f32) for _ in range(tiles)]
    scale = [jnp.zeros((tile, lanes), f32) for _ in range(tiles)]
    for j in range(size):
        own, at = j // tile, j % tile
        pivot = spread[j][own][at : at + 1, :]
        reciprocal = 1.0 / pivot
        root = lax.rsqrt(pivot)
        inverse_row = inverse[own][at : at + 1, :]
        factor = {}
        for t in range(own, tiles):
            column = spread[j][t]
            factor[t] = column * reciprocal
            if t == own:
                factor[t] = jnp.where(row_at[t] > j, factor[t], 0.0)
                scale[t] = jnp.where(row_at[t] == j, root, scale[t])
                lower[t] = jnp.where((lane_at == j) & (row_at[t] >= j), column * root, lower[t])
            else:
                lower[t] = jnp.where(lane_at == j, column * root, lower[t])
            inverse[t] = inverse[t] - factor[t] * inverse_row
        for k in range(j + 1, size):
            entry = spread[j][k // tile][k % tile : k % tile + 1, :]
            for t in range(k // tile, tiles):
                spread[k][t] = spread[k][t] - factor[t] * entry
    inverse = [inverse[t] * scale[t] for t in range(tiles)]
    return jnp.concatenate(lower, 0), jnp.concatenate(inverse, 0)


def factor_kernel(begin, end, last, ins, outs):
    state_ref, lower_ref = outs[:2]
    state_ref[...] = ins[0][...]
    if begin:
        lower_ref[...] = ins[1][...]
    size = state_ref.shape[0]
    column_at = lax.broadcasted_iota(jnp.int32, (BLOCK, size), 1)
    row_at = lax.broadcasted_iota(jnp.int32, (BLOCK, size), 0)
    for step in range(begin, end):
        start, stop = step * BLOCK, (step + 1) * BLOCK
        rows = state_ref[start:stop, :]
        lower, inverse = eliminate(rows[:, start:stop])
        lower_ref[start:stop, :] = lower
        inside = (column_at >= start) & (column_at < stop)
        rows = jnp.where(inside, jnp.where(column_at - start == row_at, 1.0, 0.0), rows)
        done = dot(inverse[:, :BLOCK], rows, ((1,), (0,)), precise)
        state_ref[start:stop, :] = done
        if stop < size:
            upper = jnp.where(column_at >= stop, done, 0.0)
            update = dot(upper, done, ((0,), (0,)), precise)[stop:, :]
            below_at = lax.broadcasted_iota(jnp.int32, (size - stop, size), 1)
            below = jnp.where(
                (below_at >= start) & (below_at < stop), 0.0, state_ref[stop:, :]
            )
            state_ref[stop:, :] = below - update
    if last:
        whole_ref = ins[2]
        triangle_ref, inverse_ref, weight_ref = outs[2:]
        column_at = lax.broadcasted_iota(jnp.int32, (size, size), 1)
        row_at = lax.broadcasted_iota(jnp.int32, (size, size), 0)
        edge = (row_at // BLOCK + 1) * BLOCK
        state = state_ref[...]
        inverse = jnp.where(column_at <= row_at, state, 0.0)
        lower = lower_ref[...]
        wide = jnp.concatenate([lower] * (size // lower.shape[1]), 1)
        for step in range(size // BLOCK):
            start, stop = step * BLOCK, (step + 1) * BLOCK
            shift = start % lower.shape[1]
            part = wide[start:stop, :]
            if shift:
                part = pltpu.roll(part, shift, 1)
            lower_full = jnp.where(
                (column_at[start:stop, :] >= start) & (column_at[start:stop, :] < stop), part, 0.0
            )
            state_ref[start:stop, :] = lower_full
        triangle_ref[...] = jnp.where(column_at >= edge, state, 0.0) + state_ref[...].T
        half = dot(inverse, whole_ref[...], ((1,), (0,)), precise)
        inverse_ref[...] = inverse
        weight = dot(inverse, half, ((0,), (0,)), precise)
        high, low = split(weight)
        for term, part in enumerate((high, low, high)):
            weight_ref[term * size : (term + 1) * size, :] = part


def factor_call(begin, end, operands, whole=None):
    size = operands[0].shape[1]
    operands = list(operands)
    shapes = [
        jax.ShapeDtypeStruct((size, size), f32),
        jax.ShapeDtypeStruct((size, 128), f32),
    ]
    if whole is not None:
        operands.append(whole)
        shapes += [
            jax.ShapeDtypeStruct((size, size), f32),
            jax.ShapeDtypeStruct((size, size), f32),
            jax.ShapeDtypeStruct((3 * size, whole.shape[1]), bf16),
        ]
    in_specs = [pl.BlockSpec(memory_space=pltpu.VMEM)] * len(operands)

    def body(*refs):
        factor_kernel(begin, end, whole is not None, refs[: len(operands)], refs[len(operands) :])

    return pl.pallas_call(
        body,
        out_shape=shapes,
        in_specs=in_specs,
        out_specs=[pl.BlockSpec(memory_space=pltpu.VMEM)] * len(shapes),
        compiler_params=pltpu.CompilerParams(vmem_limit_bytes=24 * MIB),
        cost_estimate=BRIEF,
        name="factor",
    )(*operands)


def flip(value, bit, size):
    return lax.ppermute(value, "row", [(i, i ^ bit) for i in range(size)])


def exchange(value, step, bits):
    size = 2 << len(bits)
    return lax.ppermute(
        value, "row", [(i, i ^ (bits[-1 - step] if i & 1 else bits[step])) for i in range(size)]
    )


def relative_owners(bits):
    owners = [0]
    for bit in reversed(bits):
        owners = [owner | bit for owner in owners] + owners
    return owners


def sum_shares(kept, arrived, bits):
    pairs, count = [(kept, 0), (arrived, 0)], kept.shape[0]
    cut = lambda array, at: lax.slice_in_dim(array, at, at + count, axis=0)
    for step in range(len(bits)):
        count //= 2
        out, others = yield sum(cut(array, at) for array, at in pairs)
        pairs = [(array, at + count) for array, at in pairs]
        if others:
            pairs[0] = (after(pairs[0][0], *others), pairs[0][1])
        pairs.append((exchange(out, step, bits), 0))
    yield sum(cut(array, at) for array, at in pairs)


def gather_panel(shard, depth):
    up = [(i, (i - 1) % depth) for i in range(depth)]
    down = [(i, (i + 1) % depth) for i in range(depth)]
    above = [lax.ppermute(shard, "col", up)]
    below = []
    later, _ = lax.optimization_barrier((shard, above[0]))
    for step in range(2, depth):
        if step % 2 == 0:
            above.append(lax.ppermute(above[-1], "col", up))
        else:
            below.append(lax.ppermute(below[-1] if below else later, "col", down))
    return [shard, *above, *below[::-1]]


def spread(part, bits, *others):
    for step in reversed(range(1, len(bits))):
        part = jnp.concatenate([after(exchange(part, step, bits), *others), part], 0)
    return part


def local(panel_cols, window_cols):
    size = lax.axis_size("row")
    depth = lax.axis_size("col")
    here = lax.axis_index("row").astype(jnp.int32)
    place = lax.axis_index("col").astype(jnp.int32).reshape(1)
    bits = [1 << shift for shift in range(1, size.bit_length() - 1)]
    steps = len(bits)
    share = window_cols.shape[0] // size

    tile = share // 2

    owners = [jnp.asarray(relative_owners(order), jnp.int32) for order in (bits, bits[::-1])]
    table_of = lambda device: share * (device ^ jnp.where(device & 1, owners[1], owners[0]))
    kept, given = table_of(here), table_of(here ^ 1)
    count = kept.shape[0]
    table = jnp.concatenate([kept, kept + tile, given, given + tile])
    entry = lambda side, half: (side * 2 + half) * count

    shards = gather_panel(panel_cols, depth)
    window = hold_call(table, place, window_cols)
    whole, high, low, gram = gram_call(after(place, window[0]), shards)

    def products(side, half, parts, cost, *others):
        first = after(table, *others)
        return cross_call(first, entry(side, half), parts, count, tile, window, (high, low), cost)

    (given,) = products(1, 0, 1, BRIEF, gram)
    arrived = flip(given, 1, size)
    gram = gram + exchange(gram, 0, bits)
    (kept,) = products(0, 0, 1, LONG, given)
    early = sum_shares(kept, arrived, bits)
    early_sum = next(early)
    gram = after(gram, kept)
    (given,) = products(1, 1, 1, BRIEF, early_sum, gram)
    arrived = flip(given, 1, size)
    for step in range(1, steps):
        gram = gram + after(exchange(gram, step, bits), given)
    (kept,) = products(0, 1, 1, LONG, given)
    late = sum_shares(after(kept, gram), arrived, bits)
    late_sum = next(late)
    gram = gram + flip(gram, 1, size)

    blocks = whole.shape[0] // BLOCK
    cuts = (0, blocks * 3 // 8, blocks * 6 // 8, blocks)
    state = factor_call(0, cuts[1], [after(gram, late_sum)])
    early_sum = early.send((early_sum, (state[0],)))
    state = factor_call(cuts[1], cuts[2], [after(state[0], early_sum), state[1]])
    late_sum = late.send((late_sum, (state[0],)))
    for _ in range(1, steps):
        early_sum = early.send((early_sum, (late_sum,)))
    _, _, triangle, inverse, weight = factor_call(
        cuts[2], blocks, [after(state[0], late_sum, early_sum), state[1]], whole
    )
    for _ in range(1, steps):
        late_sum = late.send((late_sum, ()))
    late_sum = after(late_sum, weight)

    early_near = spread(early_sum, bits, late_sum)
    early_far = exchange(early_near, 0, bits)
    nearer = lambda side, half: entry(side, half) + count // 2
    subtract = lambda firsts, *others: residual_call(table, firsts, tile, window, weight, *others)
    parts = [early_near, flip(early_near, 1, size)]
    residual = subtract([nearer(0, 0), nearer(1, 0)], parts, None)
    late_near = spread(late_sum, bits, residual)
    late_far = exchange(late_near, 0, bits)
    late_back = flip(late_near, 1, size)
    residual = subtract([nearer(0, 1)], [late_near], residual, LONG)
    parts = [late_back, early_far, flip(early_far, 1, size)]
    residual = subtract([nearer(1, 1), entry(0, 0), entry(1, 0)], parts, residual)
    late_far, residual = lax.optimization_barrier((late_far, residual))
    parts = [late_far, flip(late_far, 1, size)]
    residual = subtract([entry(0, 1), entry(1, 1)], parts, residual)
    summed = jnp.concatenate([after(early_sum, late_far), late_sum], 0)
    top_rows = dot(summed, inverse, ((1,), (1,)), precise)
    return triangle, top_rows, residual


def solution(mesh):
    return jax.shard_map(
        local,
        mesh=mesh,
        in_specs=(P("col", "row"), P("col", "row")),
        out_specs=(P(), P(("col", "row"), None), P("col", "row")),
        check_vma=False,
    )
```

```python
import functools

import jax
import jax.numpy as jnp
from jax import lax
from jax.experimental import pallas as pl
from jax.experimental.pallas import tpu as pltpu
from jax.sharding import PartitionSpec as P

precise = lax.Precision.HIGHEST
f32, bf16 = jnp.float32, jnp.bfloat16
BLOCK = 32
MIB = 1 << 20
ROOM = 24 * MIB
LONG = pl.CostEstimate(flops=100_000_000_000, bytes_accessed=1, transcendentals=0)
BRIEF = pl.CostEstimate(flops=1, bytes_accessed=1, transcendentals=0)


def dot(left, right, dims, precision=None):
    return lax.dot_general(
        left, right, (dims, ((), ())), precision=precision, preferred_element_type=f32
    )


def split(value):
    high = value.astype(bf16)
    return high, (value - high.astype(f32)).astype(bf16)


def after(value, *others):
    return lax.optimization_barrier((value, *others))[0]


def gram_kernel(place_ref, *refs):
    shards, (whole_ref, high_ref, low_ref, gram_ref) = refs[:-4], refs[-4:]
    rows = shards[0].shape[0]
    for step, shard in enumerate(shards):
        owner = lax.rem(place_ref[0] + step, len(shards))
        whole_ref[pl.ds(pl.multiple_of(owner * rows, rows), rows), :] = shard[...]
    whole = whole_ref[...]
    gram_ref[...] = dot(whole, whole, ((1,), (1,)), precise)
    high_ref[...], low_ref[...] = split(whole)


def gram_call(place, shards):
    rows, columns = shards[0].shape
    panel = rows * len(shards)
    in_vmem = pl.BlockSpec(memory_space=pltpu.VMEM)
    return pl.pallas_call(
        gram_kernel,
        in_specs=[pl.BlockSpec(memory_space=pltpu.SMEM)] + [in_vmem] * len(shards),
        out_specs=[in_vmem] * 4,
        out_shape=[
            jax.ShapeDtypeStruct((panel, columns), f32),
            jax.ShapeDtypeStruct((panel, columns), bf16),
            jax.ShapeDtypeStruct((panel, columns), bf16),
            jax.ShapeDtypeStruct((panel, panel), f32),
        ],
        compiler_params=pltpu.CompilerParams(vmem_limit_bytes=24 * MIB),
        cost_estimate=LONG,
        name="gram",
    )(place, *shards)


def hold_kernel(table_ref, place_ref, window_ref, high_ref, low_ref, held, arrivals):
    slots, rows, _ = held.shape
    count = window_ref.shape[0] // rows

    def arriving(step):
        start = pl.multiple_of(step * rows, rows)
        slot = lax.rem(step, slots)
        return pltpu.make_async_copy(
            window_ref.at[pl.ds(start, rows), :], held.at[slot], arrivals.at[slot]
        )

    for step in range(min(slots, count)):
        arriving(step).start()

    @pl.loop(0, count)
    def _(step):
        arriving(step).wait()
        high, low = split(held[lax.rem(step, slots)])
        here = pl.ds(pl.multiple_of(step * rows, rows), rows)
        high_ref[here, :] = high
        low_ref[here, :] = low

        @pl.when(step + slots < count)
        def _():
            arriving(step + slots).start()


def hold_call(table, place, window):
    rows, columns = window.shape
    tile = min(256, rows)
    scalars = pl.BlockSpec(memory_space=pltpu.SMEM)
    return pl.pallas_call(
        hold_kernel,
        in_specs=[scalars, scalars, pl.BlockSpec(memory_space=pl.ANY)],
        out_specs=[pl.BlockSpec(memory_space=pltpu.VMEM)] * 2,
        scratch_shapes=[
            pltpu.VMEM((4, tile, columns), f32),
            pltpu.SemaphoreType.DMA((4,)),
        ],
        out_shape=[jax.ShapeDtypeStruct(window.shape, bf16)] * 2,
        compiler_params=pltpu.CompilerParams(vmem_limit_bytes=ROOM),
        cost_estimate=BRIEF,
        name="hold",
    )(table, place, window)


def cross_kernel(first, each, table_ref, window_high, window_low, high_ref, low_ref, *outs):
    tile = outs[0].shape[0] // each
    dims = ((1,), (1,))
    pair = 3 - len(outs) if each % 2 == 0 else 1

    @pl.loop(0, each // pair)
    def _(step):
        entries = [first + step * pair + place for place in range(pair)]
        rows = [pl.ds(pl.multiple_of(table_ref[at], tile), len(outs) * tile) for at in entries]
        window = [
            jnp.concatenate([term[at, :] for at in rows], 0) for term in (window_high, window_low)
        ]
        result = dot(window[0], high_ref[...], dims) + (
            dot(window[0], low_ref[...], dims) + dot(window[1], high_ref[...], dims)
        )
        here = pl.ds(pl.multiple_of(step * pair * tile, tile), pair * tile)
        for part, cross_ref in enumerate(outs):
            cross_ref[here, :] = result[part * pair * tile : (part + 1) * pair * tile]


def cross_call(table, first, parts, each, tile, window, panel, cost):
    in_vmem = pl.BlockSpec(memory_space=pltpu.VMEM)
    return pl.pallas_call(
        functools.partial(cross_kernel, first, each),
        in_specs=[pl.BlockSpec(memory_space=pltpu.SMEM)] + [in_vmem] * 4,
        out_specs=[in_vmem] * parts,
        out_shape=[jax.ShapeDtypeStruct((each * tile, panel[0].shape[0]), f32)] * parts,
        compiler_params=pltpu.CompilerParams(vmem_limit_bytes=ROOM),
        cost_estimate=cost,
        name="cross",
    )(table, *window, *panel)


def residual_kernel(firsts, each, table_ref, window_high, window_low, weight_ref, *refs):
    totals, (out_ref, sent, departures) = refs[: len(firsts)], refs[-3:]
    _, tile, columns = sent.shape
    chunk = min(256, columns)

    def leaving(place, entry):
        start = pl.multiple_of(table_ref[entry], tile)
        return pltpu.make_async_copy(
            sent.at[place], out_ref.at[pl.ds(start, tile), :], departures.at[place]
        )

    for part, (first, total) in enumerate(zip(firsts, totals)):
        high, low = split(total[...])
        terms = jnp.concatenate([high, high, low], 1)
        rows = [pl.ds(pl.multiple_of(table_ref[first + at], tile), tile) for at in range(each)]
        for start in range(0, columns, chunk):
            here = slice(start, start + chunk)
            product = dot(terms, weight_ref[:, here], ((1,), (0,)))
            for at in range(each):
                window = window_high[rows[at], here].astype(f32)
                window = window + window_low[rows[at], here].astype(f32)
                sent[part * each + at, :, here] = window - product[at * tile : (at + 1) * tile]
        for at in range(each):
            leaving(part * each + at, first + at).start()

    for part, first in enumerate(firsts):

        @pl.loop(0, each)
        def _(step):
            leaving(part * each + step, first + step).wait()


def residual_call(table, firsts, tile, window, weight, totals, before, cost=BRIEF):
    (rows, columns), each = window[0].shape, totals[0].shape[0] // tile
    in_vmem = pl.BlockSpec(memory_space=pltpu.VMEM)
    operands = [table, *window, weight, *totals]
    in_specs = [pl.BlockSpec(memory_space=pltpu.SMEM)] + [in_vmem] * (len(operands) - 1)
    aliases = {}
    if before is not None:
        aliases = {len(operands): 0}
        operands.append(before)
        in_specs.append(pl.BlockSpec(memory_space=pl.ANY))
    return pl.pallas_call(
        functools.partial(residual_kernel, firsts, each),
        in_specs=in_specs,
        out_specs=pl.BlockSpec(memory_space=pl.ANY),
        scratch_shapes=[
            pltpu.VMEM((len(firsts) * each, tile, columns), f32),
            pltpu.SemaphoreType.DMA((len(firsts) * each,)),
        ],
        out_shape=jax.ShapeDtypeStruct((rows, columns), f32),
        input_output_aliases=aliases,
        compiler_params=pltpu.CompilerParams(vmem_limit_bytes=ROOM),
        cost_estimate=cost,
        name="residual",
    )(*operands)


def eliminate(diagonal):
    size, lanes, tile = BLOCK, 128, 8
    tiles = size // tile
    row_at = [lax.broadcasted_iota(jnp.int32, (tile, lanes), 0) + tile * t for t in range(tiles)]
    lane_at = lax.broadcasted_iota(jnp.int32, (tile, lanes), 1)
    spread = [
        [
            jnp.broadcast_to(diagonal[tile * t : tile * (t + 1), k : k + 1], (tile, lanes))
            for t in range(tiles)
        ]
        for k in range(size)
    ]
    inverse = [jnp.where(row_at[t] == lane_at, 1.0, 0.0) for t in range(tiles)]
    lower = [jnp.zeros((tile, lanes), f32) for _ in range(tiles)]
    scale = [jnp.zeros((tile, lanes), f32) for _ in range(tiles)]
    for j in range(size):
        own, at = j // tile, j % tile
        pivot = spread[j][own][at : at + 1, :]
        reciprocal = 1.0 / pivot
        root = lax.rsqrt(pivot)
        inverse_row = inverse[own][at : at + 1, :]
        factor = {}
        for t in range(own, tiles):
            column = spread[j][t]
            factor[t] = column * reciprocal
            if t == own:
                factor[t] = jnp.where(row_at[t] > j, factor[t], 0.0)
                scale[t] = jnp.where(row_at[t] == j, root, scale[t])
                lower[t] = jnp.where((lane_at == j) & (row_at[t] >= j), column * root, lower[t])
            else:
                lower[t] = jnp.where(lane_at == j, column * root, lower[t])
            inverse[t] = inverse[t] - factor[t] * inverse_row
        for k in range(j + 1, size):
            entry = spread[j][k // tile][k % tile : k % tile + 1, :]
            for t in range(k // tile, tiles):
                spread[k][t] = spread[k][t] - factor[t] * entry
    inverse = [inverse[t] * scale[t] for t in range(tiles)]
    return jnp.concatenate(lower, 0), jnp.concatenate(inverse, 0)


def factor_kernel(begin, end, last, ins, outs):
    state_ref, lower_ref = outs[:2]
    state_ref[...] = ins[0][...]
    if begin:
        lower_ref[...] = ins[1][...]
    size = state_ref.shape[0]
    column_at = lax.broadcasted_iota(jnp.int32, (BLOCK, size), 1)
    row_at = lax.broadcasted_iota(jnp.int32, (BLOCK, size), 0)
    for step in range(begin, end):
        start, stop = step * BLOCK, (step + 1) * BLOCK
        rows = state_ref[start:stop, :]
        lower, inverse = eliminate(rows[:, start:stop])
        lower_ref[start:stop, :] = lower
        inside = (column_at >= start) & (column_at < stop)
        rows = jnp.where(inside, jnp.where(column_at - start == row_at, 1.0, 0.0), rows)
        done = dot(inverse[:, :BLOCK], rows, ((1,), (0,)), precise)
        state_ref[start:stop, :] = done
        if stop < size:
            upper = jnp.where(column_at >= stop, done, 0.0)
            update = dot(upper, done, ((0,), (0,)), precise)[stop:, :]
            below_at = lax.broadcasted_iota(jnp.int32, (size - stop, size), 1)
            below = jnp.where(
                (below_at >= start) & (below_at < stop), 0.0, state_ref[stop:, :]
            )
            state_ref[stop:, :] = below - update
    if last:
        whole_ref = ins[2]
        triangle_ref, inverse_ref, weight_ref = outs[2:]
        column_at = lax.broadcasted_iota(jnp.int32, (size, size), 1)
        row_at = lax.broadcasted_iota(jnp.int32, (size, size), 0)
        edge = (row_at // BLOCK + 1) * BLOCK
        state = state_ref[...]
        inverse = jnp.where(column_at <= row_at, state, 0.0)
        lower = lower_ref[...]
        wide = jnp.concatenate([lower] * (size // lower.shape[1]), 1)
        for step in range(size // BLOCK):
            start, stop = step * BLOCK, (step + 1) * BLOCK
            shift = start % lower.shape[1]
            part = wide[start:stop, :]
            if shift:
                part = pltpu.roll(part, shift, 1)
            lower_full = jnp.where(
                (column_at[start:stop, :] >= start) & (column_at[start:stop, :] < stop), part, 0.0
            )
            state_ref[start:stop, :] = lower_full
        triangle_ref[...] = jnp.where(column_at >= edge, state, 0.0) + state_ref[...].T
        half = dot(inverse, whole_ref[...], ((1,), (0,)), precise)
        inverse_ref[...] = inverse
        weight = dot(inverse, half, ((0,), (0,)), precise)
        high, low = split(weight)
        for term, part in enumerate((high, low, high)):
            weight_ref[term * size : (term + 1) * size, :] = part


def factor_call(begin, end, operands, whole=None):
    size = operands[0].shape[1]
    operands = list(operands)
    shapes = [
        jax.ShapeDtypeStruct((size, size), f32),
        jax.ShapeDtypeStruct((size, 128), f32),
    ]
    if whole is not None:
        operands.append(whole)
        shapes += [
            jax.ShapeDtypeStruct((size, size), f32),
            jax.ShapeDtypeStruct((size, size), f32),
            jax.ShapeDtypeStruct((3 * size, whole.shape[1]), bf16),
        ]
    in_specs = [pl.BlockSpec(memory_space=pltpu.VMEM)] * len(operands)

    def body(*refs):
        factor_kernel(begin, end, whole is not None, refs[: len(operands)], refs[len(operands) :])

    return pl.pallas_call(
        body,
        out_shape=shapes,
        in_specs=in_specs,
        out_specs=[pl.BlockSpec(memory_space=pltpu.VMEM)] * len(shapes),
        compiler_params=pltpu.CompilerParams(vmem_limit_bytes=24 * MIB),
        cost_estimate=BRIEF,
        name="factor",
    )(*operands)


def flip(value, bit, size):
    return lax.ppermute(value, "row", [(i, i ^ bit) for i in range(size)])


def exchange(value, step, bits):
    size = 2 << len(bits)
    return lax.ppermute(
        value, "row", [(i, i ^ (bits[-1 - step] if i & 1 else bits[step])) for i in range(size)]
    )


def relative_owners(bits):
    owners = [0]
    for bit in reversed(bits):
        owners = [owner | bit for owner in owners] + owners
    return owners


def sum_shares(kept, arrived, bits):
    pairs, count = [(kept, 0), (arrived, 0)], kept.shape[0]
    cut = lambda array, at: lax.slice_in_dim(array, at, at + count, axis=0)
    for step in range(len(bits)):
        count //= 2
        out, others = yield sum(cut(array, at) for array, at in pairs)
        pairs = [(array, at + count) for array, at in pairs]
        if others:
            pairs[0] = (after(pairs[0][0], *others), pairs[0][1])
        pairs.append((exchange(out, step, bits), 0))
    yield sum(cut(array, at) for array, at in pairs)


def gather_panel(shard, depth):
    up = [(i, (i - 1) % depth) for i in range(depth)]
    down = [(i, (i + 1) % depth) for i in range(depth)]
    above = [lax.ppermute(shard, "col", up)]
    below = []
    later, _ = lax.optimization_barrier((shard, above[0]))
    for step in range(2, depth):
        if step % 2 == 0:
            above.append(lax.ppermute(above[-1], "col", up))
        else:
            below.append(lax.ppermute(below[-1] if below else later, "col", down))
    return [shard, *above, *below[::-1]]


def spread(part, bits, *others):
    for step in reversed(range(1, len(bits))):
        part = jnp.concatenate([after(exchange(part, step, bits), *others), part], 0)
    return part


def local(panel_cols, window_cols):
    size = lax.axis_size("row")
    depth = lax.axis_size("col")
    here = lax.axis_index("row").astype(jnp.int32)
    place = lax.axis_index("col").astype(jnp.int32).reshape(1)
    bits = [1 << shift for shift in range(1, size.bit_length() - 1)]
    steps = len(bits)
    share = window_cols.shape[0] // size

    tile = share // 2

    owners = [jnp.asarray(relative_owners(order), jnp.int32) for order in (bits, bits[::-1])]
    table_of = lambda device: share * (device ^ jnp.where(device & 1, owners[1], owners[0]))
    kept, given = table_of(here), table_of(here ^ 1)
    count = kept.shape[0]
    table = jnp.concatenate([kept, kept + tile, given, given + tile])
    entry = lambda side, half: (side * 2 + half) * count

    shards = gather_panel(panel_cols, depth)
    window = hold_call(table, place, window_cols)
    whole, high, low, gram = gram_call(after(place, window[0]), shards)

    def products(side, half, parts, cost, *others):
        first = after(table, *others)
        return cross_call(first, entry(side, half), parts, count, tile, window, (high, low), cost)

    (given,) = products(1, 0, 1, BRIEF, gram)
    arrived = flip(given, 1, size)
    gram = gram + exchange(gram, 0, bits)
    (kept,) = products(0, 0, 1, LONG, given)
    early = sum_shares(kept, arrived, bits)
    early_sum = next(early)
    gram = after(gram, kept)
    (given,) = products(1, 1, 1, BRIEF, early_sum, gram)
    arrived = flip(given, 1, size)
    for step in range(1, steps):
        gram = gram + after(exchange(gram, step, bits), given)
    (kept,) = products(0, 1, 1, LONG, given)
    late = sum_shares(after(kept, gram), arrived, bits)
    late_sum = next(late)
    gram = gram + flip(gram, 1, size)

    blocks = whole.shape[0] // BLOCK
    cuts = (0, blocks * 3 // 8, blocks * 6 // 8, blocks)
    state = factor_call(0, cuts[1], [after(gram, late_sum)])
    early_sum = early.send((early_sum, (state[0],)))
    late_sum = late.send((late_sum, (early_sum,)))
    state = factor_call(cuts[1], cuts[2], [after(state[0], early_sum, late_sum), state[1]])
    for _ in range(1, steps):
        early_sum = early.send((early_sum, (state[0],)))
    for _ in range(1, steps):
        late_sum = late.send((late_sum, (early_sum,)))
    _, _, triangle, inverse, weight = factor_call(
        cuts[2], blocks, [after(state[0], early_sum, late_sum), state[1]], whole
    )

    early_near = spread(early_sum, bits, weight)
    late_near = spread(late_sum, bits, early_near)
    early_far, late_far = [exchange(part, 0, bits) for part in (early_near, late_near)]
    nearer = lambda side, half: entry(side, half) + count // 2
    subtract = lambda firsts, *others: residual_call(table, firsts, tile, window, weight, *others)
    parts = [early_near, flip(early_near, 1, size), late_near]
    residual = subtract([nearer(0, 0), nearer(1, 0), nearer(0, 1)], parts, None)
    late_back = flip(late_near, 1, size)
    early_far, residual = lax.optimization_barrier((early_far, residual))
    residual = subtract([nearer(1, 1), entry(0, 0)], [late_back, early_far], residual)
    late_far, residual = lax.optimization_barrier((late_far, residual))
    parts = [flip(early_far, 1, size), late_far, flip(late_far, 1, size)]
    residual = subtract([entry(1, 0), entry(0, 1), entry(1, 1)], parts, residual)
    summed = jnp.concatenate([after(early_sum, late_far), late_sum], 0)
    top_rows = dot(summed, inverse, ((1,), (1,)), precise)
    return triangle, top_rows, residual


def solution(mesh):
    return jax.shard_map(
        local,
        mesh=mesh,
        in_specs=(P("col", "row"), P("col", "row")),
        out_specs=(P(), P(("col", "row"), None), P("col", "row")),
        check_vma=False,
    )
```

```python
import functools

import jax
import jax.numpy as jnp
from jax import lax
from jax.experimental import pallas as pl
from jax.experimental.pallas import tpu as pltpu
from jax.sharding import PartitionSpec as P

precise = lax.Precision.HIGHEST
f32, bf16 = jnp.float32, jnp.bfloat16
BLOCK = 32
MIB = 1 << 20
ROOM = 24 * MIB
LONG = pl.CostEstimate(flops=100_000_000_000, bytes_accessed=1, transcendentals=0)
BRIEF = pl.CostEstimate(flops=1, bytes_accessed=1, transcendentals=0)


def dot(left, right, dims, precision=None):
    return lax.dot_general(
        left, right, (dims, ((), ())), precision=precision, preferred_element_type=f32
    )


def split(value):
    high = value.astype(bf16)
    return high, (value - high.astype(f32)).astype(bf16)


def after(value, *others):
    return lax.optimization_barrier((value, *others))[0]


def gram_kernel(place_ref, *refs):
    shards, (whole_ref, high_ref, low_ref, gram_ref) = refs[:-4], refs[-4:]
    rows = shards[0].shape[0]
    for step, shard in enumerate(shards):
        owner = lax.rem(place_ref[0] + step, len(shards))
        whole_ref[pl.ds(pl.multiple_of(owner * rows, rows), rows), :] = shard[...]
    whole = whole_ref[...]
    gram_ref[...] = dot(whole, whole, ((1,), (1,)), precise)
    high_ref[...], low_ref[...] = split(whole)


def gram_call(place, shards):
    rows, columns = shards[0].shape
    panel = rows * len(shards)
    in_vmem = pl.BlockSpec(memory_space=pltpu.VMEM)
    return pl.pallas_call(
        gram_kernel,
        in_specs=[pl.BlockSpec(memory_space=pltpu.SMEM)] + [in_vmem] * len(shards),
        out_specs=[in_vmem] * 4,
        out_shape=[
            jax.ShapeDtypeStruct((panel, columns), f32),
            jax.ShapeDtypeStruct((panel, columns), bf16),
            jax.ShapeDtypeStruct((panel, columns), bf16),
            jax.ShapeDtypeStruct((panel, panel), f32),
        ],
        compiler_params=pltpu.CompilerParams(vmem_limit_bytes=24 * MIB),
        cost_estimate=LONG,
        name="gram",
    )(place, *shards)


def hold_kernel(table_ref, place_ref, window_ref, high_ref, low_ref, held, arrivals):
    slots, rows, _ = held.shape
    count = window_ref.shape[0] // rows

    def arriving(step):
        start = pl.multiple_of(step * rows, rows)
        slot = lax.rem(step, slots)
        return pltpu.make_async_copy(
            window_ref.at[pl.ds(start, rows), :], held.at[slot], arrivals.at[slot]
        )

    for step in range(min(slots, count)):
        arriving(step).start()

    @pl.loop(0, count)
    def _(step):
        arriving(step).wait()
        high, low = split(held[lax.rem(step, slots)])
        here = pl.ds(pl.multiple_of(step * rows, rows), rows)
        high_ref[here, :] = high
        low_ref[here, :] = low

        @pl.when(step + slots < count)
        def _():
            arriving(step + slots).start()


def hold_call(table, place, window):
    rows, columns = window.shape
    tile = min(256, rows)
    scalars = pl.BlockSpec(memory_space=pltpu.SMEM)
    return pl.pallas_call(
        hold_kernel,
        in_specs=[scalars, scalars, pl.BlockSpec(memory_space=pl.ANY)],
        out_specs=[pl.BlockSpec(memory_space=pltpu.VMEM)] * 2,
        scratch_shapes=[
            pltpu.VMEM((4, tile, columns), f32),
            pltpu.SemaphoreType.DMA((4,)),
        ],
        out_shape=[jax.ShapeDtypeStruct(window.shape, bf16)] * 2,
        compiler_params=pltpu.CompilerParams(vmem_limit_bytes=ROOM),
        cost_estimate=BRIEF,
        name="hold",
    )(table, place, window)


def cross_kernel(first, each, table_ref, window_high, window_low, high_ref, low_ref, *outs):
    tile = outs[0].shape[0] // each
    dims = ((1,), (1,))
    pair = 3 - len(outs) if each % 2 == 0 else 1

    @pl.loop(0, each // pair)
    def _(step):
        entries = [first + step * pair + place for place in range(pair)]
        rows = [pl.ds(pl.multiple_of(table_ref[at], tile), len(outs) * tile) for at in entries]
        window = [
            jnp.concatenate([term[at, :] for at in rows], 0) for term in (window_high, window_low)
        ]
        result = dot(window[0], high_ref[...], dims) + (
            dot(window[0], low_ref[...], dims) + dot(window[1], high_ref[...], dims)
        )
        here = pl.ds(pl.multiple_of(step * pair * tile, tile), pair * tile)
        for part, cross_ref in enumerate(outs):
            cross_ref[here, :] = result[part * pair * tile : (part + 1) * pair * tile]


def cross_call(table, first, parts, each, tile, window, panel, cost):
    in_vmem = pl.BlockSpec(memory_space=pltpu.VMEM)
    return pl.pallas_call(
        functools.partial(cross_kernel, first, each),
        in_specs=[pl.BlockSpec(memory_space=pltpu.SMEM)] + [in_vmem] * 4,
        out_specs=[in_vmem] * parts,
        out_shape=[jax.ShapeDtypeStruct((each * tile, panel[0].shape[0]), f32)] * parts,
        compiler_params=pltpu.CompilerParams(vmem_limit_bytes=ROOM),
        cost_estimate=cost,
        name="cross",
    )(table, *window, *panel)


def residual_kernel(firsts, each, table_ref, window_high, window_low, weight_ref, *refs):
    totals, (out_ref, sent, departures) = refs[: len(firsts)], refs[-3:]
    _, tile, columns = sent.shape
    chunk = min(256, columns)

    def leaving(place, entry, part):
        rows = pl.ds(pl.multiple_of(table_ref[entry], tile), tile)
        here = pl.ds(part * chunk, chunk)
        return pltpu.make_async_copy(
            sent.at[place, :, here], out_ref.at[rows, here], departures.at[place, part]
        )

    for part, (first, total) in enumerate(zip(firsts, totals)):
        high, low = split(total[...])
        terms = jnp.concatenate([high, high, low], 1)
        rows = [pl.ds(pl.multiple_of(table_ref[first + at], tile), tile) for at in range(each)]
        for start in range(0, columns, chunk):
            here = slice(start, start + chunk)
            product = dot(terms, weight_ref[:, here], ((1,), (0,)))
            for at in range(each):
                window = window_high[rows[at], here].astype(f32)
                window = window + window_low[rows[at], here].astype(f32)
                sent[part * each + at, :, here] = window - product[at * tile : (at + 1) * tile]
                leaving(part * each + at, first + at, start // chunk).start()

    for part, first in enumerate(firsts):
        for at in range(each):
            for piece in range(columns // chunk):
                leaving(part * each + at, first + at, piece).wait()


def residual_call(table, firsts, tile, window, weight, totals, before, cost=BRIEF):
    (rows, columns), each = window[0].shape, totals[0].shape[0] // tile
    in_vmem = pl.BlockSpec(memory_space=pltpu.VMEM)
    operands = [table, *window, weight, *totals]
    in_specs = [pl.BlockSpec(memory_space=pltpu.SMEM)] + [in_vmem] * (len(operands) - 1)
    aliases = {}
    if before is not None:
        aliases = {len(operands): 0}
        operands.append(before)
        in_specs.append(pl.BlockSpec(memory_space=pl.ANY))
    return pl.pallas_call(
        functools.partial(residual_kernel, firsts, each),
        in_specs=in_specs,
        out_specs=pl.BlockSpec(memory_space=pl.ANY),
        scratch_shapes=[
            pltpu.VMEM((len(firsts) * each, tile, columns), f32),
            pltpu.SemaphoreType.DMA((len(firsts) * each, columns // min(256, columns))),
        ],
        out_shape=jax.ShapeDtypeStruct((rows, columns), f32),
        input_output_aliases=aliases,
        compiler_params=pltpu.CompilerParams(vmem_limit_bytes=ROOM),
        cost_estimate=cost,
        name="residual",
    )(*operands)


def eliminate(diagonal):
    size, lanes, tile = BLOCK, 128, 8
    tiles = size // tile
    row_at = [lax.broadcasted_iota(jnp.int32, (tile, lanes), 0) + tile * t for t in range(tiles)]
    lane_at = lax.broadcasted_iota(jnp.int32, (tile, lanes), 1)
    spread = [
        [
            jnp.broadcast_to(diagonal[tile * t : tile * (t + 1), k : k + 1], (tile, lanes))
            for t in range(tiles)
        ]
        for k in range(size)
    ]
    inverse = [jnp.where(row_at[t] == lane_at, 1.0, 0.0) for t in range(tiles)]
    lower = [jnp.zeros((tile, lanes), f32) for _ in range(tiles)]
    scale = [jnp.zeros((tile, lanes), f32) for _ in range(tiles)]
    for j in range(size):
        own, at = j // tile, j % tile
        pivot = spread[j][own][at : at + 1, :]
        reciprocal = 1.0 / pivot
        root = lax.rsqrt(pivot)
        inverse_row = inverse[own][at : at + 1, :]
        factor = {}
        for t in range(own, tiles):
            column = spread[j][t]
            factor[t] = column * reciprocal
            if t == own:
                factor[t] = jnp.where(row_at[t] > j, factor[t], 0.0)
                scale[t] = jnp.where(row_at[t] == j, root, scale[t])
                lower[t] = jnp.where((lane_at == j) & (row_at[t] >= j), column * root, lower[t])
            else:
                lower[t] = jnp.where(lane_at == j, column * root, lower[t])
            inverse[t] = inverse[t] - factor[t] * inverse_row
        for k in range(j + 1, size):
            entry = spread[j][k // tile][k % tile : k % tile + 1, :]
            for t in range(k // tile, tiles):
                spread[k][t] = spread[k][t] - factor[t] * entry
    inverse = [inverse[t] * scale[t] for t in range(tiles)]
    return jnp.concatenate(lower, 0), jnp.concatenate(inverse, 0)


def factor_kernel(begin, end, last, ins, outs):
    state_ref, lower_ref = outs[:2]
    state_ref[...] = ins[0][...]
    if begin:
        lower_ref[...] = ins[1][...]
    size = state_ref.shape[0]
    column_at = lax.broadcasted_iota(jnp.int32, (BLOCK, size), 1)
    row_at = lax.broadcasted_iota(jnp.int32, (BLOCK, size), 0)
    for step in range(begin, end):
        start, stop = step * BLOCK, (step + 1) * BLOCK
        rows = state_ref[start:stop, :]
        lower, inverse = eliminate(rows[:, start:stop])
        lower_ref[start:stop, :] = lower
        inside = (column_at >= start) & (column_at < stop)
        rows = jnp.where(inside, jnp.where(column_at - start == row_at, 1.0, 0.0), rows)
        done = dot(inverse[:, :BLOCK], rows, ((1,), (0,)), precise)
        state_ref[start:stop, :] = done
        if stop < size:
            upper = jnp.where(column_at >= stop, done, 0.0)
            update = dot(upper, done, ((0,), (0,)), precise)[stop:, :]
            below_at = lax.broadcasted_iota(jnp.int32, (size - stop, size), 1)
            below = jnp.where(
                (below_at >= start) & (below_at < stop), 0.0, state_ref[stop:, :]
            )
            state_ref[stop:, :] = below - update
    if last:
        whole_ref = ins[2]
        triangle_ref, inverse_ref, weight_ref = outs[2:]
        column_at = lax.broadcasted_iota(jnp.int32, (size, size), 1)
        row_at = lax.broadcasted_iota(jnp.int32, (size, size), 0)
        edge = (row_at // BLOCK + 1) * BLOCK
        state = state_ref[...]
        inverse = jnp.where(column_at <= row_at, state, 0.0)
        lower = lower_ref[...]
        wide = jnp.concatenate([lower] * (size // lower.shape[1]), 1)
        for step in range(size // BLOCK):
            start, stop = step * BLOCK, (step + 1) * BLOCK
            shift = start % lower.shape[1]
            part = wide[start:stop, :]
            if shift:
                part = pltpu.roll(part, shift, 1)
            lower_full = jnp.where(
                (column_at[start:stop, :] >= start) & (column_at[start:stop, :] < stop), part, 0.0
            )
            state_ref[start:stop, :] = lower_full
        triangle_ref[...] = jnp.where(column_at >= edge, state, 0.0) + state_ref[...].T
        half = dot(inverse, whole_ref[...], ((1,), (0,)), precise)
        inverse_ref[...] = inverse
        weight = dot(inverse, half, ((0,), (0,)), precise)
        high, low = split(weight)
        for term, part in enumerate((high, low, high)):
            weight_ref[term * size : (term + 1) * size, :] = part


def factor_call(begin, end, operands, whole=None):
    size = operands[0].shape[1]
    operands = list(operands)
    shapes = [
        jax.ShapeDtypeStruct((size, size), f32),
        jax.ShapeDtypeStruct((size, 128), f32),
    ]
    if whole is not None:
        operands.append(whole)
        shapes += [
            jax.ShapeDtypeStruct((size, size), f32),
            jax.ShapeDtypeStruct((size, size), f32),
            jax.ShapeDtypeStruct((3 * size, whole.shape[1]), bf16),
        ]
    in_specs = [pl.BlockSpec(memory_space=pltpu.VMEM)] * len(operands)

    def body(*refs):
        factor_kernel(begin, end, whole is not None, refs[: len(operands)], refs[len(operands) :])

    return pl.pallas_call(
        body,
        out_shape=shapes,
        in_specs=in_specs,
        out_specs=[pl.BlockSpec(memory_space=pltpu.VMEM)] * len(shapes),
        compiler_params=pltpu.CompilerParams(vmem_limit_bytes=24 * MIB),
        cost_estimate=BRIEF,
        name="factor",
    )(*operands)


def flip(value, bit, size):
    return lax.ppermute(value, "row", [(i, i ^ bit) for i in range(size)])


def exchange(value, step, bits):
    size = 2 << len(bits)
    return lax.ppermute(
        value, "row", [(i, i ^ (bits[-1 - step] if i & 1 else bits[step])) for i in range(size)]
    )


def relative_owners(bits):
    owners = [0]
    for bit in reversed(bits):
        owners = [owner | bit for owner in owners] + owners
    return owners


def sum_shares(kept, arrived, bits):
    pairs, count = [(kept, 0), (arrived, 0)], kept.shape[0]
    cut = lambda array, at: lax.slice_in_dim(array, at, at + count, axis=0)
    for step in range(len(bits)):
        count //= 2
        out, others = yield sum(cut(array, at) for array, at in pairs)
        pairs = [(array, at + count) for array, at in pairs]
        if others:
            pairs[0] = (after(pairs[0][0], *others), pairs[0][1])
        pairs.append((exchange(out, step, bits), 0))
    yield sum(cut(array, at) for array, at in pairs)


def gather_panel(shard, depth):
    up = [(i, (i - 1) % depth) for i in range(depth)]
    down = [(i, (i + 1) % depth) for i in range(depth)]
    above = [lax.ppermute(shard, "col", up)]
    below = []
    later, _ = lax.optimization_barrier((shard, above[0]))
    for step in range(2, depth):
        if step % 2 == 0:
            above.append(lax.ppermute(above[-1], "col", up))
        else:
            below.append(lax.ppermute(below[-1] if below else later, "col", down))
    return [shard, *above, *below[::-1]]


def spread(part, bits, *others):
    for step in reversed(range(1, len(bits))):
        part = jnp.concatenate([after(exchange(part, step, bits), *others), part], 0)
    return part


def local(panel_cols, window_cols):
    size = lax.axis_size("row")
    depth = lax.axis_size("col")
    here = lax.axis_index("row").astype(jnp.int32)
    place = lax.axis_index("col").astype(jnp.int32).reshape(1)
    bits = [1 << shift for shift in range(1, size.bit_length() - 1)]
    steps = len(bits)
    share = window_cols.shape[0] // size

    tile = share // 2

    owners = [jnp.asarray(relative_owners(order), jnp.int32) for order in (bits, bits[::-1])]
    table_of = lambda device: share * (device ^ jnp.where(device & 1, owners[1], owners[0]))
    kept, given = table_of(here), table_of(here ^ 1)
    count = kept.shape[0]
    table = jnp.concatenate([kept, kept + tile, given, given + tile])
    entry = lambda side, half: (side * 2 + half) * count

    shards = gather_panel(panel_cols, depth)
    window = hold_call(table, place, window_cols)
    whole, high, low, gram = gram_call(after(place, window[0]), shards)

    def products(side, half, parts, cost, *others):
        first = after(table, *others)
        return cross_call(first, entry(side, half), parts, count, tile, window, (high, low), cost)

    (given,) = products(1, 0, 1, BRIEF, gram)
    arrived = flip(given, 1, size)
    gram = gram + exchange(gram, 0, bits)
    (kept,) = products(0, 0, 1, LONG, given)
    early = sum_shares(kept, arrived, bits)
    early_sum = next(early)
    gram = after(gram, kept)
    (given,) = products(1, 1, 1, BRIEF, early_sum, gram)
    arrived = flip(given, 1, size)
    for step in range(1, steps):
        gram = gram + after(exchange(gram, step, bits), given)
    (kept,) = products(0, 1, 1, LONG, given)
    late = sum_shares(after(kept, gram), arrived, bits)
    late_sum = next(late)
    gram = gram + flip(gram, 1, size)

    blocks = whole.shape[0] // BLOCK
    cuts = (0, blocks * 3 // 8, blocks * 6 // 8, blocks)
    state = factor_call(0, cuts[1], [after(gram, late_sum)])
    early_sum = early.send((early_sum, (state[0],)))
    late_sum = late.send((late_sum, (early_sum,)))
    state = factor_call(cuts[1], cuts[2], [after(state[0], early_sum, late_sum), state[1]])
    for _ in range(1, steps):
        early_sum = early.send((early_sum, (state[0],)))
    for _ in range(1, steps):
        late_sum = late.send((late_sum, (early_sum,)))
    _, _, triangle, inverse, weight = factor_call(
        cuts[2], blocks, [after(state[0], early_sum, late_sum), state[1]], whole
    )

    early_near = spread(early_sum, bits, weight)
    late_near = spread(late_sum, bits, early_near)
    early_far, late_far = [exchange(part, 0, bits) for part in (early_near, late_near)]
    nearer = lambda side, half: entry(side, half) + count // 2
    subtract = lambda firsts, *others: residual_call(table, firsts, tile, window, weight, *others)
    parts = [early_near, flip(early_near, 1, size), late_near]
    residual = subtract([nearer(0, 0), nearer(1, 0), nearer(0, 1)], parts, None)
    late_back = flip(late_near, 1, size)
    early_far, residual = lax.optimization_barrier((early_far, residual))
    residual = subtract([nearer(1, 1), entry(0, 0)], [late_back, early_far], residual)
    late_far, residual = lax.optimization_barrier((late_far, residual))
    parts = [flip(early_far, 1, size), late_far, flip(late_far, 1, size)]
    residual = subtract([entry(1, 0), entry(0, 1), entry(1, 1)], parts, residual)
    summed = jnp.concatenate([after(early_sum, late_far), late_sum], 0)
    top_rows = dot(summed, inverse, ((1,), (1,)), precise)
    return triangle, top_rows, residual


def solution(mesh):
    return jax.shard_map(
        local,
        mesh=mesh,
        in_specs=(P("col", "row"), P("col", "row")),
        out_specs=(P(), P(("col", "row"), None), P("col", "row")),
        check_vma=False,
    )
```

```python
import functools

import jax
import jax.numpy as jnp
from jax import lax
from jax.experimental import pallas as pl
from jax.experimental.pallas import tpu as pltpu
from jax.sharding import PartitionSpec as P

precise = lax.Precision.HIGHEST
f32, bf16 = jnp.float32, jnp.bfloat16
BLOCK = 32
MIB = 1 << 20
ROOM = 24 * MIB
LONG = pl.CostEstimate(flops=100_000_000_000, bytes_accessed=1, transcendentals=0)
BRIEF = pl.CostEstimate(flops=1, bytes_accessed=1, transcendentals=0)


def dot(left, right, dims, precision=None):
    return lax.dot_general(
        left, right, (dims, ((), ())), precision=precision, preferred_element_type=f32
    )


def split(value):
    high = value.astype(bf16)
    return high, (value - high.astype(f32)).astype(bf16)


def after(value, *others):
    return lax.optimization_barrier((value, *others))[0]


def gram_kernel(place_ref, *refs):
    shards, (whole_ref, high_ref, low_ref, gram_ref) = refs[:-4], refs[-4:]
    rows = shards[0].shape[0]
    for step, shard in enumerate(shards):
        owner = lax.rem(place_ref[0] + step, len(shards))
        whole_ref[pl.ds(pl.multiple_of(owner * rows, rows), rows), :] = shard[...]
    whole = whole_ref[...]
    gram_ref[...] = dot(whole, whole, ((1,), (1,)), precise)
    high_ref[...], low_ref[...] = split(whole)


def gram_call(place, shards):
    rows, columns = shards[0].shape
    panel = rows * len(shards)
    in_vmem = pl.BlockSpec(memory_space=pltpu.VMEM)
    return pl.pallas_call(
        gram_kernel,
        in_specs=[pl.BlockSpec(memory_space=pltpu.SMEM)] + [in_vmem] * len(shards),
        out_specs=[in_vmem] * 4,
        out_shape=[
            jax.ShapeDtypeStruct((panel, columns), f32),
            jax.ShapeDtypeStruct((panel, columns), bf16),
            jax.ShapeDtypeStruct((panel, columns), bf16),
            jax.ShapeDtypeStruct((panel, panel), f32),
        ],
        compiler_params=pltpu.CompilerParams(vmem_limit_bytes=24 * MIB),
        cost_estimate=LONG,
        name="gram",
    )(place, *shards)


def hold_kernel(table_ref, place_ref, window_ref, high_ref, low_ref, held, arrivals):
    slots, rows, _ = held.shape
    count = window_ref.shape[0] // rows

    def arriving(step):
        start = pl.multiple_of(step * rows, rows)
        slot = lax.rem(step, slots)
        return pltpu.make_async_copy(
            window_ref.at[pl.ds(start, rows), :], held.at[slot], arrivals.at[slot]
        )

    for step in range(min(slots, count)):
        arriving(step).start()

    @pl.loop(0, count)
    def _(step):
        arriving(step).wait()
        high, low = split(held[lax.rem(step, slots)])
        here = pl.ds(pl.multiple_of(step * rows, rows), rows)
        high_ref[here, :] = high
        low_ref[here, :] = low

        @pl.when(step + slots < count)
        def _():
            arriving(step + slots).start()


def hold_call(table, place, window):
    rows, columns = window.shape
    tile = min(256, rows)
    scalars = pl.BlockSpec(memory_space=pltpu.SMEM)
    return pl.pallas_call(
        hold_kernel,
        in_specs=[scalars, scalars, pl.BlockSpec(memory_space=pl.ANY)],
        out_specs=[pl.BlockSpec(memory_space=pltpu.VMEM)] * 2,
        scratch_shapes=[
            pltpu.VMEM((4, tile, columns), f32),
            pltpu.SemaphoreType.DMA((4,)),
        ],
        out_shape=[jax.ShapeDtypeStruct(window.shape, bf16)] * 2,
        compiler_params=pltpu.CompilerParams(vmem_limit_bytes=ROOM),
        cost_estimate=BRIEF,
        name="hold",
    )(table, place, window)


def cross_kernel(first, each, table_ref, window_high, window_low, high_ref, low_ref, *outs):
    tile = outs[0].shape[0] // each
    dims = ((1,), (1,))
    pair = 3 - len(outs) if each % 2 == 0 else 1

    @pl.loop(0, each // pair)
    def _(step):
        entries = [first + step * pair + place for place in range(pair)]
        rows = [pl.ds(pl.multiple_of(table_ref[at], tile), len(outs) * tile) for at in entries]
        window = [
            jnp.concatenate([term[at, :] for at in rows], 0) for term in (window_high, window_low)
        ]
        result = dot(window[0], high_ref[...], dims) + (
            dot(window[0], low_ref[...], dims) + dot(window[1], high_ref[...], dims)
        )
        here = pl.ds(pl.multiple_of(step * pair * tile, tile), pair * tile)
        for part, cross_ref in enumerate(outs):
            cross_ref[here, :] = result[part * pair * tile : (part + 1) * pair * tile]


def cross_call(table, first, parts, each, tile, window, panel, cost):
    in_vmem = pl.BlockSpec(memory_space=pltpu.VMEM)
    return pl.pallas_call(
        functools.partial(cross_kernel, first, each),
        in_specs=[pl.BlockSpec(memory_space=pltpu.SMEM)] + [in_vmem] * 4,
        out_specs=[in_vmem] * parts,
        out_shape=[jax.ShapeDtypeStruct((each * tile, panel[0].shape[0]), f32)] * parts,
        compiler_params=pltpu.CompilerParams(vmem_limit_bytes=ROOM),
        cost_estimate=cost,
        name="cross",
    )(table, *window, *panel)


def residual_kernel(firsts, each, table_ref, window_high, window_low, weight_ref, *refs):
    totals, (out_ref, sent, departures) = refs[: len(firsts)], refs[-3:]
    _, tile, columns = sent.shape
    chunk = min(256, columns)

    def leaving(place, entry, part):
        rows = pl.ds(pl.multiple_of(table_ref[entry], tile), tile)
        here = pl.ds(part * chunk, chunk)
        return pltpu.make_async_copy(
            sent.at[place, :, here], out_ref.at[rows, here], departures.at[place, part]
        )

    pairs = [split(total[...]) for total in totals]
    high, low = [jnp.concatenate(term, 0) for term in zip(*pairs)]
    terms = jnp.concatenate([high, high, low], 1)
    entries = [first + at for first in firsts for at in range(each)]
    rows = [pl.ds(pl.multiple_of(table_ref[at], tile), tile) for at in entries]
    for start in range(0, columns, chunk):
        here = slice(start, start + chunk)
        product = dot(terms, weight_ref[:, here], ((1,), (0,)))
        for place, entry in enumerate(entries):
            window = window_high[rows[place], here].astype(f32)
            window = window + window_low[rows[place], here].astype(f32)
            sent[place, :, here] = window - product[place * tile : (place + 1) * tile]
            leaving(place, entry, start // chunk).start()

    for part, first in enumerate(firsts):
        for at in range(each):
            for piece in range(columns // chunk):
                leaving(part * each + at, first + at, piece).wait()


def residual_call(table, firsts, tile, window, weight, totals, before, cost=BRIEF):
    (rows, columns), each = window[0].shape, totals[0].shape[0] // tile
    in_vmem = pl.BlockSpec(memory_space=pltpu.VMEM)
    operands = [table, *window, weight, *totals]
    in_specs = [pl.BlockSpec(memory_space=pltpu.SMEM)] + [in_vmem] * (len(operands) - 1)
    aliases = {}
    if before is not None:
        aliases = {len(operands): 0}
        operands.append(before)
        in_specs.append(pl.BlockSpec(memory_space=pl.ANY))
    return pl.pallas_call(
        functools.partial(residual_kernel, firsts, each),
        in_specs=in_specs,
        out_specs=pl.BlockSpec(memory_space=pl.ANY),
        scratch_shapes=[
            pltpu.VMEM((len(firsts) * each, tile, columns), f32),
            pltpu.SemaphoreType.DMA((len(firsts) * each, columns // min(256, columns))),
        ],
        out_shape=jax.ShapeDtypeStruct((rows, columns), f32),
        input_output_aliases=aliases,
        compiler_params=pltpu.CompilerParams(vmem_limit_bytes=ROOM),
        cost_estimate=cost,
        name="residual",
    )(*operands)


def eliminate(diagonal):
    size, lanes, tile = BLOCK, 128, 8
    tiles = size // tile
    row_at = [lax.broadcasted_iota(jnp.int32, (tile, lanes), 0) + tile * t for t in range(tiles)]
    lane_at = lax.broadcasted_iota(jnp.int32, (tile, lanes), 1)
    spread = [
        [
            jnp.broadcast_to(diagonal[tile * t : tile * (t + 1), k : k + 1], (tile, lanes))
            for t in range(tiles)
        ]
        for k in range(size)
    ]
    inverse = [jnp.where(row_at[t] == lane_at, 1.0, 0.0) for t in range(tiles)]
    lower = [jnp.zeros((tile, lanes), f32) for _ in range(tiles)]
    row_of = lambda parts, row: parts[row // tile][row % tile : row % tile + 1, :]
    pivot = row_of(spread[0], 0)
    for j in range(size):
        own = j // tile
        root = lax.rsqrt(pivot)
        if j + 1 < size:
            entry = row_of(spread[j], j + 1) * root
            pivot = row_of(spread[j + 1], j + 1) - entry * entry
        inverse_row = row_of(inverse, j) * root
        column = {t: spread[j][t] * root for t in range(own, tiles)}
        below = dict(column)
        below[own] = jnp.where(row_at[own] > j, column[own], 0.0)
        lower[own] = jnp.where((lane_at == j) & (row_at[own] >= j), column[own], lower[own])
        for t in range(own + 1, tiles):
            lower[t] = jnp.where(lane_at == j, column[t], lower[t])
        for t in range(own, tiles):
            inverse[t] = inverse[t] - below[t] * inverse_row
        inverse[own] = jnp.where(row_at[own] == j, inverse_row, inverse[own])
        for k in range(j + 1, size):
            entry = row_of(column, k)
            for t in range(k // tile, tiles):
                spread[k][t] = spread[k][t] - below[t] * entry
    return jnp.concatenate(lower, 0), jnp.concatenate(inverse, 0)


def factor_kernel(begin, end, last, ins, outs):
    state_ref, lower_ref = outs[:2]
    state_ref[...] = ins[0][...]
    if begin:
        lower_ref[...] = ins[1][...]
    size = state_ref.shape[0]
    column_at = lax.broadcasted_iota(jnp.int32, (BLOCK, size), 1)
    row_at = lax.broadcasted_iota(jnp.int32, (BLOCK, size), 0)
    for step in range(begin, end):
        start, stop = step * BLOCK, (step + 1) * BLOCK
        rows = state_ref[start:stop, :]
        lower, inverse = eliminate(rows[:, start:stop])
        lower_ref[start:stop, :] = lower
        inside = (column_at >= start) & (column_at < stop)
        rows = jnp.where(inside, jnp.where(column_at - start == row_at, 1.0, 0.0), rows)
        done = dot(inverse[:, :BLOCK], rows, ((1,), (0,)), precise)
        state_ref[start:stop, :] = done
        if stop < size:
            upper = jnp.where(column_at >= stop, done, 0.0)
            update = dot(upper, done, ((0,), (0,)), precise)[stop:, :]
            below_at = lax.broadcasted_iota(jnp.int32, (size - stop, size), 1)
            below = jnp.where(
                (below_at >= start) & (below_at < stop), 0.0, state_ref[stop:, :]
            )
            state_ref[stop:, :] = below - update
    if last:
        whole_ref = ins[2]
        triangle_ref, inverse_ref, weight_ref = outs[2:]
        column_at = lax.broadcasted_iota(jnp.int32, (size, size), 1)
        row_at = lax.broadcasted_iota(jnp.int32, (size, size), 0)
        edge = (row_at // BLOCK + 1) * BLOCK
        state = state_ref[...]
        inverse = jnp.where(column_at <= row_at, state, 0.0)
        lower = lower_ref[...]
        wide = jnp.concatenate([lower] * (size // lower.shape[1]), 1)
        for step in range(size // BLOCK):
            start, stop = step * BLOCK, (step + 1) * BLOCK
            shift = start % lower.shape[1]
            part = wide[start:stop, :]
            if shift:
                part = pltpu.roll(part, shift, 1)
            lower_full = jnp.where(
                (column_at[start:stop, :] >= start) & (column_at[start:stop, :] < stop), part, 0.0
            )
            state_ref[start:stop, :] = lower_full
        triangle_ref[...] = jnp.where(column_at >= edge, state, 0.0) + state_ref[...].T
        half = dot(inverse, whole_ref[...], ((1,), (0,)), precise)
        inverse_ref[...] = inverse
        weight = dot(inverse, half, ((0,), (0,)), precise)
        high, low = split(weight)
        for term, part in enumerate((high, low, high)):
            weight_ref[term * size : (term + 1) * size, :] = part


def factor_call(begin, end, operands, whole=None):
    size = operands[0].shape[1]
    operands = list(operands)
    shapes = [
        jax.ShapeDtypeStruct((size, size), f32),
        jax.ShapeDtypeStruct((size, 128), f32),
    ]
    if whole is not None:
        operands.append(whole)
        shapes += [
            jax.ShapeDtypeStruct((size, size), f32),
            jax.ShapeDtypeStruct((size, size), f32),
            jax.ShapeDtypeStruct((3 * size, whole.shape[1]), bf16),
        ]
    in_specs = [pl.BlockSpec(memory_space=pltpu.VMEM)] * len(operands)

    def body(*refs):
        factor_kernel(begin, end, whole is not None, refs[: len(operands)], refs[len(operands) :])

    return pl.pallas_call(
        body,
        out_shape=shapes,
        in_specs=in_specs,
        out_specs=[pl.BlockSpec(memory_space=pltpu.VMEM)] * len(shapes),
        compiler_params=pltpu.CompilerParams(vmem_limit_bytes=24 * MIB),
        cost_estimate=BRIEF,
        name="factor",
    )(*operands)


def flip(value, bit, size):
    return lax.ppermute(value, "row", [(i, i ^ bit) for i in range(size)])


def exchange(value, step, bits):
    size = 2 << len(bits)
    return lax.ppermute(
        value, "row", [(i, i ^ (bits[-1 - step] if i & 1 else bits[step])) for i in range(size)]
    )


def relative_owners(bits):
    owners = [0]
    for bit in reversed(bits):
        owners = [owner | bit for owner in owners] + owners
    return owners


def sum_shares(kept, arrived, bits):
    pairs, count = [(kept, 0), (arrived, 0)], kept.shape[0]
    cut = lambda array, at: lax.slice_in_dim(array, at, at + count, axis=0)
    for step in range(len(bits)):
        count //= 2
        out, others = yield sum(cut(array, at) for array, at in pairs)
        pairs = [(array, at + count) for array, at in pairs]
        if others:
            pairs[0] = (after(pairs[0][0], *others), pairs[0][1])
        pairs.append((exchange(out, step, bits), 0))
    yield sum(cut(array, at) for array, at in pairs)


def gather_panel(shard, depth):
    up = [(i, (i - 1) % depth) for i in range(depth)]
    down = [(i, (i + 1) % depth) for i in range(depth)]
    above = [lax.ppermute(shard, "col", up)]
    below = []
    later, _ = lax.optimization_barrier((shard, above[0]))
    for step in range(2, depth):
        if step % 2 == 0:
            above.append(lax.ppermute(above[-1], "col", up))
        else:
            below.append(lax.ppermute(below[-1] if below else later, "col", down))
    return [shard, *above, *below[::-1]]


def spread(part, bits, *others):
    for step in reversed(range(1, len(bits))):
        part = jnp.concatenate([after(exchange(part, step, bits), *others), part], 0)
    return part


def local(panel_cols, window_cols):
    size = lax.axis_size("row")
    depth = lax.axis_size("col")
    here = lax.axis_index("row").astype(jnp.int32)
    place = lax.axis_index("col").astype(jnp.int32).reshape(1)
    bits = [1 << shift for shift in range(1, size.bit_length() - 1)]
    steps = len(bits)
    share = window_cols.shape[0] // size

    tile = share // 2

    owners = [jnp.asarray(relative_owners(order), jnp.int32) for order in (bits, bits[::-1])]
    table_of = lambda device: share * (device ^ jnp.where(device & 1, owners[1], owners[0]))
    kept, given = table_of(here), table_of(here ^ 1)
    count = kept.shape[0]
    table = jnp.concatenate([kept, kept + tile, given, given + tile])
    entry = lambda side, half: (side * 2 + half) * count

    shards = gather_panel(panel_cols, depth)
    window = hold_call(table, place, window_cols)
    whole, high, low, gram = gram_call(after(place, window[0]), shards)

    def products(side, half, parts, cost, *others):
        first = after(table, *others)
        return cross_call(first, entry(side, half), parts, count, tile, window, (high, low), cost)

    (given,) = products(1, 0, 1, BRIEF, gram)
    arrived = flip(given, 1, size)
    gram = gram + exchange(gram, 0, bits)
    (kept,) = products(0, 0, 1, LONG, given)
    early = sum_shares(kept, arrived, bits)
    early_sum = next(early)
    gram = after(gram, kept)
    (given,) = products(1, 1, 1, BRIEF, early_sum, gram)
    arrived = flip(given, 1, size)
    for step in range(1, steps):
        gram = gram + after(exchange(gram, step, bits), given)
    (kept,) = products(0, 1, 1, LONG, given)
    late = sum_shares(after(kept, gram), arrived, bits)
    late_sum = next(late)
    gram = gram + flip(gram, 1, size)

    blocks = whole.shape[0] // BLOCK
    cuts = (0, blocks * 3 // 8, blocks * 6 // 8, blocks)
    state = factor_call(0, cuts[1], [after(gram, late_sum)])
    early_sum = early.send((early_sum, (state[0],)))
    late_sum = late.send((late_sum, (early_sum,)))
    state = factor_call(cuts[1], cuts[2], [after(state[0], early_sum, late_sum), state[1]])
    for _ in range(1, steps):
        early_sum = early.send((early_sum, (state[0],)))
    for _ in range(1, steps):
        late_sum = late.send((late_sum, (early_sum,)))
    _, _, triangle, inverse, weight = factor_call(
        cuts[2], blocks, [after(state[0], early_sum, late_sum), state[1]], whole
    )

    early_near = spread(early_sum, bits, weight)
    late_near = spread(late_sum, bits, early_near)
    early_far, late_far = [exchange(part, 0, bits) for part in (early_near, late_near)]
    nearer = lambda side, half: entry(side, half) + count // 2
    subtract = lambda firsts, *others: residual_call(table, firsts, tile, window, weight, *others)
    parts = [early_near, flip(early_near, 1, size), late_near]
    residual = subtract([nearer(0, 0), nearer(1, 0), nearer(0, 1)], parts, None)
    late_back = flip(late_near, 1, size)
    early_far, residual = lax.optimization_barrier((early_far, residual))
    residual = subtract([nearer(1, 1), entry(0, 0)], [late_back, early_far], residual)
    late_far, residual = lax.optimization_barrier((late_far, residual))
    parts = [flip(early_far, 1, size), late_far, flip(late_far, 1, size)]
    residual = subtract([entry(1, 0), entry(0, 1), entry(1, 1)], parts, residual)
    summed = jnp.concatenate([after(early_sum, late_far), late_sum], 0)
    top_rows = dot(summed, inverse, ((1,), (1,)), precise)
    return triangle, top_rows, residual


def solution(mesh):
    return jax.shard_map(
        local,
        mesh=mesh,
        in_specs=(P("col", "row"), P("col", "row")),
        out_specs=(P(), P(("col", "row"), None), P("col", "row")),
        check_vma=False,
    )
```

```python
import functools

import jax
import jax.numpy as jnp
from jax import lax
from jax.experimental import pallas as pl
from jax.experimental.pallas import tpu as pltpu
from jax.sharding import PartitionSpec as P

precise = lax.Precision.HIGHEST
f32, bf16 = jnp.float32, jnp.bfloat16
BLOCK = 32
MIB = 1 << 20
ROOM = 24 * MIB
LONG = pl.CostEstimate(flops=100_000_000_000, bytes_accessed=1, transcendentals=0)
BRIEF = pl.CostEstimate(flops=1, bytes_accessed=1, transcendentals=0)


def dot(left, right, dims, precision=None):
    return lax.dot_general(
        left, right, (dims, ((), ())), precision=precision, preferred_element_type=f32
    )


def split(value):
    high = value.astype(bf16)
    return high, (value - high.astype(f32)).astype(bf16)


def after(value, *others):
    return lax.optimization_barrier((value, *others))[0]


def gram_kernel(place_ref, *refs):
    shards, (whole_ref, high_ref, low_ref, gram_ref) = refs[:-4], refs[-4:]
    rows = shards[0].shape[0]
    for step, shard in enumerate(shards):
        owner = lax.rem(place_ref[0] + step, len(shards))
        whole_ref[pl.ds(pl.multiple_of(owner * rows, rows), rows), :] = shard[...]
    whole = whole_ref[...]
    gram_ref[...] = dot(whole, whole, ((1,), (1,)), precise)
    high_ref[...], low_ref[...] = split(whole.T)


def gram_call(place, shards):
    rows, columns = shards[0].shape
    panel = rows * len(shards)
    in_vmem = pl.BlockSpec(memory_space=pltpu.VMEM)
    return pl.pallas_call(
        gram_kernel,
        in_specs=[pl.BlockSpec(memory_space=pltpu.SMEM)] + [in_vmem] * len(shards),
        out_specs=[in_vmem] * 4,
        out_shape=[
            jax.ShapeDtypeStruct((panel, columns), f32),
            jax.ShapeDtypeStruct((columns, panel), bf16),
            jax.ShapeDtypeStruct((columns, panel), bf16),
            jax.ShapeDtypeStruct((panel, panel), f32),
        ],
        compiler_params=pltpu.CompilerParams(vmem_limit_bytes=24 * MIB),
        cost_estimate=LONG,
        name="gram",
    )(place, *shards)


def hold_kernel(table_ref, place_ref, window_ref, high_ref, low_ref, held, arrivals):
    slots, rows, _ = held.shape
    count = window_ref.shape[0] // rows

    def arriving(step):
        start = pl.multiple_of(step * rows, rows)
        slot = lax.rem(step, slots)
        return pltpu.make_async_copy(
            window_ref.at[pl.ds(start, rows), :], held.at[slot], arrivals.at[slot]
        )

    for step in range(min(slots, count)):
        arriving(step).start()

    @pl.loop(0, count)
    def _(step):
        arriving(step).wait()
        high, low = split(held[lax.rem(step, slots)])
        here = pl.ds(pl.multiple_of(step * rows, rows), rows)
        high_ref[here, :] = high
        low_ref[here, :] = low

        @pl.when(step + slots < count)
        def _():
            arriving(step + slots).start()


def hold_call(table, place, window):
    rows, columns = window.shape
    tile = min(256, rows)
    scalars = pl.BlockSpec(memory_space=pltpu.SMEM)
    return pl.pallas_call(
        hold_kernel,
        in_specs=[scalars, scalars, pl.BlockSpec(memory_space=pl.ANY)],
        out_specs=[pl.BlockSpec(memory_space=pltpu.VMEM)] * 2,
        scratch_shapes=[
            pltpu.VMEM((4, tile, columns), f32),
            pltpu.SemaphoreType.DMA((4,)),
        ],
        out_shape=[jax.ShapeDtypeStruct(window.shape, bf16)] * 2,
        compiler_params=pltpu.CompilerParams(vmem_limit_bytes=ROOM),
        cost_estimate=BRIEF,
        name="hold",
    )(table, place, window)


def cross_kernel(first, each, table_ref, window_high, window_low, high_ref, low_ref, *outs):
    tile = outs[0].shape[0] // each
    dims = ((1,), (0,))
    pair = 3 - len(outs) if each % 2 == 0 else 1

    @pl.loop(0, each // pair)
    def _(step):
        entries = [first + step * pair + place for place in range(pair)]
        rows = [pl.ds(pl.multiple_of(table_ref[at], tile), len(outs) * tile) for at in entries]
        window = [
            jnp.concatenate([term[at, :] for at in rows], 0) for term in (window_high, window_low)
        ]
        result = dot(window[0], high_ref[...], dims) + (
            dot(window[0], low_ref[...], dims) + dot(window[1], high_ref[...], dims)
        )
        here = pl.ds(pl.multiple_of(step * pair * tile, tile), pair * tile)
        for part, cross_ref in enumerate(outs):
            cross_ref[here, :] = result[part * pair * tile : (part + 1) * pair * tile]


def cross_call(table, first, parts, each, tile, window, panel, cost):
    in_vmem = pl.BlockSpec(memory_space=pltpu.VMEM)
    return pl.pallas_call(
        functools.partial(cross_kernel, first, each),
        in_specs=[pl.BlockSpec(memory_space=pltpu.SMEM)] + [in_vmem] * 4,
        out_specs=[in_vmem] * parts,
        out_shape=[jax.ShapeDtypeStruct((each * tile, panel[0].shape[1]), f32)] * parts,
        compiler_params=pltpu.CompilerParams(vmem_limit_bytes=ROOM),
        cost_estimate=cost,
        name="cross",
    )(table, *window, *panel)


def residual_kernel(firsts, each, table_ref, window_high, window_low, weight_ref, *refs):
    totals, (out_ref, sent, departures) = refs[: len(firsts)], refs[-3:]
    _, tile, columns = sent.shape
    chunk = min(256, columns)

    def leaving(place, entry, part):
        rows = pl.ds(pl.multiple_of(table_ref[entry], tile), tile)
        here = pl.ds(part * chunk, chunk)
        return pltpu.make_async_copy(
            sent.at[place, :, here], out_ref.at[rows, here], departures.at[place, part]
        )

    for part, (first, total) in enumerate(zip(firsts, totals)):
        high, low = split(total[...])
        terms = jnp.concatenate([high, high, low], 1)
        rows = [pl.ds(pl.multiple_of(table_ref[first + at], tile), tile) for at in range(each)]
        for start in range(0, columns, chunk):
            here = slice(start, start + chunk)
            product = dot(terms, weight_ref[:, here], ((1,), (0,)))
            for at in range(each):
                window = window_high[rows[at], here].astype(f32)
                window = window + window_low[rows[at], here].astype(f32)
                sent[part * each + at, :, here] = window - product[at * tile : (at + 1) * tile]
                leaving(part * each + at, first + at, start // chunk).start()

    for part, first in enumerate(firsts):
        for at in range(each):
            for piece in range(columns // chunk):
                leaving(part * each + at, first + at, piece).wait()


def residual_call(table, firsts, tile, window, weight, totals, before, cost=BRIEF):
    (rows, columns), each = window[0].shape, totals[0].shape[0] // tile
    in_vmem = pl.BlockSpec(memory_space=pltpu.VMEM)
    operands = [table, *window, weight, *totals]
    in_specs = [pl.BlockSpec(memory_space=pltpu.SMEM)] + [in_vmem] * (len(operands) - 1)
    aliases = {}
    if before is not None:
        aliases = {len(operands): 0}
        operands.append(before)
        in_specs.append(pl.BlockSpec(memory_space=pl.ANY))
    return pl.pallas_call(
        functools.partial(residual_kernel, firsts, each),
        in_specs=in_specs,
        out_specs=pl.BlockSpec(memory_space=pl.ANY),
        scratch_shapes=[
            pltpu.VMEM((len(firsts) * each, tile, columns), f32),
            pltpu.SemaphoreType.DMA((len(firsts) * each, columns // min(256, columns))),
        ],
        out_shape=jax.ShapeDtypeStruct((rows, columns), f32),
        input_output_aliases=aliases,
        compiler_params=pltpu.CompilerParams(vmem_limit_bytes=ROOM),
        cost_estimate=cost,
        name="residual",
    )(*operands)


def eliminate(diagonal):
    size, lanes, tile = BLOCK, 128, 8
    tiles = size // tile
    row_at = [lax.broadcasted_iota(jnp.int32, (tile, lanes), 0) + tile * t for t in range(tiles)]
    lane_at = lax.broadcasted_iota(jnp.int32, (tile, lanes), 1)
    spread = [
        [
            jnp.broadcast_to(diagonal[tile * t : tile * (t + 1), k : k + 1], (tile, lanes))
            for t in range(tiles)
        ]
        for k in range(size)
    ]
    inverse = [jnp.where(row_at[t] == lane_at, 1.0, 0.0) for t in range(tiles)]
    lower = [jnp.zeros((tile, lanes), f32) for _ in range(tiles)]
    row_of = lambda parts, row: parts[row // tile][row % tile : row % tile + 1, :]
    pivot = row_of(spread[0], 0)
    for j in range(size):
        own = j // tile
        root = lax.rsqrt(pivot)
        if j + 1 < size:
            entry = row_of(spread[j], j + 1) * root
            pivot = row_of(spread[j + 1], j + 1) - entry * entry
        inverse_row = row_of(inverse, j) * root
        column = {t: spread[j][t] * root for t in range(own, tiles)}
        below = dict(column)
        below[own] = jnp.where(row_at[own] > j, column[own], 0.0)
        lower[own] = jnp.where((lane_at == j) & (row_at[own] >= j), column[own], lower[own])
        for t in range(own + 1, tiles):
            lower[t] = jnp.where(lane_at == j, column[t], lower[t])
        for t in range(own, tiles):
            inverse[t] = inverse[t] - below[t] * inverse_row
        inverse[own] = jnp.where(row_at[own] == j, inverse_row, inverse[own])
        for k in range(j + 1, size):
            entry = row_of(column, k)
            for t in range(k // tile, tiles):
                spread[k][t] = spread[k][t] - below[t] * entry
    return jnp.concatenate(lower, 0), jnp.concatenate(inverse, 0)


def factor_kernel(begin, end, last, ins, outs):
    state_ref, lower_ref = outs[:2]
    state_ref[...] = ins[0][...]
    if begin:
        lower_ref[...] = ins[1][...]
    size = state_ref.shape[0]
    column_at = lax.broadcasted_iota(jnp.int32, (BLOCK, size), 1)
    row_at = lax.broadcasted_iota(jnp.int32, (BLOCK, size), 0)
    for step in range(begin, end):
        start, stop = step * BLOCK, (step + 1) * BLOCK
        rows = state_ref[start:stop, :]
        lower, inverse = eliminate(rows[:, start:stop])
        lower_ref[start:stop, :] = lower
        inside = (column_at >= start) & (column_at < stop)
        rows = jnp.where(inside, jnp.where(column_at - start == row_at, 1.0, 0.0), rows)
        done = dot(inverse[:, :BLOCK], rows, ((1,), (0,)), precise)
        state_ref[start:stop, :] = done
        if stop < size:
            upper = jnp.where(column_at >= stop, done, 0.0)
            update = dot(upper, done, ((0,), (0,)), precise)[stop:, :]
            below_at = lax.broadcasted_iota(jnp.int32, (size - stop, size), 1)
            below = jnp.where(
                (below_at >= start) & (below_at < stop), 0.0, state_ref[stop:, :]
            )
            state_ref[stop:, :] = below - update
    if last:
        whole_ref = ins[2]
        triangle_ref, inverse_ref, weight_ref = outs[2:]
        column_at = lax.broadcasted_iota(jnp.int32, (size, size), 1)
        row_at = lax.broadcasted_iota(jnp.int32, (size, size), 0)
        edge = (row_at // BLOCK + 1) * BLOCK
        state = state_ref[...]
        inverse = jnp.where(column_at <= row_at, state, 0.0)
        lower = lower_ref[...]
        wide = jnp.concatenate([lower] * (size // lower.shape[1]), 1)
        for step in range(size // BLOCK):
            start, stop = step * BLOCK, (step + 1) * BLOCK
            shift = start % lower.shape[1]
            part = wide[start:stop, :]
            if shift:
                part = pltpu.roll(part, shift, 1)
            lower_full = jnp.where(
                (column_at[start:stop, :] >= start) & (column_at[start:stop, :] < stop), part, 0.0
            )
            state_ref[start:stop, :] = lower_full
        triangle_ref[...] = jnp.where(column_at >= edge, state, 0.0) + state_ref[...].T
        half = dot(inverse, whole_ref[...], ((1,), (0,)), precise)
        inverse_ref[...] = inverse
        weight = dot(inverse, half, ((0,), (0,)), precise)
        high, low = split(weight)
        for term, part in enumerate((high, low, high)):
            weight_ref[term * size : (term + 1) * size, :] = part


def factor_call(begin, end, operands, whole=None):
    size = operands[0].shape[1]
    operands = list(operands)
    shapes = [
        jax.ShapeDtypeStruct((size, size), f32),
        jax.ShapeDtypeStruct((size, 128), f32),
    ]
    if whole is not None:
        operands.append(whole)
        shapes += [
            jax.ShapeDtypeStruct((size, size), f32),
            jax.ShapeDtypeStruct((size, size), f32),
            jax.ShapeDtypeStruct((3 * size, whole.shape[1]), bf16),
        ]
    in_specs = [pl.BlockSpec(memory_space=pltpu.VMEM)] * len(operands)

    def body(*refs):
        factor_kernel(begin, end, whole is not None, refs[: len(operands)], refs[len(operands) :])

    return pl.pallas_call(
        body,
        out_shape=shapes,
        in_specs=in_specs,
        out_specs=[pl.BlockSpec(memory_space=pltpu.VMEM)] * len(shapes),
        compiler_params=pltpu.CompilerParams(vmem_limit_bytes=24 * MIB),
        cost_estimate=BRIEF,
        name="factor",
    )(*operands)


def flip(value, bit, size):
    return lax.ppermute(value, "row", [(i, i ^ bit) for i in range(size)])


def exchange(value, step, bits):
    size = 2 << len(bits)
    return lax.ppermute(
        value, "row", [(i, i ^ (bits[-1 - step] if i & 1 else bits[step])) for i in range(size)]
    )


def relative_owners(bits):
    owners = [0]
    for bit in reversed(bits):
        owners = [owner | bit for owner in owners] + owners
    return owners


def sum_shares(kept, arrived, bits):
    pairs, count = [(kept, 0), (arrived, 0)], kept.shape[0]
    cut = lambda array, at: lax.slice_in_dim(array, at, at + count, axis=0)
    for step in range(len(bits)):
        count //= 2
        out, others = yield sum(cut(array, at) for array, at in pairs)
        pairs = [(array, at + count) for array, at in pairs]
        if others:
            pairs[0] = (after(pairs[0][0], *others), pairs[0][1])
        pairs.append((exchange(out, step, bits), 0))
    yield sum(cut(array, at) for array, at in pairs)


def gather_panel(shard, depth):
    up = [(i, (i - 1) % depth) for i in range(depth)]
    down = [(i, (i + 1) % depth) for i in range(depth)]
    above = [lax.ppermute(shard, "col", up)]
    below = []
    later, _ = lax.optimization_barrier((shard, above[0]))
    for step in range(2, depth):
        if step % 2 == 0:
            above.append(lax.ppermute(above[-1], "col", up))
        else:
            below.append(lax.ppermute(below[-1] if below else later, "col", down))
    return [shard, *above, *below[::-1]]


def spread(part, bits, *others):
    for step in reversed(range(1, len(bits))):
        part = jnp.concatenate([after(exchange(part, step, bits), *others), part], 0)
    return part


def local(panel_cols, window_cols):
    size = lax.axis_size("row")
    depth = lax.axis_size("col")
    here = lax.axis_index("row").astype(jnp.int32)
    place = lax.axis_index("col").astype(jnp.int32).reshape(1)
    bits = [1 << shift for shift in range(1, size.bit_length() - 1)]
    steps = len(bits)
    share = window_cols.shape[0] // size

    tile = share // 2

    owners = [jnp.asarray(relative_owners(order), jnp.int32) for order in (bits, bits[::-1])]
    table_of = lambda device: share * (device ^ jnp.where(device & 1, owners[1], owners[0]))
    kept, given = table_of(here), table_of(here ^ 1)
    count = kept.shape[0]
    table = jnp.concatenate([kept, kept + tile, given, given + tile])
    entry = lambda side, half: (side * 2 + half) * count

    shards = gather_panel(panel_cols, depth)
    window = hold_call(table, place, window_cols)
    whole, high, low, gram = gram_call(after(place, window[0]), shards)

    def products(side, half, parts, cost, *others):
        first = after(table, *others)
        return cross_call(first, entry(side, half), parts, count, tile, window, (high, low), cost)

    (given,) = products(1, 0, 1, BRIEF, gram)
    arrived = flip(given, 1, size)
    gram = gram + exchange(gram, 0, bits)
    (kept,) = products(0, 0, 1, LONG, given)
    early = sum_shares(kept, arrived, bits)
    early_sum = next(early)
    gram = after(gram, kept)
    (given,) = products(1, 1, 1, BRIEF, early_sum, gram)
    arrived = flip(given, 1, size)
    for step in range(1, steps):
        gram = gram + after(exchange(gram, step, bits), given)
    (kept,) = products(0, 1, 1, LONG, given)
    late = sum_shares(after(kept, gram), arrived, bits)
    late_sum = next(late)
    gram = gram + flip(gram, 1, size)

    blocks = whole.shape[0] // BLOCK
    cuts = (0, blocks * 3 // 8, blocks * 6 // 8, blocks)
    state = factor_call(0, cuts[1], [after(gram, late_sum)])
    early_sum = early.send((early_sum, (state[0],)))
    late_sum = late.send((late_sum, (early_sum,)))
    state = factor_call(cuts[1], cuts[2], [after(state[0], early_sum, late_sum), state[1]])
    for _ in range(1, steps):
        early_sum = early.send((early_sum, (state[0],)))
    for _ in range(1, steps):
        late_sum = late.send((late_sum, (early_sum,)))
    _, _, triangle, inverse, weight = factor_call(
        cuts[2], blocks, [after(state[0], early_sum, late_sum), state[1]], whole
    )

    early_near = spread(early_sum, bits, weight)
    late_near = spread(late_sum, bits, early_near)
    early_far, late_far = [exchange(part, 0, bits) for part in (early_near, late_near)]
    nearer = lambda side, half: entry(side, half) + count // 2
    subtract = lambda firsts, *others: residual_call(table, firsts, tile, window, weight, *others)
    parts = [early_near, flip(early_near, 1, size), late_near]
    residual = subtract([nearer(0, 0), nearer(1, 0), nearer(0, 1)], parts, None)
    late_back = flip(late_near, 1, size)
    early_far, residual = lax.optimization_barrier((early_far, residual))
    residual = subtract([nearer(1, 1), entry(0, 0)], [late_back, early_far], residual)
    late_far, residual = lax.optimization_barrier((late_far, residual))
    parts = [flip(early_far, 1, size), late_far, flip(late_far, 1, size)]
    residual = subtract([entry(1, 0), entry(0, 1), entry(1, 1)], parts, residual)
    summed = jnp.concatenate([after(early_sum, late_far), late_sum], 0)
    top_rows = dot(summed, inverse, ((1,), (1,)), precise)
    return triangle, top_rows, residual


def solution(mesh):
    return jax.shard_map(
        local,
        mesh=mesh,
        in_specs=(P("col", "row"), P("col", "row")),
        out_specs=(P(), P(("col", "row"), None), P("col", "row")),
        check_vma=False,
    )
```

```python
import functools

import jax
import jax.numpy as jnp
from jax import lax
from jax.experimental import pallas as pl
from jax.experimental.pallas import tpu as pltpu
from jax.sharding import PartitionSpec as P

precise = lax.Precision.HIGHEST
f32, bf16 = jnp.float32, jnp.bfloat16
BLOCK = 32
MIB = 1 << 20
ROOM = 24 * MIB
LONG = pl.CostEstimate(flops=100_000_000_000, bytes_accessed=1, transcendentals=0)
BRIEF = pl.CostEstimate(flops=1, bytes_accessed=1, transcendentals=0)


def dot(left, right, dims, precision=None):
    return lax.dot_general(
        left, right, (dims, ((), ())), precision=precision, preferred_element_type=f32
    )


def split(value):
    high = value.astype(bf16)
    return high, (value - high.astype(f32)).astype(bf16)


def after(value, *others):
    return lax.optimization_barrier((value, *others))[0]


def gram_kernel(place_ref, *refs):
    shards, (whole_ref, high_ref, low_ref, gram_ref) = refs[:-4], refs[-4:]
    rows = shards[0].shape[0]
    for step, shard in enumerate(shards):
        owner = lax.rem(place_ref[0] + step, len(shards))
        whole_ref[pl.ds(pl.multiple_of(owner * rows, rows), rows), :] = shard[...]
    whole = whole_ref[...]
    gram_ref[...] = dot(whole, whole, ((1,), (1,)), precise)
    high_ref[...], low_ref[...] = split(whole.T)


def gram_call(place, shards):
    rows, columns = shards[0].shape
    panel = rows * len(shards)
    in_vmem = pl.BlockSpec(memory_space=pltpu.VMEM)
    return pl.pallas_call(
        gram_kernel,
        in_specs=[pl.BlockSpec(memory_space=pltpu.SMEM)] + [in_vmem] * len(shards),
        out_specs=[in_vmem] * 4,
        out_shape=[
            jax.ShapeDtypeStruct((panel, columns), f32),
            jax.ShapeDtypeStruct((columns, panel), bf16),
            jax.ShapeDtypeStruct((columns, panel), bf16),
            jax.ShapeDtypeStruct((panel, panel), f32),
        ],
        compiler_params=pltpu.CompilerParams(vmem_limit_bytes=24 * MIB),
        cost_estimate=LONG,
        name="gram",
    )(place, *shards)


def hold_kernel(table_ref, place_ref, window_ref, high_ref, low_ref, held, arrivals):
    slots, rows, _ = held.shape
    count = window_ref.shape[0] // rows

    def arriving(step):
        start = pl.multiple_of(step * rows, rows)
        slot = lax.rem(step, slots)
        return pltpu.make_async_copy(
            window_ref.at[pl.ds(start, rows), :], held.at[slot], arrivals.at[slot]
        )

    for step in range(min(slots, count)):
        arriving(step).start()

    @pl.loop(0, count)
    def _(step):
        arriving(step).wait()
        high, low = split(held[lax.rem(step, slots)])
        here = pl.ds(pl.multiple_of(step * rows, rows), rows)
        high_ref[here, :] = high
        low_ref[here, :] = low

        @pl.when(step + slots < count)
        def _():
            arriving(step + slots).start()


def hold_call(table, place, window):
    rows, columns = window.shape
    tile = min(256, rows)
    scalars = pl.BlockSpec(memory_space=pltpu.SMEM)
    return pl.pallas_call(
        hold_kernel,
        in_specs=[scalars, scalars, pl.BlockSpec(memory_space=pl.ANY)],
        out_specs=[pl.BlockSpec(memory_space=pltpu.VMEM)] * 2,
        scratch_shapes=[
            pltpu.VMEM((4, tile, columns), f32),
            pltpu.SemaphoreType.DMA((4,)),
        ],
        out_shape=[jax.ShapeDtypeStruct(window.shape, bf16)] * 2,
        compiler_params=pltpu.CompilerParams(vmem_limit_bytes=ROOM),
        cost_estimate=BRIEF,
        name="hold",
    )(table, place, window)


def cross_kernel(first, each, table_ref, window_high, window_low, high_ref, low_ref, *outs):
    tile = outs[0].shape[0] // each
    dims = ((1,), (0,))
    pair = 3 - len(outs) if each % 2 == 0 else 1

    @pl.loop(0, each // pair)
    def _(step):
        entries = [first + step * pair + place for place in range(pair)]
        rows = [pl.ds(pl.multiple_of(table_ref[at], tile), len(outs) * tile) for at in entries]
        window = [
            jnp.concatenate([term[at, :] for at in rows], 0) for term in (window_high, window_low)
        ]
        result = dot(window[0], high_ref[...], dims) + (
            dot(window[0], low_ref[...], dims) + dot(window[1], high_ref[...], dims)
        )
        here = pl.ds(pl.multiple_of(step * pair * tile, tile), pair * tile)
        for part, cross_ref in enumerate(outs):
            cross_ref[here, :] = result[part * pair * tile : (part + 1) * pair * tile]


def cross_call(table, first, parts, each, tile, window, panel, cost):
    in_vmem = pl.BlockSpec(memory_space=pltpu.VMEM)
    return pl.pallas_call(
        functools.partial(cross_kernel, first, each),
        in_specs=[pl.BlockSpec(memory_space=pltpu.SMEM)] + [in_vmem] * 4,
        out_specs=[in_vmem] * parts,
        out_shape=[jax.ShapeDtypeStruct((each * tile, panel[0].shape[1]), f32)] * parts,
        compiler_params=pltpu.CompilerParams(vmem_limit_bytes=ROOM),
        cost_estimate=cost,
        name="cross",
    )(table, *window, *panel)


def residual_kernel(firsts, each, table_ref, window_high, window_low, weight_ref, *refs):
    totals, (out_ref, sent, departures) = refs[: len(firsts)], refs[-3:]
    _, tile, columns = sent.shape
    chunk = min(256, columns)

    def leaving(place, entry, part):
        rows = pl.ds(pl.multiple_of(table_ref[entry], tile), tile)
        here = pl.ds(part * chunk, chunk)
        return pltpu.make_async_copy(
            sent.at[place, :, here], out_ref.at[rows, here], departures.at[place, part]
        )

    for part, (first, total) in enumerate(zip(firsts, totals)):
        high, low = split(total[...])
        terms = jnp.concatenate([high, high, low], 1)
        rows = [pl.ds(pl.multiple_of(table_ref[first + at], tile), tile) for at in range(each)]
        for start in range(0, columns, chunk):
            here = slice(start, start + chunk)
            product = dot(terms, weight_ref[:, here], ((1,), (0,)))
            for at in range(each):
                window = window_high[rows[at], here].astype(f32)
                window = window + window_low[rows[at], here].astype(f32)
                sent[part * each + at, :, here] = window - product[at * tile : (at + 1) * tile]
                leaving(part * each + at, first + at, start // chunk).start()

    for part, first in enumerate(firsts):
        for at in range(each):
            for piece in range(columns // chunk):
                leaving(part * each + at, first + at, piece).wait()


def residual_call(table, firsts, tile, window, weight, totals, before, cost=BRIEF):
    (rows, columns), each = window[0].shape, totals[0].shape[0] // tile
    in_vmem = pl.BlockSpec(memory_space=pltpu.VMEM)
    operands = [table, *window, weight, *totals]
    in_specs = [pl.BlockSpec(memory_space=pltpu.SMEM)] + [in_vmem] * (len(operands) - 1)
    aliases = {}
    if before is not None:
        aliases = {len(operands): 0}
        operands.append(before)
        in_specs.append(pl.BlockSpec(memory_space=pl.ANY))
    return pl.pallas_call(
        functools.partial(residual_kernel, firsts, each),
        in_specs=in_specs,
        out_specs=pl.BlockSpec(memory_space=pl.ANY),
        scratch_shapes=[
            pltpu.VMEM((len(firsts) * each, tile, columns), f32),
            pltpu.SemaphoreType.DMA((len(firsts) * each, columns // min(256, columns))),
        ],
        out_shape=jax.ShapeDtypeStruct((rows, columns), f32),
        input_output_aliases=aliases,
        compiler_params=pltpu.CompilerParams(vmem_limit_bytes=ROOM),
        cost_estimate=cost,
        name="residual",
    )(*operands)


def eliminate(diagonal):
    size, lanes, tile = BLOCK, 128, 8
    tiles = size // tile
    row_at = [lax.broadcasted_iota(jnp.int32, (tile, lanes), 0) + tile * t for t in range(tiles)]
    lane_at = lax.broadcasted_iota(jnp.int32, (tile, lanes), 1)
    spread = [
        [
            jnp.broadcast_to(diagonal[tile * t : tile * (t + 1), k : k + 1], (tile, lanes))
            for t in range(tiles)
        ]
        for k in range(size)
    ]
    inverse = [jnp.where(row_at[t] == lane_at, 1.0, 0.0) for t in range(tiles)]
    lower = [jnp.zeros((tile, lanes), f32) for _ in range(tiles)]
    row_of = lambda parts, row: parts[row // tile][row % tile : row % tile + 1, :]
    pivot = row_of(spread[0], 0)
    for j in range(size):
        own = j // tile
        root = lax.rsqrt(pivot)
        if j + 1 < size:
            entry = row_of(spread[j], j + 1) * root
            pivot = row_of(spread[j + 1], j + 1) - entry * entry
        inverse_row = row_of(inverse, j) * root
        column = {t: spread[j][t] * root for t in range(own, tiles)}
        below = dict(column)
        below[own] = jnp.where(row_at[own] > j, column[own], 0.0)
        lower[own] = jnp.where((lane_at == j) & (row_at[own] >= j), column[own], lower[own])
        for t in range(own + 1, tiles):
            lower[t] = jnp.where(lane_at == j, column[t], lower[t])
        for t in range(own, tiles):
            inverse[t] = inverse[t] - below[t] * inverse_row
        inverse[own] = jnp.where(row_at[own] == j, inverse_row, inverse[own])
        for k in range(j + 1, size):
            entry = row_of(column, k)
            for t in range(k // tile, tiles):
                spread[k][t] = spread[k][t] - below[t] * entry
    return jnp.concatenate(lower, 0), jnp.concatenate(inverse, 0)


def factor_kernel(begin, end, last, ins, outs):
    state_ref, lower_ref = outs[:2]
    state_ref[...] = ins[0][...]
    if begin:
        lower_ref[...] = ins[1][...]
    size = state_ref.shape[0]
    column_at = lax.broadcasted_iota(jnp.int32, (BLOCK, size), 1)
    row_at = lax.broadcasted_iota(jnp.int32, (BLOCK, size), 0)
    for step in range(begin, end):
        start, stop = step * BLOCK, (step + 1) * BLOCK
        rows = state_ref[start:stop, :]
        lower, inverse = eliminate(rows[:, start:stop])
        lower_ref[start:stop, :] = lower
        inside = (column_at >= start) & (column_at < stop)
        rows = jnp.where(inside, jnp.where(column_at - start == row_at, 1.0, 0.0), rows)
        done = dot(inverse[:, :BLOCK], rows, ((1,), (0,)), precise)
        state_ref[start:stop, :] = done
        if stop < size:
            upper = jnp.where(column_at >= stop, done, 0.0)
            update = dot(upper, done, ((0,), (0,)), precise)[stop:, :]
            below_at = lax.broadcasted_iota(jnp.int32, (size - stop, size), 1)
            below = jnp.where(
                (below_at >= start) & (below_at < stop), 0.0, state_ref[stop:, :]
            )
            state_ref[stop:, :] = below - update
    if last:
        whole_ref = ins[2]
        triangle_ref, inverse_ref, weight_ref = outs[2:]
        column_at = lax.broadcasted_iota(jnp.int32, (size, size), 1)
        row_at = lax.broadcasted_iota(jnp.int32, (size, size), 0)
        edge = (row_at // BLOCK + 1) * BLOCK
        state = state_ref[...]
        inverse = jnp.where(column_at <= row_at, state, 0.0)
        lower = lower_ref[...]
        wide = jnp.concatenate([lower] * (size // lower.shape[1]), 1)
        for step in range(size // BLOCK):
            start, stop = step * BLOCK, (step + 1) * BLOCK
            shift = start % lower.shape[1]
            part = wide[start:stop, :]
            if shift:
                part = pltpu.roll(part, shift, 1)
            lower_full = jnp.where(
                (column_at[start:stop, :] >= start) & (column_at[start:stop, :] < stop), part, 0.0
            )
            state_ref[start:stop, :] = lower_full
        triangle_ref[...] = jnp.where(column_at >= edge, state, 0.0) + state_ref[...].T
        half = dot(inverse, whole_ref[...], ((1,), (0,)), precise)
        inverse_ref[...] = inverse
        weight = dot(inverse, half, ((0,), (0,)), precise)
        high, low = split(weight)
        for term, part in enumerate((high, low, high)):
            weight_ref[term * size : (term + 1) * size, :] = part


def factor_call(begin, end, operands, whole=None):
    size = operands[0].shape[1]
    operands = list(operands)
    shapes = [
        jax.ShapeDtypeStruct((size, size), f32),
        jax.ShapeDtypeStruct((size, 128), f32),
    ]
    if whole is not None:
        operands.append(whole)
        shapes += [
            jax.ShapeDtypeStruct((size, size), f32),
            jax.ShapeDtypeStruct((size, size), f32),
            jax.ShapeDtypeStruct((3 * size, whole.shape[1]), bf16),
        ]
    in_specs = [pl.BlockSpec(memory_space=pltpu.VMEM)] * len(operands)

    def body(*refs):
        factor_kernel(begin, end, whole is not None, refs[: len(operands)], refs[len(operands) :])

    return pl.pallas_call(
        body,
        out_shape=shapes,
        in_specs=in_specs,
        out_specs=[pl.BlockSpec(memory_space=pltpu.VMEM)] * len(shapes),
        compiler_params=pltpu.CompilerParams(vmem_limit_bytes=24 * MIB),
        cost_estimate=BRIEF,
        name="factor",
    )(*operands)


def flip(value, bit, size):
    return lax.ppermute(value, "row", [(i, i ^ bit) for i in range(size)])


def exchange(value, step, bits):
    size = 2 << len(bits)
    return lax.ppermute(
        value, "row", [(i, i ^ (bits[-1 - step] if i & 1 else bits[step])) for i in range(size)]
    )


def relative_owners(bits):
    owners = [0]
    for bit in reversed(bits):
        owners = [owner | bit for owner in owners] + owners
    return owners


def sum_shares(kept, arrived, bits):
    pairs, count = [(kept, 0), (arrived, 0)], kept.shape[0]
    cut = lambda array, at: lax.slice_in_dim(array, at, at + count, axis=0)
    for step in range(len(bits)):
        count //= 2
        out, others = yield sum(cut(array, at) for array, at in pairs)
        pairs = [(array, at + count) for array, at in pairs]
        if others:
            pairs[0] = (after(pairs[0][0], *others), pairs[0][1])
        pairs.append((exchange(out, step, bits), 0))
    yield sum(cut(array, at) for array, at in pairs)


def gather_panel(shard, depth):
    up = [(i, (i - 1) % depth) for i in range(depth)]
    down = [(i, (i + 1) % depth) for i in range(depth)]
    above = [lax.ppermute(shard, "col", up)]
    below = []
    later, _ = lax.optimization_barrier((shard, above[0]))
    for step in range(2, depth):
        if step % 2 == 0:
            above.append(lax.ppermute(above[-1], "col", up))
        else:
            below.append(lax.ppermute(below[-1] if below else later, "col", down))
    return [shard, *above, *below[::-1]]


def spread(part, bits, *others):
    for step in reversed(range(1, len(bits))):
        part = jnp.concatenate([after(exchange(part, step, bits), *others), part], 0)
    return part


def local(panel_cols, window_cols):
    size = lax.axis_size("row")
    depth = lax.axis_size("col")
    here = lax.axis_index("row").astype(jnp.int32)
    place = lax.axis_index("col").astype(jnp.int32).reshape(1)
    bits = [1 << shift for shift in range(1, size.bit_length() - 1)]
    steps = len(bits)
    share = window_cols.shape[0] // size

    tile = share // 2

    owners = [jnp.asarray(relative_owners(order), jnp.int32) for order in (bits, bits[::-1])]
    table_of = lambda device: share * (device ^ jnp.where(device & 1, owners[1], owners[0]))
    kept, given = table_of(here), table_of(here ^ 1)
    count = kept.shape[0]
    table = jnp.concatenate([kept, kept + tile, given, given + tile])
    entry = lambda side, half: (side * 2 + half) * count

    shards = gather_panel(panel_cols, depth)
    window = hold_call(table, place, window_cols)
    whole, high, low, gram = gram_call(after(place, window[0]), shards)

    def products(side, half, parts, cost, *others):
        first = after(table, *others)
        return cross_call(first, entry(side, half), parts, count, tile, window, (high, low), cost)

    (given,) = products(1, 0, 1, BRIEF, gram)
    arrived = flip(given, 1, size)
    gram = gram + exchange(gram, 0, bits)
    (kept,) = products(0, 0, 1, LONG, given)
    early = sum_shares(kept, arrived, bits)
    early_sum = next(early)
    gram = after(gram, kept)
    (given,) = products(1, 1, 1, BRIEF, early_sum, gram)
    arrived = flip(given, 1, size)
    for step in range(1, steps):
        gram = gram + after(exchange(gram, step, bits), given)
    (kept,) = products(0, 1, 1, LONG, given)
    late = sum_shares(after(kept, gram), arrived, bits)
    late_sum = next(late)
    gram = gram + flip(gram, 1, size)

    blocks = whole.shape[0] // BLOCK
    cuts = (0, blocks * 3 // 8, blocks * 6 // 8, blocks)
    state = factor_call(0, cuts[1], [after(gram, late_sum)])
    early_sum = early.send((early_sum, (state[0],)))
    late_sum = late.send((late_sum, (early_sum,)))
    state = factor_call(cuts[1], cuts[2], [after(state[0], early_sum, late_sum), state[1]])
    for _ in range(1, steps):
        early_sum = early.send((early_sum, (state[0],)))
    for _ in range(1, steps):
        late_sum = late.send((late_sum, (early_sum,)))
    _, _, triangle, inverse, weight = factor_call(
        cuts[2], blocks, [after(state[0], early_sum, late_sum), state[1]], whole
    )

    early_near = spread(early_sum, bits, weight)
    late_near = spread(late_sum, bits, early_near)
    early_far, late_far = [exchange(part, 0, bits) for part in (early_near, late_near)]
    nearer = lambda side, half: entry(side, half) + count // 2
    subtract = lambda firsts, *others: residual_call(table, firsts, tile, window, weight, *others)
    parts = [early_near, flip(early_near, 1, size), late_near]
    residual = subtract([nearer(0, 0), nearer(1, 0), nearer(0, 1)], parts, None)
    late_back = flip(late_near, 1, size)
    early_far, residual = lax.optimization_barrier((early_far, residual))
    residual = subtract([nearer(1, 1), entry(0, 0)], [late_back, early_far], residual)
    summed = jnp.concatenate([after(early_sum, residual), late_sum], 0)
    top_rows = dot(summed, inverse, ((1,), (1,)), precise)
    late_far, residual, top_rows = lax.optimization_barrier((late_far, residual, top_rows))
    residual = subtract([entry(0, 1)], [late_far], residual)
    parts = [flip(early_far, 1, size), flip(late_far, 1, size)]
    residual = subtract([entry(1, 0), entry(1, 1)], parts, residual)
    return triangle, top_rows, residual


def solution(mesh):
    return jax.shard_map(
        local,
        mesh=mesh,
        in_specs=(P("col", "row"), P("col", "row")),
        out_specs=(P(), P(("col", "row"), None), P("col", "row")),
        check_vma=False,
    )
```

```python
import functools

import jax
import jax.numpy as jnp
from jax import lax
from jax.experimental import pallas as pl
from jax.experimental.pallas import tpu as pltpu
from jax.sharding import PartitionSpec as P

precise = lax.Precision.HIGHEST
f32, bf16 = jnp.float32, jnp.bfloat16
BLOCK = 32
MIB = 1 << 20
ROOM = 24 * MIB
LONG = pl.CostEstimate(flops=100_000_000_000, bytes_accessed=1, transcendentals=0)
BRIEF = pl.CostEstimate(flops=1, bytes_accessed=1, transcendentals=0)


def dot(left, right, dims, precision=None):
    return lax.dot_general(
        left, right, (dims, ((), ())), precision=precision, preferred_element_type=f32
    )


def split(value):
    high = value.astype(bf16)
    return high, (value - high.astype(f32)).astype(bf16)


def after(value, *others):
    return lax.optimization_barrier((value, *others))[0]


def gram_kernel(place_ref, *refs):
    shards, (whole_ref, high_ref, low_ref, gram_ref) = refs[:-4], refs[-4:]
    rows = shards[0].shape[0]
    for step, shard in enumerate(shards):
        owner = lax.rem(place_ref[0] + step, len(shards))
        whole_ref[pl.ds(pl.multiple_of(owner * rows, rows), rows), :] = shard[...]
    whole = whole_ref[...]
    gram_ref[...] = dot(whole, whole, ((1,), (1,)), precise)
    high_ref[...], low_ref[...] = split(whole.T)


def gram_call(place, shards):
    rows, columns = shards[0].shape
    panel = rows * len(shards)
    in_vmem = pl.BlockSpec(memory_space=pltpu.VMEM)
    return pl.pallas_call(
        gram_kernel,
        in_specs=[pl.BlockSpec(memory_space=pltpu.SMEM)] + [in_vmem] * len(shards),
        out_specs=[in_vmem] * 4,
        out_shape=[
            jax.ShapeDtypeStruct((panel, columns), f32),
            jax.ShapeDtypeStruct((columns, panel), bf16),
            jax.ShapeDtypeStruct((columns, panel), bf16),
            jax.ShapeDtypeStruct((panel, panel), f32),
        ],
        compiler_params=pltpu.CompilerParams(vmem_limit_bytes=24 * MIB),
        cost_estimate=LONG,
        name="gram",
    )(place, *shards)


def hold_kernel(table_ref, place_ref, window_ref, high_ref, low_ref, held, arrivals):
    slots, rows, _ = held.shape
    count = window_ref.shape[0] // rows

    def arriving(step):
        start = pl.multiple_of(step * rows, rows)
        slot = lax.rem(step, slots)
        return pltpu.make_async_copy(
            window_ref.at[pl.ds(start, rows), :], held.at[slot], arrivals.at[slot]
        )

    for step in range(min(slots, count)):
        arriving(step).start()

    @pl.loop(0, count)
    def _(step):
        arriving(step).wait()
        high, low = split(held[lax.rem(step, slots)])
        here = pl.ds(pl.multiple_of(step * rows, rows), rows)
        high_ref[here, :] = high
        low_ref[here, :] = low

        @pl.when(step + slots < count)
        def _():
            arriving(step + slots).start()


def hold_call(table, place, window):
    rows, columns = window.shape
    tile = min(256, rows)
    scalars = pl.BlockSpec(memory_space=pltpu.SMEM)
    return pl.pallas_call(
        hold_kernel,
        in_specs=[scalars, scalars, pl.BlockSpec(memory_space=pl.ANY)],
        out_specs=[pl.BlockSpec(memory_space=pltpu.VMEM)] * 2,
        scratch_shapes=[
            pltpu.VMEM((4, tile, columns), f32),
            pltpu.SemaphoreType.DMA((4,)),
        ],
        out_shape=[jax.ShapeDtypeStruct(window.shape, bf16)] * 2,
        compiler_params=pltpu.CompilerParams(vmem_limit_bytes=ROOM),
        cost_estimate=BRIEF,
        name="hold",
    )(table, place, window)


def cross_kernel(first, each, table_ref, window_high, window_low, high_ref, low_ref, *outs):
    tile = outs[0].shape[0] // each
    dims = ((1,), (0,))
    pair = 3 - len(outs) if each % 2 == 0 else 1

    @pl.loop(0, each // pair)
    def _(step):
        entries = [first + step * pair + place for place in range(pair)]
        rows = [pl.ds(pl.multiple_of(table_ref[at], tile), len(outs) * tile) for at in entries]
        window = [
            jnp.concatenate([term[at, :] for at in rows], 0) for term in (window_high, window_low)
        ]
        result = dot(window[0], high_ref[...], dims) + (
            dot(window[0], low_ref[...], dims) + dot(window[1], high_ref[...], dims)
        )
        here = pl.ds(pl.multiple_of(step * pair * tile, tile), pair * tile)
        for part, cross_ref in enumerate(outs):
            cross_ref[here, :] = result[part * pair * tile : (part + 1) * pair * tile]


def cross_call(table, first, parts, each, tile, window, panel, cost):
    in_vmem = pl.BlockSpec(memory_space=pltpu.VMEM)
    return pl.pallas_call(
        functools.partial(cross_kernel, first, each),
        in_specs=[pl.BlockSpec(memory_space=pltpu.SMEM)] + [in_vmem] * 4,
        out_specs=[in_vmem] * parts,
        out_shape=[jax.ShapeDtypeStruct((each * tile, panel[0].shape[1]), f32)] * parts,
        compiler_params=pltpu.CompilerParams(vmem_limit_bytes=ROOM),
        cost_estimate=cost,
        name="cross",
    )(table, *window, *panel)


def residual_kernel(firsts, each, table_ref, window_high, window_low, weight_ref, *refs):
    totals, (out_ref, sent, departures) = refs[: len(firsts)], refs[-3:]
    _, tile, columns = sent.shape
    chunk = min(256, columns)

    def leaving(place, entry, part):
        rows = pl.ds(pl.multiple_of(table_ref[entry], tile), tile)
        here = pl.ds(part * chunk, chunk)
        return pltpu.make_async_copy(
            sent.at[place, :, here], out_ref.at[rows, here], departures.at[place, part]
        )

    for part, (first, total) in enumerate(zip(firsts, totals)):
        high, low = split(total[...])
        terms = jnp.concatenate([high, high, low], 1)
        rows = [pl.ds(pl.multiple_of(table_ref[first + at], tile), tile) for at in range(each)]
        for start in range(0, columns, chunk):
            here = slice(start, start + chunk)
            product = dot(terms, weight_ref[:, here], ((1,), (0,)))
            for at in range(each):
                window = window_high[rows[at], here].astype(f32)
                window = window + window_low[rows[at], here].astype(f32)
                sent[part * each + at, :, here] = window - product[at * tile : (at + 1) * tile]
                leaving(part * each + at, first + at, start // chunk).start()

    for part, first in enumerate(firsts):
        for at in range(each):
            for piece in range(columns // chunk):
                leaving(part * each + at, first + at, piece).wait()


def residual_call(table, firsts, tile, window, weight, totals, before, cost=BRIEF):
    (rows, columns), each = window[0].shape, totals[0].shape[0] // tile
    in_vmem = pl.BlockSpec(memory_space=pltpu.VMEM)
    operands = [table, *window, weight, *totals]
    in_specs = [pl.BlockSpec(memory_space=pltpu.SMEM)] + [in_vmem] * (len(operands) - 1)
    aliases = {}
    if before is not None:
        aliases = {len(operands): 0}
        operands.append(before)
        in_specs.append(pl.BlockSpec(memory_space=pl.ANY))
    return pl.pallas_call(
        functools.partial(residual_kernel, firsts, each),
        in_specs=in_specs,
        out_specs=pl.BlockSpec(memory_space=pl.ANY),
        scratch_shapes=[
            pltpu.VMEM((len(firsts) * each, tile, columns), f32),
            pltpu.SemaphoreType.DMA((len(firsts) * each, columns // min(256, columns))),
        ],
        out_shape=jax.ShapeDtypeStruct((rows, columns), f32),
        input_output_aliases=aliases,
        compiler_params=pltpu.CompilerParams(vmem_limit_bytes=ROOM),
        cost_estimate=cost,
        name="residual",
    )(*operands)


def eliminate(diagonal):
    size, lanes, tile = BLOCK, 128, 8
    tiles = size // tile
    row_at = [lax.broadcasted_iota(jnp.int32, (tile, lanes), 0) + tile * t for t in range(tiles)]
    lane_at = lax.broadcasted_iota(jnp.int32, (tile, lanes), 1)
    spread = [
        [
            jnp.broadcast_to(diagonal[tile * t : tile * (t + 1), k : k + 1], (tile, lanes))
            for t in range(tiles)
        ]
        for k in range(size)
    ]
    inverse = [jnp.where(row_at[t] == lane_at, 1.0, 0.0) for t in range(tiles)]
    lower = [jnp.zeros((tile, lanes), f32) for _ in range(tiles)]
    row_of = lambda parts, row: parts[row // tile][row % tile : row % tile + 1, :]
    pivot = row_of(spread[0], 0)
    for j in range(size):
        own = j // tile
        root = lax.rsqrt(pivot)
        if j + 1 < size:
            entry = row_of(spread[j], j + 1) * root
            pivot = row_of(spread[j + 1], j + 1) - entry * entry
        inverse_row = row_of(inverse, j) * root
        column = {t: spread[j][t] * root for t in range(own, tiles)}
        below = dict(column)
        below[own] = jnp.where(row_at[own] > j, column[own], 0.0)
        lower[own] = jnp.where((lane_at == j) & (row_at[own] >= j), column[own], lower[own])
        for t in range(own + 1, tiles):
            lower[t] = jnp.where(lane_at == j, column[t], lower[t])
        for t in range(own, tiles):
            inverse[t] = inverse[t] - below[t] * inverse_row
        inverse[own] = jnp.where(row_at[own] == j, inverse_row, inverse[own])
        for k in range(j + 1, size):
            entry = row_of(column, k)
            for t in range(k // tile, tiles):
                spread[k][t] = spread[k][t] - below[t] * entry
    return jnp.concatenate(lower, 0), jnp.concatenate(inverse, 0)


def factor_kernel(begin, end, last, ins, outs):
    state_ref, lower_ref = outs[:2]
    state_ref[...] = ins[0][...]
    if begin:
        lower_ref[...] = ins[1][...]
    size = state_ref.shape[0]
    column_at = lax.broadcasted_iota(jnp.int32, (BLOCK, size), 1)
    row_at = lax.broadcasted_iota(jnp.int32, (BLOCK, size), 0)
    for step in range(begin, end):
        start, stop = step * BLOCK, (step + 1) * BLOCK
        rows = state_ref[start:stop, :]
        lower, inverse = eliminate(rows[:, start:stop])
        lower_ref[start:stop, :] = lower
        inside = (column_at >= start) & (column_at < stop)
        rows = jnp.where(inside, jnp.where(column_at - start == row_at, 1.0, 0.0), rows)
        done = dot(inverse[:, :BLOCK], rows, ((1,), (0,)), precise)
        state_ref[start:stop, :] = done
        if stop < size:
            upper = jnp.where(column_at >= stop, done, 0.0)
            update = dot(upper, done, ((0,), (0,)), precise)[stop:, :]
            below_at = lax.broadcasted_iota(jnp.int32, (size - stop, size), 1)
            below = jnp.where(
                (below_at >= start) & (below_at < stop), 0.0, state_ref[stop:, :]
            )
            state_ref[stop:, :] = below - update
    if last:
        whole_ref = ins[2]
        triangle_ref, inverse_ref, weight_ref = outs[2:]
        column_at = lax.broadcasted_iota(jnp.int32, (size, size), 1)
        row_at = lax.broadcasted_iota(jnp.int32, (size, size), 0)
        edge = (row_at // BLOCK + 1) * BLOCK
        state = state_ref[...]
        inverse = jnp.where(column_at <= row_at, state, 0.0)
        lower = lower_ref[...]
        wide = jnp.concatenate([lower] * (size // lower.shape[1]), 1)
        for step in range(size // BLOCK):
            start, stop = step * BLOCK, (step + 1) * BLOCK
            shift = start % lower.shape[1]
            part = wide[start:stop, :]
            if shift:
                part = pltpu.roll(part, shift, 1)
            lower_full = jnp.where(
                (column_at[start:stop, :] >= start) & (column_at[start:stop, :] < stop), part, 0.0
            )
            state_ref[start:stop, :] = lower_full
        triangle_ref[...] = jnp.where(column_at >= edge, state, 0.0) + state_ref[...].T
        half = dot(inverse, whole_ref[...], ((1,), (0,)), precise)
        inverse_ref[...] = inverse
        weight = dot(inverse, half, ((0,), (0,)), precise)
        high, low = split(weight)
        for term, part in enumerate((high, low, high)):
            weight_ref[term * size : (term + 1) * size, :] = part


def factor_call(begin, end, operands, whole=None):
    size = operands[0].shape[1]
    operands = list(operands)
    shapes = [
        jax.ShapeDtypeStruct((size, size), f32),
        jax.ShapeDtypeStruct((size, 128), f32),
    ]
    if whole is not None:
        operands.append(whole)
        shapes += [
            jax.ShapeDtypeStruct((size, size), f32),
            jax.ShapeDtypeStruct((size, size), f32),
            jax.ShapeDtypeStruct((3 * size, whole.shape[1]), bf16),
        ]
    in_specs = [pl.BlockSpec(memory_space=pltpu.VMEM)] * len(operands)

    def body(*refs):
        factor_kernel(begin, end, whole is not None, refs[: len(operands)], refs[len(operands) :])

    return pl.pallas_call(
        body,
        out_shape=shapes,
        in_specs=in_specs,
        out_specs=[pl.BlockSpec(memory_space=pltpu.VMEM)] * len(shapes),
        compiler_params=pltpu.CompilerParams(vmem_limit_bytes=24 * MIB),
        cost_estimate=BRIEF,
        name="factor",
    )(*operands)


def flip(value, bit, size):
    return lax.ppermute(value, "row", [(i, i ^ bit) for i in range(size)])


def exchange(value, step, bits):
    size = 2 << len(bits)
    return lax.ppermute(
        value, "row", [(i, i ^ (bits[-1 - step] if i & 1 else bits[step])) for i in range(size)]
    )


def relative_owners(bits):
    owners = [0]
    for bit in reversed(bits):
        owners = [owner | bit for owner in owners] + owners
    return owners


def sum_shares(kept, arrived, bits):
    pairs, count = [(kept, 0), (arrived, 0)], kept.shape[0]
    cut = lambda array, at: lax.slice_in_dim(array, at, at + count, axis=0)
    for step in range(len(bits)):
        count //= 2
        out, others = yield sum(cut(array, at) for array, at in pairs)
        pairs = [(array, at + count) for array, at in pairs]
        if others:
            pairs[0] = (after(pairs[0][0], *others), pairs[0][1])
        pairs.append((exchange(out, step, bits), 0))
    yield sum(cut(array, at) for array, at in pairs)


def gather_panel(shard, depth):
    up = [(i, (i - 1) % depth) for i in range(depth)]
    down = [(i, (i + 1) % depth) for i in range(depth)]
    above = [lax.ppermute(shard, "col", up)]
    below = []
    later, _ = lax.optimization_barrier((shard, above[0]))
    for step in range(2, depth):
        if step % 2 == 0:
            above.append(lax.ppermute(above[-1], "col", up))
        else:
            below.append(lax.ppermute(below[-1] if below else later, "col", down))
    return [shard, *above, *below[::-1]]


def spread(part, bits, *others):
    for step in reversed(range(1, len(bits))):
        part = jnp.concatenate([after(exchange(part, step, bits), *others), part], 0)
    return part


def local(panel_cols, window_cols):
    size = lax.axis_size("row")
    depth = lax.axis_size("col")
    here = lax.axis_index("row").astype(jnp.int32)
    place = lax.axis_index("col").astype(jnp.int32).reshape(1)
    bits = [1 << shift for shift in range(1, size.bit_length() - 1)]
    steps = len(bits)
    share = window_cols.shape[0] // size

    tile = share // 2

    owners = [jnp.asarray(relative_owners(order), jnp.int32) for order in (bits, bits[::-1])]
    table_of = lambda device: share * (device ^ jnp.where(device & 1, owners[1], owners[0]))
    kept, given = table_of(here), table_of(here ^ 1)
    count = kept.shape[0]
    table = jnp.concatenate([kept, kept + tile, given, given + tile])
    entry = lambda side, half: (side * 2 + half) * count

    shards = gather_panel(panel_cols, depth)
    window = hold_call(table, place, window_cols)
    whole, high, low, gram = gram_call(after(place, window[0]), shards)

    def products(side, half, parts, cost, *others):
        first = after(table, *others)
        return cross_call(first, entry(side, half), parts, count, tile, window, (high, low), cost)

    (given,) = products(1, 0, 1, BRIEF, gram)
    arrived = flip(given, 1, size)
    gram = gram + exchange(gram, 0, bits)
    (kept,) = products(0, 0, 1, LONG, given)
    early = sum_shares(kept, arrived, bits)
    early_sum = next(early)
    gram = after(gram, kept)
    (given,) = products(1, 1, 1, BRIEF, early_sum, gram)
    arrived = flip(given, 1, size)
    (kept,) = products(0, 1, 1, LONG, given)
    late = sum_shares(kept, arrived, bits)
    late_sum = next(late)
    for step in range(1, steps):
        gram = gram + after(exchange(gram, step, bits), late_sum)
    gram = gram + flip(gram, 1, size)

    blocks = whole.shape[0] // BLOCK
    cuts = (0, blocks * 3 // 8, blocks * 6 // 8, blocks)
    state = factor_call(0, cuts[1], [after(gram, late_sum)])
    early_sum = early.send((early_sum, (state[0],)))
    late_sum = late.send((late_sum, (early_sum,)))
    state = factor_call(cuts[1], cuts[2], [after(state[0], early_sum, late_sum), state[1]])
    for _ in range(1, steps):
        early_sum = early.send((early_sum, (state[0],)))
    for _ in range(1, steps):
        late_sum = late.send((late_sum, (early_sum,)))
    _, _, triangle, inverse, weight = factor_call(
        cuts[2], blocks, [after(state[0], early_sum, late_sum), state[1]], whole
    )

    early_near = spread(early_sum, bits, weight)
    late_near = spread(late_sum, bits, early_near)
    early_far, late_far = [exchange(part, 0, bits) for part in (early_near, late_near)]
    nearer = lambda side, half: entry(side, half) + count // 2
    subtract = lambda firsts, *others: residual_call(table, firsts, tile, window, weight, *others)
    parts = [early_near, flip(early_near, 1, size), late_near]
    residual = subtract([nearer(0, 0), nearer(1, 0), nearer(0, 1)], parts, None)
    late_back = flip(late_near, 1, size)
    early_far, residual = lax.optimization_barrier((early_far, residual))
    residual = subtract([nearer(1, 1), entry(0, 0)], [late_back, early_far], residual)
    summed = jnp.concatenate([after(early_sum, residual), late_sum], 0)
    top_rows = dot(summed, inverse, ((1,), (1,)), precise)
    late_far, residual, top_rows = lax.optimization_barrier((late_far, residual, top_rows))
    residual = subtract([entry(0, 1)], [late_far], residual)
    parts = [flip(early_far, 1, size), flip(late_far, 1, size)]
    residual = subtract([entry(1, 0), entry(1, 1)], parts, residual)
    return triangle, top_rows, residual


def solution(mesh):
    return jax.shard_map(
        local,
        mesh=mesh,
        in_specs=(P("col", "row"), P("col", "row")),
        out_specs=(P(), P(("col", "row"), None), P("col", "row")),
        check_vma=False,
    )
```
